256 devices in a mesh: depth: 2 (over x_lo), row: 4 (over y), col: 32 (over z, x_hi, core).
Axes of the slice: x: 4 (x_hi: 2, x_lo: 2; x = x_hi * 2 + x_lo), y: 4, z: 8, core: 2. Of those that a mesh axis runs over, the one named last changes fastest.
Arguments:
- object_field: float32 [2, 2, 2048, 16384], P('depth', None, 'row', 'col'), may hold values from -1 to 1.9
- probe: bfloat16 [2, 256, 256], replicated, may hold values from -4 to 4
- amplitude: bfloat16 [4, 32, 2, 256, 256], P('row', 'col'), may hold values from 0.19921875 to 1.59375
- positions: int32 [4, 32, 2, 2], P('row', 'col'), may hold values from 0 to 512, as said below
- live: int32 [4, 32, 2], P('row', 'col'), may hold values from 0 to 1
Outputs:
- object_grad: float32 [2, 2, 2048, 16384], P('depth', None, 'row', 'col')
The draws below stay inside these ranges and needn't reach their ends.
Inputs may be any that keep to these rules, and one draw needn't show every extreme that they name: `positions`: offsets of a patch's corner inside its tile's region widened by 128 cells on every side.
All inputs are finite; a program needn't handle non-finite values.
Results may differ from the reference program's by a relative error of at most 0.009.
Values may be sent and summed in bfloat16 or wider, within the bound.
A program may use at most 64 MiB of HBM per device.

```python
import math
import jax
import jax.numpy as jnp
from jax import lax

PATCH = 256
TILE = 512
MICRO = 2
SLICES = 2
ROWS = 2048
COLS = 16384
N_ROW = 4
N_COL = 32


def draw_object_field(key, part):
    key = jax.random.fold_in(key, 11)
    first_key, second_key = jax.random.split(key)
    field_shape = (SLICES, ROWS, COLS)
    real_part = 0.9 + 0.25 * jnp.clip(jax.random.normal(first_key, field_shape, jnp.float32), -4.0, 4.0)
    imag_part = 0.25 * jnp.clip(jax.random.normal(second_key, field_shape, jnp.float32), -4.0, 4.0)
    return jnp.stack((real_part, imag_part), axis=1)


def draw_positions(key, part):
    key = jax.random.fold_in(key, 23)
    corners = jax.random.randint(key, (N_ROW, N_COL, MICRO, 2), 0, TILE + 1, dtype=jnp.int32)
    corners = corners.at[0, 0, 0, 0].set(0)
    corners = corners.at[0, 0, 0, 1].set(TILE)
    return corners


def draw_live(key, part):
    key = jax.random.fold_in(key, 37)
    picks = jax.random.randint(key, (N_ROW, N_COL, MICRO), 0, 4, dtype=jnp.int32)
    live_flags = jnp.where(picks > 0, 1, 0).astype(jnp.int32)
    live_flags = live_flags.at[0, 0, :].set(1)
    live_flags = live_flags.at[N_ROW - 1, N_COL - 1, 0].set(0)
    return live_flags


def shard_levels(key, dims, cuts, low, top_value):
    def one(dim, blocks):
        draws = jax.random.uniform(jax.random.fold_in(jax.random.fold_in(key, 6), dim), (blocks,), jnp.float32, low / len(cuts), top_value / len(cuts))
        return jnp.repeat(jnp.exp(draws), dims[dim] // blocks).reshape((-1,) + (1,) * (len(dims) - dim - 1))

    gain = one(*cuts[0])
    for cut in cuts[1:]:
        gain = gain * one(*cut)
    return gain


def normal_values(rng, extent, spread, bound, kind=jnp.bfloat16):
    entries = jax.random.normal(rng, extent, jnp.float32) * spread
    return jnp.minimum(jnp.maximum(entries, -bound), bound).astype(kind)


def setup_inputs(seed: int = 0) -> dict:
    keys = jax.random.split(jax.random.key(seed), 6)
    return {
        "object_field": draw_object_field(jax.random.fold_in(keys[5], 71), 0),
        "probe": normal_values(keys[1], (2, PATCH, PATCH), 0.7, 4.0),
        "amplitude": jnp.clip(0.19921875 + 1.3945312 * jax.random.uniform(keys[2], (N_ROW, N_COL, MICRO, PATCH, PATCH), jnp.float32) ** shard_levels(keys[2], (N_ROW, N_COL, MICRO, PATCH, PATCH), ((0, 4), (1, 32)), -0.2, 0.2), 0.19921875, 1.59375).astype(jnp.bfloat16),
        "positions": draw_positions(jax.random.fold_in(keys[5], 71), 0),
        "live": draw_live(jax.random.fold_in(keys[5], 71), 0),
    }


def rounded(values):
    return lax.optimization_barrier(values.astype(jnp.bfloat16)).astype(jnp.float32)


def rounded_wave(values):
    return lax.complex(rounded(jnp.real(values)), rounded(jnp.imag(values)))


def forward_fft(values):
    return jnp.fft.fft2(values, norm="ortho")


def inverse_fft(values):
    return jnp.fft.ifft2(values, norm="ortho")


def reference(object_field, probe, amplitude, positions, live):
    patch_size = PATCH
    rim_width = patch_size // 2
    offsets = jnp.arange(patch_size, dtype=jnp.int32)
    frequency = ((offsets + rim_width) % patch_size - rim_width).astype(jnp.float32)
    phases = -math.pi * (frequency[:, None] ** 2 + frequency[None, :] ** 2) / (2.0 * patch_size)
    chirp_table = lax.complex(jnp.cos(phases), jnp.sin(phases))
    start_wave = lax.complex(probe[0].astype(jnp.float32), probe[1].astype(jnp.float32))

    def one_patch(counter, gradient):
        tile_row = counter // (N_COL * MICRO)
        tile_col = (counter // MICRO) % N_COL
        batch_slot = counter % MICRO
        row_index = (tile_row * TILE - rim_width + positions[tile_row, tile_col, batch_slot, 0] + offsets) % ROWS
        col_index = (tile_col * TILE - rim_width + positions[tile_row, tile_col, batch_slot, 1] + offsets) % COLS
        pieces = object_field[:, :, row_index[:, None], col_index[None, :]]
        transmit = lax.complex(pieces[:, 0], pieces[:, 1])
        wave_now = start_wave
        waves = []
        for layer_index in range(SLICES):
            waves.append(wave_now)
            transmitted = wave_now * transmit[layer_index]
            if layer_index + 1 < SLICES:
                wave_now = rounded_wave(inverse_fft(chirp_table * forward_fft(transmitted)))
        far_wave = forward_fft(transmitted)
        modulus = jnp.abs(far_wave)
        measured = amplitude[tile_row, tile_col, batch_slot].astype(jnp.float32)
        weight = live[tile_row, tile_col, batch_slot].astype(jnp.float32)
        residual = weight * far_wave * (1.0 - measured / jnp.maximum(modulus, 0.25))
        back_wave = rounded_wave(inverse_fft(residual))
        grad_terms = [None] * SLICES
        for layer_index in reversed(range(SLICES)):
            product = jnp.conj(waves[layer_index]) * back_wave
            grad_terms[layer_index] = jnp.stack((jnp.real(product), jnp.imag(product)))
            if layer_index > 0:
                pulled = jnp.conj(transmit[layer_index]) * back_wave
                back_wave = rounded_wave(inverse_fft(jnp.conj(chirp_table) * forward_fft(pulled)))
        update = jnp.stack(grad_terms)
        return gradient.at[:, :, row_index[:, None], col_index[None, :]].add(update)

    summed = lax.fori_loop(jnp.int32(0), jnp.int32(N_ROW * N_COL * MICRO), one_patch, jnp.zeros(object_field.shape, jnp.float32))
    return summed
```

```python
import functools
import math

import jax
import jax.numpy as jnp
import ml_dtypes
import numpy as np
from jax import lax
from jax.experimental import pallas as pl
from jax.experimental.pallas import tpu as pltpu
from jax.sharding import PartitionSpec as P

MESH = pl.DeviceIdType.MESH
SIDES = ((0, -1), (0, 1), (-1, -1), (-1, 1), (1, -1), (1, 1), (-1, 0), (1, 0))
SCALE = 16384.0
F32 = jnp.float32
BF16 = jnp.bfloat16


def split(values):
    high = values.astype(ml_dtypes.bfloat16)
    low = (values - high.astype(np.float64)).astype(ml_dtypes.bfloat16)
    return high, low


def tables(size):
    steps = np.arange(size)
    angles = 2.0 * math.pi * ((steps[:, None] * steps[None, :]) % size) / size
    fourier = np.exp(-1j * angles) / math.sqrt(size)
    frequency = (steps + size // 2) % size - size // 2
    chirp = np.exp(-1j * math.pi * frequency.astype(np.float64) ** 2 / (2.0 * size))
    spread = fourier.conj() @ (chirp[:, None] * fourier)
    packed = []
    for table in (spread, fourier):
        real_high, real_low = split(table.real)
        imag_high, imag_low = split(table.imag)
        packed.append(np.stack((real_high, imag_high, real_low, imag_low)))
    return np.stack(packed)


def dot(left, right):
    return jnp.dot(left, right, preferred_element_type=F32)


def halves(values):
    high = values.astype(BF16)
    return high, (values - high.astype(F32)).astype(BF16)


def kernel(
    tile, patch, n_row, n_col,
    pos, live, obj, probe, amp, tab, out,
    pad, win, wsend, grads, gpart, gpad, got_x, got_y, got_c, left3, right3, stack, wide,
    halo_send, halo_recv, win_send, win_recv, grad_send, grad_recv, rim_send, rim_recv,
):
    rim = patch // 2
    full = tile + patch
    span = patch + rim
    depth, row, col = lax.axis_index("depth"), lax.axis_index("row"), lax.axis_index("col")
    partner = (1 - depth, row, col)

    def neighbour(side):
        return (
            depth,
            lax.rem(row + side[0] + n_row, n_row),
            lax.rem(col + side[1] + n_col, n_col),
        )

    barrier = pltpu.get_barrier_semaphore()
    for side in SIDES:
        pl.semaphore_signal(barrier, inc=1, device_id=neighbour(side), device_id_type=MESH)
    pl.semaphore_signal(barrier, inc=1, device_id=partner, device_id_type=MESH)

    for part in range(2):
        pad[part, rim:rim + tile, rim:rim + tile] = (
            jnp.round(obj[0, part] * SCALE).astype(jnp.int32).astype(jnp.int16)
        )
    pl.semaphore_wait(barrier, len(SIDES) + 1)

    inner = {-1: (rim, rim), 0: (rim, tile), 1: (tile, rim)}
    outer = {-1: (rim + tile, rim), 0: (rim, tile), 1: (0, rim)}
    halo = []
    for index, (dy, dx) in enumerate(SIDES):
        halo.append(
            pltpu.make_async_remote_copy(
                src_ref=pad.at[:, pl.ds(*inner[dy]), pl.ds(*inner[dx])],
                dst_ref=pad.at[:, pl.ds(*outer[dy]), pl.ds(*outer[dx])],
                send_sem=halo_send.at[index],
                recv_sem=halo_recv.at[index],
                device_id=neighbour((dy, dx)),
                device_id_type=MESH,
            )
        )
        halo[-1].start()

    for which in range(2):
        for place, level in enumerate((0, 2, 0)):
            real, imag = tab[which, level], tab[which, level + 1]
            minus = -imag
            base = place * 2 * patch
            left3[which, 0:patch, base:base + patch] = real
            left3[which, 0:patch, base + patch:base + 2 * patch] = minus
            left3[which, patch:2 * patch, base:base + patch] = imag
            left3[which, patch:2 * patch, base + patch:base + 2 * patch] = real
            right3[which, base:base + patch, 0:patch] = real
            right3[which, base:base + patch, patch:2 * patch] = imag
            right3[which, base + patch:base + 2 * patch, 0:patch] = minus
            right3[which, base + patch:base + 2 * patch, patch:2 * patch] = real

    def transform3(real, imag, which):
        for part, values in enumerate((real, imag)):
            high, low = halves(values)
            at = part * patch
            stack[at:at + patch] = high
            stack[2 * patch + at:3 * patch + at] = high
            stack[4 * patch + at:5 * patch + at] = low
        mid = dot(left3[which], stack[...])
        for part in range(2):
            high, low = halves(mid[part * patch:(part + 1) * patch])
            at = part * patch
            wide[:, at:at + patch] = high
            wide[:, 2 * patch + at:3 * patch + at] = high
            wide[:, 4 * patch + at:5 * patch + at] = low
        end = dot(wide[...], right3[which])
        return end[:, :patch], end[:, patch:]

    def conjugate1(real, imag, which):
        stack[0:patch] = real.astype(BF16)
        stack[patch:2 * patch] = imag.astype(BF16)
        mid = dot(right3[which, 0:2 * patch], stack[0:2 * patch])
        wide[:, 0:patch] = mid[:patch].astype(BF16)
        wide[:, patch:2 * patch] = mid[patch:].astype(BF16)
        end = dot(wide[:, 0:2 * patch], left3[which, :, 0:2 * patch])
        return end[:, :patch], end[:, patch:]

    def extract(slot, store):
        first, second = pos[2 * slot], pos[2 * slot + 1]
        row_block = jnp.minimum(first >> 7, (full - span) // 128)
        col_block = jnp.minimum(second >> 7, (full - span) // 128)
        row_shift = first - row_block * 128
        col_shift = second - col_block * 128
        pick_rows = (
            lax.broadcasted_iota(jnp.int32, (patch, span), 1)
            == lax.broadcasted_iota(jnp.int32, (patch, span), 0) + row_shift
        ).astype(F32).astype(BF16)
        pick_cols = (
            lax.broadcasted_iota(jnp.int32, (span, patch), 0)
            == lax.broadcasted_iota(jnp.int32, (span, patch), 1) + col_shift
        ).astype(F32).astype(BF16)
        for part in range(2):
            block = pad[
                part,
                pl.ds(row_block * 128, span),
                pl.ds(col_block * 128, span),
            ].astype(F32)
            high, low = halves(block)
            rows = dot(pick_rows, jnp.concatenate((high, low), axis=1)).astype(BF16)
            cells = dot(rows[:, :span], pick_cols) + dot(rows[:, span:], pick_cols)
            store(part, cells.astype(jnp.int32).astype(jnp.int16))

    for copy in halo:
        copy.wait_recv()

    def to_send(part, cells):
        wsend[part] = cells

    extract(1 - depth, to_send)
    window_copy = pltpu.make_async_remote_copy(
        src_ref=wsend, dst_ref=win.at[depth], send_sem=win_send, recv_sem=win_recv,
        device_id=partner, device_id_type=MESH,
    )
    window_copy.start()

    def to_keep(part, cells):
        win[depth, part] = cells

    extract(depth, to_keep)

    @pl.when(depth == 1)
    def _():
        window_copy.wait_recv()

    def patch_of(section):
        return (
            win[section, 0].astype(F32) * (1.0 / SCALE),
            win[section, 1].astype(F32) * (1.0 / SCALE),
        )

    probe_real, probe_imag = probe[0].astype(F32), probe[1].astype(F32)
    obj_real, obj_imag = patch_of(0)
    wave_real, wave_imag = transform3(
        probe_real * obj_real - probe_imag * obj_imag,
        probe_real * obj_imag + probe_imag * obj_real,
        0,
    )
    wave_real = wave_real.astype(BF16).astype(F32)
    wave_imag = wave_imag.astype(BF16).astype(F32)

    @pl.when(depth == 0)
    def _():
        window_copy.wait_recv()

    obj_real, obj_imag = patch_of(1)
    far_real, far_imag = transform3(
        wave_real * obj_real - wave_imag * obj_imag,
        wave_real * obj_imag + wave_imag * obj_real,
        1,
    )
    power = far_real * far_real + far_imag * far_imag
    weight = live[depth].astype(F32)
    factor = weight * (1.0 - amp[0, 0, depth].astype(F32) * lax.rsqrt(jnp.maximum(power, 0.0625)))
    back_real, back_imag = conjugate1(far_real * factor, far_imag * factor, 1)
    back_real = back_real.astype(BF16).astype(F32)
    back_imag = back_imag.astype(BF16).astype(F32)
    grads[1, 0] = (wave_real * back_real + wave_imag * back_imag).astype(BF16)
    grads[1, 1] = (wave_real * back_imag - wave_imag * back_real).astype(BF16)

    grad_copy = pltpu.make_async_remote_copy(
        src_ref=grads.at[1 - depth], dst_ref=gpart, send_sem=grad_send, recv_sem=grad_recv,
        device_id=partner, device_id_type=MESH,
    )

    @pl.when(depth == 0)
    def _():
        grad_copy.start()

    back_real, back_imag = conjugate1(
        obj_real * back_real + obj_imag * back_imag,
        obj_real * back_imag - obj_imag * back_real,
        0,
    )
    back_real = back_real.astype(BF16).astype(F32)
    back_imag = back_imag.astype(BF16).astype(F32)
    grads[0, 0] = (probe_real * back_real + probe_imag * back_imag).astype(BF16)
    grads[0, 1] = (probe_real * back_imag - probe_imag * back_real).astype(BF16)

    @pl.when(depth == 1)
    def _():
        grad_copy.start()

    def put_rows(slot):
        return (
            lax.broadcasted_iota(jnp.int32, (full, patch), 0)
            == lax.broadcasted_iota(jnp.int32, (full, patch), 1) + pos[2 * slot]
        ).astype(F32).astype(BF16)

    def put_cols(slot):
        return (
            lax.broadcasted_iota(jnp.int32, (patch, full), 1)
            == lax.broadcasted_iota(jnp.int32, (patch, full), 0) + pos[2 * slot + 1]
        ).astype(F32).astype(BF16)

    place_rows = jnp.concatenate((put_rows(depth), put_rows(1 - depth)), axis=1)
    own_cols, other_cols = put_cols(depth), put_cols(1 - depth)
    spread_own = [dot(grads[depth, part], own_cols).astype(BF16) for part in range(2)]
    grad_copy.wait_recv()
    spread = [
        jnp.concatenate((spread_own[part], dot(gpart[part], other_cols).astype(BF16)), axis=0)
        for part in range(2)
    ]
    for part in range(2):
        gpad[part, :, 0:rim] = dot(place_rows, spread[part][:, 0:rim]).astype(BF16)
        gpad[part, :, rim + tile:] = dot(place_rows, spread[part][:, rim + tile:]).astype(BF16)

    edge = {-1: (0, rim), 0: (rim, tile), 1: (rim + tile, rim)}
    landing = {
        (0, -1): got_x.at[0], (0, 1): got_x.at[1],
        (-1, 0): got_y.at[0], (1, 0): got_y.at[1],
        (-1, -1): got_c.at[0], (-1, 1): got_c.at[1], (1, -1): got_c.at[2], (1, 1): got_c.at[3],
    }
    rims = {}
    for index, (dy, dx) in enumerate(SIDES):
        if (dy, dx) == (-1, 0):
            for part in range(2):
                gpad[part, 0:rim, rim:rim + tile] = dot(
                    place_rows[0:rim], spread[part][:, rim:rim + tile]
                ).astype(BF16)
                gpad[part, rim + tile:, rim:rim + tile] = dot(
                    place_rows[rim + tile:], spread[part][:, rim:rim + tile]
                ).astype(BF16)
        rims[dy, dx] = pltpu.make_async_remote_copy(
            src_ref=gpad.at[:, pl.ds(*edge[dy]), pl.ds(*edge[dx])],
            dst_ref=landing[dy, dx],
            send_sem=rim_send.at[index],
            recv_sem=rim_recv.at[index],
            device_id=neighbour((dy, dx)),
            device_id_type=MESH,
        )
        rims[dy, dx].start()

    for part in range(2):
        out[0, part] = dot(place_rows[rim:rim + tile], spread[part][:, rim:rim + tile])

    within = {-1: (tile - rim, rim), 0: (0, tile), 1: (0, rim)}
    for (dy, dx), copy in rims.items():
        copy.wait_recv()
        rows, cols = pl.ds(*within[dy]), pl.ds(*within[dx])
        for part in range(2):
            out[0, part, rows, cols] += landing[dy, dx][part].astype(F32)

    for copy in halo:
        copy.wait_send()
    window_copy.wait_send()
    grad_copy.wait_send()
    for copy in rims.values():
        copy.wait_send()


def on_device(object_field, probe, amplitude, positions, live):
    tile = object_field.shape[2]
    patch = probe.shape[1]
    rim = patch // 2
    full = tile + patch
    sides = len(SIDES)
    packed = jnp.asarray(tables(patch))
    vmem = pl.BlockSpec(memory_space=pltpu.VMEM)
    smem = pl.BlockSpec(memory_space=pltpu.SMEM)
    dma = pltpu.SemaphoreType.DMA
    return pl.pallas_call(
        functools.partial(
            kernel, tile, patch, lax.axis_size("row"), lax.axis_size("col")
        ),
        out_shape=jax.ShapeDtypeStruct(object_field.shape, F32),
        in_specs=[smem, smem, vmem, vmem, vmem, vmem],
        out_specs=vmem,
        scratch_shapes=[
            pltpu.VMEM((2, full, full), jnp.int16),
            pltpu.VMEM((2, 2, patch, patch), jnp.int16),
            pltpu.VMEM((2, patch, patch), jnp.int16),
            pltpu.VMEM((2, 2, patch, patch), BF16),
            pltpu.VMEM((2, patch, patch), BF16),
            pltpu.VMEM((2, full, full), BF16),
            pltpu.VMEM((2, 2, tile, rim), BF16),
            pltpu.VMEM((2, 2, rim, tile), BF16),
            pltpu.VMEM((4, 2, rim, rim), BF16),
            pltpu.VMEM((2, 2 * patch, 6 * patch), BF16),
            pltpu.VMEM((2, 6 * patch, 2 * patch), BF16),
            pltpu.VMEM((6 * patch, patch), BF16),
            pltpu.VMEM((patch, 6 * patch), BF16),
            dma((sides,)), dma((sides,)), dma, dma, dma, dma, dma((sides,)), dma((sides,)),
        ],
        compiler_params=pltpu.CompilerParams(
            collective_id=0, has_side_effects=True, vmem_limit_bytes=56 * 1024 * 1024
        ),
    )(positions.reshape(-1), live.reshape(-1), object_field, probe, amplitude, packed)


def solution(mesh):
    in_specs = (
        P("depth", None, "row", "col"),
        P(),
        P("row", "col", None, None, None),
        P("row", "col", None, None),
        P("row", "col", None),
    )
    out_specs = P("depth", None, "row", "col")
    return jax.shard_map(
        on_device, mesh=mesh, in_specs=in_specs, out_specs=out_specs, check_vma=False
    )
```

```python
import functools
import math

import jax
import jax.numpy as jnp
import ml_dtypes
import numpy as np
from jax import lax
from jax.experimental import pallas as pl
from jax.experimental.pallas import tpu as pltpu
from jax.sharding import PartitionSpec as P

MESH = pl.DeviceIdType.MESH
SIDES = ((0, -1), (0, 1), (-1, -1), (-1, 1), (1, -1), (1, 1), (-1, 0), (1, 0))
SCALE = 16384.0
F32 = jnp.float32
BF16 = jnp.bfloat16


def split(values):
    high = values.astype(ml_dtypes.bfloat16)
    low = (values - high.astype(np.float64)).astype(ml_dtypes.bfloat16)
    return high, low


def tables(size):
    steps = np.arange(size)
    angles = 2.0 * math.pi * ((steps[:, None] * steps[None, :]) % size) / size
    fourier = np.exp(-1j * angles) / math.sqrt(size)
    frequency = (steps + size // 2) % size - size // 2
    chirp = np.exp(-1j * math.pi * frequency.astype(np.float64) ** 2 / (2.0 * size))
    spread = fourier.conj() @ (chirp[:, None] * fourier)
    packed = []
    for table in (spread, fourier):
        real_high, real_low = split(table.real)
        imag_high, imag_low = split(table.imag)
        packed.append(np.stack((real_high, imag_high, real_low, imag_low)))
    return np.stack(packed)


def dot(left, right):
    return jnp.dot(left, right, preferred_element_type=F32)


def halves(values):
    high = values.astype(BF16)
    return high, (values - high.astype(F32)).astype(BF16)


def kernel(
    tile, patch, n_row, n_col,
    pos, live, obj_hbm, probe_hbm, amp_hbm, tab_hbm, out,
    obj, probe, amp, tab, pad, win, wave, grads, center, gpad, got_x, got_y, got_c,
    left3, right3, stack, wide,
    in_sem, halo_send, halo_recv, swap_send, swap_recv, rim_send, rim_recv,
):
    rim = patch // 2
    full = tile + patch
    span = patch + rim
    depth, row, col = lax.axis_index("depth"), lax.axis_index("row"), lax.axis_index("col")
    partner = (1 - depth, row, col)

    def neighbour(side):
        return (
            depth,
            lax.rem(row + side[0] + n_row, n_row),
            lax.rem(col + side[1] + n_col, n_col),
        )

    barrier = pltpu.get_barrier_semaphore()
    for side in SIDES:
        pl.semaphore_signal(barrier, inc=1, device_id=neighbour(side), device_id_type=MESH)
    pl.semaphore_signal(barrier, inc=1, device_id=partner, device_id_type=MESH)
    loads = [
        pltpu.make_async_copy(source, target, in_sem.at[index])
        for index, (source, target) in enumerate((
            (obj_hbm.at[0, 0], obj.at[0]), (obj_hbm.at[0, 1], obj.at[1]),
            (tab_hbm, tab), (probe_hbm, probe), (amp_hbm.at[0, 0], amp),
        ))
    ]
    for load in loads:
        load.start()

    for part in range(2):
        loads[part].wait()
        pad[part, rim:rim + tile, rim:rim + tile] = (
            jnp.round(obj[part] * SCALE).astype(jnp.int32).astype(jnp.int16)
        )
    pl.semaphore_wait(barrier, len(SIDES) + 1)

    inner = {-1: (rim, rim), 0: (rim, tile), 1: (tile, rim)}
    outer = {-1: (rim + tile, rim), 0: (rim, tile), 1: (0, rim)}
    halo = []
    for index, (dy, dx) in enumerate(SIDES):
        halo.append(
            pltpu.make_async_remote_copy(
                src_ref=pad.at[:, pl.ds(*inner[dy]), pl.ds(*inner[dx])],
                dst_ref=pad.at[:, pl.ds(*outer[dy]), pl.ds(*outer[dx])],
                send_sem=halo_send.at[index],
                recv_sem=halo_recv.at[index],
                device_id=neighbour((dy, dx)),
                device_id_type=MESH,
            )
        )
        halo[-1].start()

    loads[2].wait()
    for which in range(2):
        for place, level in enumerate((0, 2, 0)):
            real, imag = tab[which, level], tab[which, level + 1]
            minus = -imag
            base = place * 2 * patch
            left3[which, 0:patch, base:base + patch] = real
            left3[which, 0:patch, base + patch:base + 2 * patch] = minus
            left3[which, patch:2 * patch, base:base + patch] = imag
            left3[which, patch:2 * patch, base + patch:base + 2 * patch] = real
            right3[which, base:base + patch, 0:patch] = real
            right3[which, base:base + patch, patch:2 * patch] = imag
            right3[which, base + patch:base + 2 * patch, 0:patch] = minus
            right3[which, base + patch:base + 2 * patch, patch:2 * patch] = real

    def transform3(real, imag, which):
        for part, values in enumerate((real, imag)):
            high, low = halves(values)
            at = part * patch
            stack[at:at + patch] = high
            stack[2 * patch + at:3 * patch + at] = high
            stack[4 * patch + at:5 * patch + at] = low
        mid = dot(left3[which], stack[...])
        for part in range(2):
            high, low = halves(mid[part * patch:(part + 1) * patch])
            at = part * patch
            wide[:, at:at + patch] = high
            wide[:, 2 * patch + at:3 * patch + at] = high
            wide[:, 4 * patch + at:5 * patch + at] = low
        end = dot(wide[...], right3[which])
        return end[:, :patch], end[:, patch:]

    def conjugate1(real, imag, which):
        stack[0:patch] = real.astype(BF16)
        stack[patch:2 * patch] = imag.astype(BF16)
        mid = dot(right3[which, 0:2 * patch], stack[0:2 * patch])
        wide[:, 0:patch] = mid[:patch].astype(BF16)
        wide[:, patch:2 * patch] = mid[patch:].astype(BF16)
        end = dot(wide[:, 0:2 * patch], left3[which, :, 0:2 * patch])
        return end[:, :patch], end[:, patch:]

    def extract(slot):
        first, second = pos[0, 0, slot, 0], pos[0, 0, slot, 1]
        row_block = jnp.minimum(first >> 7, (full - span) // 128)
        col_block = jnp.minimum(second >> 7, (full - span) // 128)
        row_shift = first - row_block * 128
        col_shift = second - col_block * 128
        pick_rows = (
            lax.broadcasted_iota(jnp.int32, (patch, span), 1)
            == lax.broadcasted_iota(jnp.int32, (patch, span), 0) + row_shift
        ).astype(F32).astype(BF16)
        pick_cols = (
            lax.broadcasted_iota(jnp.int32, (span, patch), 0)
            == lax.broadcasted_iota(jnp.int32, (span, patch), 1) + col_shift
        ).astype(F32).astype(BF16)
        for part in range(2):
            block = pad[part, pl.ds(row_block * 128, span), pl.ds(col_block * 128, span)]
            high, low = halves(block.astype(F32))
            rows = dot(pick_rows, jnp.concatenate((high, low), axis=1)).astype(BF16)
            cells = dot(rows[:, :span], pick_cols) + dot(rows[:, span:], pick_cols)
            win[depth, slot, part] = cells.astype(jnp.int32).astype(jnp.int16)

    def swap(buffer, slot):
        return pltpu.make_async_remote_copy(
            src_ref=buffer.at[slot], dst_ref=buffer.at[slot],
            send_sem=swap_send.at[slot], recv_sem=swap_recv.at[slot],
            device_id=partner, device_id_type=MESH,
        )

    def patch_of(section, slot):
        return (
            win[section, slot, 0].astype(F32) * (1.0 / SCALE),
            win[section, slot, 1].astype(F32) * (1.0 / SCALE),
        )

    loads[3].wait()
    probe_real, probe_imag = probe[0].astype(F32), probe[1].astype(F32)
    for copy in halo:
        copy.wait_recv()

    for slot in range(2):
        extract(slot)

        @pl.when(depth == 1)
        def _():
            swap(win.at[1], slot).start()

    @pl.when(depth == 0)
    def _():
        for slot in range(2):
            obj_real, obj_imag = patch_of(0, slot)
            wave_real, wave_imag = transform3(
                probe_real * obj_real - probe_imag * obj_imag,
                probe_real * obj_imag + probe_imag * obj_real,
                0,
            )
            wave[slot, 0] = wave_real.astype(BF16)
            wave[slot, 1] = wave_imag.astype(BF16)
            swap(wave, slot).start()

    loads[4].wait()
    spread = []
    for slot in range(2):
        @pl.when(depth == 0)
        def _():
            swap(win.at[1], slot).wait_recv()

        @pl.when(depth == 1)
        def _():
            swap(wave, slot).wait_recv()

        wave_real, wave_imag = wave[slot, 0].astype(F32), wave[slot, 1].astype(F32)
        obj_real, obj_imag = patch_of(1, slot)
        far_real, far_imag = transform3(
            wave_real * obj_real - wave_imag * obj_imag,
            wave_real * obj_imag + wave_imag * obj_real,
            1,
        )
        power = far_real * far_real + far_imag * far_imag
        weight = live[0, 0, slot].astype(F32)
        factor = weight * (
            1.0 - amp[slot].astype(F32) * lax.rsqrt(jnp.maximum(power, 0.0625))
        )
        back_real, back_imag = conjugate1(far_real * factor, far_imag * factor, 1)
        back_real = back_real.astype(BF16).astype(F32)
        back_imag = back_imag.astype(BF16).astype(F32)

        @pl.when(depth == 1)
        def _():
            grads[slot, 0] = (wave_real * back_real + wave_imag * back_imag).astype(BF16)
            grads[slot, 1] = (wave_real * back_imag - wave_imag * back_real).astype(BF16)

        @pl.when(depth == 0)
        def _():
            first_real, first_imag = conjugate1(
                obj_real * back_real + obj_imag * back_imag,
                obj_real * back_imag - obj_imag * back_real,
                0,
            )
            first_real = first_real.astype(BF16).astype(F32)
            first_imag = first_imag.astype(BF16).astype(F32)
            grads[slot, 0] = (probe_real * first_real + probe_imag * first_imag).astype(BF16)
            grads[slot, 1] = (probe_real * first_imag - probe_imag * first_real).astype(BF16)

        put_cols = (
            lax.broadcasted_iota(jnp.int32, (patch, full), 1)
            == lax.broadcasted_iota(jnp.int32, (patch, full), 0) + pos[0, 0, slot, 1]
        ).astype(F32).astype(BF16)
        spread.append([dot(grads[slot, part], put_cols).astype(BF16) for part in range(2)])

    put_rows = [
        (
            lax.broadcasted_iota(jnp.int32, (full, patch), 0)
            == lax.broadcasted_iota(jnp.int32, (full, patch), 1) + pos[0, 0, slot, 0]
        ).astype(F32).astype(BF16)
        for slot in range(2)
    ]
    place_rows = jnp.concatenate(put_rows, axis=1)
    spread = [jnp.concatenate((spread[0][part], spread[1][part]), axis=0) for part in range(2)]
    for part in range(2):
        gpad[part, :, 0:rim] = dot(place_rows, spread[part][:, 0:rim]).astype(BF16)
        gpad[part, :, rim + tile:] = dot(place_rows, spread[part][:, rim + tile:]).astype(BF16)

    edge = {-1: (0, rim), 0: (rim, tile), 1: (rim + tile, rim)}
    landing = {
        (0, -1): got_x.at[0], (0, 1): got_x.at[1],
        (-1, 0): got_y.at[0], (1, 0): got_y.at[1],
        (-1, -1): got_c.at[0], (-1, 1): got_c.at[1], (1, -1): got_c.at[2], (1, 1): got_c.at[3],
    }
    rims = {}
    for index, (dy, dx) in enumerate(SIDES):
        if (dy, dx) == (-1, 0):
            for part in range(2):
                gpad[part, 0:rim, rim:rim + tile] = dot(
                    place_rows[0:rim], spread[part][:, rim:rim + tile]
                ).astype(BF16)
                gpad[part, rim + tile:, rim:rim + tile] = dot(
                    place_rows[rim + tile:], spread[part][:, rim:rim + tile]
                ).astype(BF16)
        rims[dy, dx] = pltpu.make_async_remote_copy(
            src_ref=gpad.at[:, pl.ds(*edge[dy]), pl.ds(*edge[dx])],
            dst_ref=landing[dy, dx],
            send_sem=rim_send.at[index],
            recv_sem=rim_recv.at[index],
            device_id=neighbour((dy, dx)),
            device_id_type=MESH,
        )
        rims[dy, dx].start()

    for part in range(2):
        center[part] = dot(place_rows[rim:rim + tile], spread[part][:, rim:rim + tile])

    starts = {1: (0, rim), 0: (rim, tile - 2 * rim), -1: (tile - rim, rim)}
    for copy in rims.values():
        copy.wait_recv()
    for down in (-1, 0, 1):
        for right in (-1, 0, 1):
            (top, height), (left, width) = starts[down], starts[right]
            rows, cols = pl.ds(top, height), pl.ds(left, width)
            for part in range(2):
                total = center[part, rows, cols]
                if right:
                    total = total + landing[0, right][part, rows, :].astype(F32)
                if down:
                    total = total + landing[down, 0][part, :, cols].astype(F32)
                if right and down:
                    total = total + landing[down, right][part].astype(F32)
                out[0, part, rows, cols] = total.astype(BF16)

    for copy in halo:
        copy.wait_send()
    for slot in range(2):
        swap(wave, slot).wait_send()
    for copy in rims.values():
        copy.wait_send()


def on_device(object_field, probe, amplitude, positions, live):
    tile = object_field.shape[2]
    patch = probe.shape[1]
    rim = patch // 2
    full = tile + patch
    sides = len(SIDES)
    packed = jnp.asarray(tables(patch))
    vmem = pl.BlockSpec(memory_space=pltpu.VMEM)
    smem = pl.BlockSpec(memory_space=pltpu.SMEM)
    hbm = pl.BlockSpec(memory_space=pl.ANY)
    dma = pltpu.SemaphoreType.DMA
    gradient = pl.pallas_call(
        functools.partial(
            kernel, tile, patch, lax.axis_size("row"), lax.axis_size("col")
        ),
        out_shape=jax.ShapeDtypeStruct(object_field.shape, BF16),
        in_specs=[smem, smem, hbm, hbm, hbm, hbm],
        out_specs=vmem,
        scratch_shapes=[
            pltpu.VMEM((2, tile, tile), F32),
            pltpu.VMEM((2, patch, patch), BF16),
            pltpu.VMEM((2, patch, patch), BF16),
            pltpu.VMEM(packed.shape, BF16),
            pltpu.VMEM((2, full, full), jnp.int16),
            pltpu.VMEM((2, 2, 2, patch, patch), jnp.int16),
            pltpu.VMEM((2, 2, patch, patch), BF16),
            pltpu.VMEM((2, 2, patch, patch), BF16),
            pltpu.VMEM((2, tile, tile), F32),
            pltpu.VMEM((2, full, full), BF16),
            pltpu.VMEM((2, 2, tile, rim), BF16),
            pltpu.VMEM((2, 2, rim, tile), BF16),
            pltpu.VMEM((4, 2, rim, rim), BF16),
            pltpu.VMEM((2, 2 * patch, 6 * patch), BF16),
            pltpu.VMEM((2, 6 * patch, 2 * patch), BF16),
            pltpu.VMEM((6 * patch, patch), BF16),
            pltpu.VMEM((patch, 6 * patch), BF16),
            dma((5,)), dma((sides,)), dma((sides,)), dma((2,)), dma((2,)),
            dma((sides,)), dma((sides,)),
        ],
        compiler_params=pltpu.CompilerParams(
            collective_id=0, has_side_effects=True, vmem_limit_bytes=56 * 1024 * 1024
        ),
    )(positions, live, object_field, probe, amplitude, packed)
    return gradient.astype(F32)


def solution(mesh):
    in_specs = (
        P("depth", None, "row", "col"),
        P(),
        P("row", "col", None, None, None),
        P("row", "col", None, None),
        P("row", "col", None),
    )
    out_specs = P("depth", None, "row", "col")
    return jax.shard_map(
        on_device, mesh=mesh, in_specs=in_specs, out_specs=out_specs, check_vma=False
    )
```

```python
import functools
import math

import jax
import jax.numpy as jnp
import ml_dtypes
import numpy as np
from jax import lax
from jax.experimental import pallas as pl
from jax.experimental.pallas import tpu as pltpu
from jax.sharding import PartitionSpec as P

MESH = pl.DeviceIdType.MESH
SCALE = 16384.0
F32 = jnp.float32
BF16 = jnp.bfloat16


def split(values):
    high = values.astype(ml_dtypes.bfloat16)
    low = (values - high.astype(np.float64)).astype(ml_dtypes.bfloat16)
    return high, low


def tables(size):
    steps = np.arange(size)
    angles = 2.0 * math.pi * ((steps[:, None] * steps[None, :]) % size) / size
    fourier = np.exp(-1j * angles) / math.sqrt(size)
    frequency = (steps + size // 2) % size - size // 2
    chirp = np.exp(-1j * math.pi * frequency.astype(np.float64) ** 2 / (2.0 * size))
    spread = fourier.conj() @ (chirp[:, None] * fourier)
    packed = []
    for table in (spread, fourier):
        real_high, real_low = split(table.real)
        imag_high, imag_low = split(table.imag)
        packed.append(np.stack((real_high, imag_high, real_low, imag_low)))
    return np.stack(packed)


def dot(left, right):
    return jnp.dot(left, right, preferred_element_type=F32)


def halves(values):
    high = values.astype(BF16)
    return high, (values - high.astype(F32)).astype(BF16)


def kernel(
    tile, patch, n_row, n_col,
    pos, live, obj_hbm, probe_hbm, amp_hbm, tab_hbm, out,
    obj, probe, amp, tab, pad, win, wave, grads, center, gpad, got_x, got_y, got_c,
    left3, right3, stack, wide,
    in_sem, halo_send, halo_recv, swap_send, swap_recv, rim_send, rim_recv,
):
    rim = patch // 2
    full = tile + patch
    span = patch + rim
    depth, row, col = lax.axis_index("depth"), lax.axis_index("row"), lax.axis_index("col")
    partner = (1 - depth, row, col)

    odd = lax.rem(col, 2)
    away = 2 * odd - 1
    mate = (depth, row, col - away)
    cross = (depth, row, lax.rem(col + away + n_col, n_col))
    along = [(depth, lax.rem(row + step + n_row, n_row), col) for step in (-1, 1)]

    def send(source, target, sems, index, device):
        copy = pltpu.make_async_remote_copy(
            src_ref=source, dst_ref=target, send_sem=sems[0].at[index],
            recv_sem=sems[1].at[index], device_id=device, device_id_type=MESH,
        )
        copy.start()
        return copy

    barrier = pltpu.get_barrier_semaphore()
    for device in (mate, cross, *along, partner):
        pl.semaphore_signal(barrier, inc=1, device_id=device, device_id_type=MESH)
    loads = [
        pltpu.make_async_copy(source, target, in_sem.at[index])
        for index, (source, target) in enumerate((
            (obj_hbm.at[0, 0], obj.at[0]), (obj_hbm.at[0, 1], obj.at[1]),
            (tab_hbm, tab), (probe_hbm, probe), (amp_hbm.at[0, 0], amp),
        ))
    ]
    for load in loads:
        load.start()

    for part in range(2):
        loads[part].wait()
        pad[part, rim:rim + tile, rim:rim + tile] = (
            jnp.round(obj[part] * SCALE).astype(jnp.int32).astype(jnp.int16)
        )
    pl.semaphore_wait(barrier, 5)

    last = tile // rim
    near_mate, near_cross = pl.ds(rim * (last - (last - 1) * odd), rim), pl.ds(rim * (1 + (last - 1) * odd), rim)
    past_mate, past_cross = pl.ds(rim * ((last + 1) * (1 - odd)), rim), pl.ds(rim * ((last + 1) * odd), rim)
    middle = pl.ds(rim, tile)
    inner_rows = (pl.ds(rim, rim), pl.ds(tile, rim))
    outer_rows = (pl.ds(rim + tile, rim), pl.ds(0, rim))
    halo_sems = (halo_send, halo_recv)
    halo = [
        send(pad.at[:, rows, near_cross], pad.at[:, rows, past_mate], halo_sems, index, cross)
        for index, rows in enumerate((*inner_rows, pl.ds(2 * rim, tile - 2 * rim)))
    ]
    halo += [
        send(pad.at[:, inner_rows[k], middle], pad.at[:, outer_rows[k], middle], halo_sems, 3 + k, along[k])
        for k in range(2)
    ]
    halo.append(send(pad.at[:, middle, near_mate], pad.at[:, middle, past_cross], halo_sems, 5, mate))

    loads[2].wait()
    for which in range(2):
        for place, level in enumerate((0, 2, 0)):
            real, imag = tab[which, level], tab[which, level + 1]
            minus = -imag
            base = place * 2 * patch
            left3[which, 0:patch, base:base + patch] = real
            left3[which, 0:patch, base + patch:base + 2 * patch] = minus
            left3[which, patch:2 * patch, base:base + patch] = imag
            left3[which, patch:2 * patch, base + patch:base + 2 * patch] = real
            right3[which, base:base + patch, 0:patch] = real
            right3[which, base:base + patch, patch:2 * patch] = imag
            right3[which, base + patch:base + 2 * patch, 0:patch] = minus
            right3[which, base + patch:base + 2 * patch, patch:2 * patch] = real

    def transform3(real, imag, which):
        for part, values in enumerate((real, imag)):
            high, low = halves(values)
            at = part * patch
            stack[at:at + patch] = high
            stack[2 * patch + at:3 * patch + at] = high
            stack[4 * patch + at:5 * patch + at] = low
        mid = dot(left3[which], stack[...])
        for part in range(2):
            high, low = halves(mid[part * patch:(part + 1) * patch])
            at = part * patch
            wide[:, at:at + patch] = high
            wide[:, 2 * patch + at:3 * patch + at] = high
            wide[:, 4 * patch + at:5 * patch + at] = low
        end = dot(wide[...], right3[which])
        return end[:, :patch], end[:, patch:]

    def conjugate1(real, imag, which):
        stack[0:patch] = real.astype(BF16)
        stack[patch:2 * patch] = imag.astype(BF16)
        mid = dot(right3[which, 0:2 * patch], stack[0:2 * patch])
        wide[:, 0:patch] = mid[:patch].astype(BF16)
        wide[:, patch:2 * patch] = mid[patch:].astype(BF16)
        end = dot(wide[:, 0:2 * patch], left3[which, :, 0:2 * patch])
        return end[:, :patch], end[:, patch:]

    def extract(slot):
        first, second = pos[0, 0, slot, 0], pos[0, 0, slot, 1]
        row_block = jnp.minimum(first >> 7, (full - span) // 128)
        col_block = jnp.minimum(second >> 7, (full - span) // 128)
        row_shift = first - row_block * 128
        col_shift = second - col_block * 128
        pick_rows = (
            lax.broadcasted_iota(jnp.int32, (patch, span), 1)
            == lax.broadcasted_iota(jnp.int32, (patch, span), 0) + row_shift
        ).astype(F32).astype(BF16)
        pick_cols = (
            lax.broadcasted_iota(jnp.int32, (span, patch), 0)
            == lax.broadcasted_iota(jnp.int32, (span, patch), 1) + col_shift
        ).astype(F32).astype(BF16)
        for part in range(2):
            block = pad[part, pl.ds(row_block * 128, span), pl.ds(col_block * 128, span)]
            high, low = halves(block.astype(F32))
            rows = dot(pick_rows, jnp.concatenate((high, low), axis=1)).astype(BF16)
            cells = dot(rows[:, :span], pick_cols) + dot(rows[:, span:], pick_cols)
            win[depth, slot, part] = cells.astype(jnp.int32).astype(jnp.int16)

    def swap(buffer, slot):
        return pltpu.make_async_remote_copy(
            src_ref=buffer.at[slot], dst_ref=buffer.at[slot],
            send_sem=swap_send.at[slot], recv_sem=swap_recv.at[slot],
            device_id=partner, device_id_type=MESH,
        )

    def patch_of(section, slot):
        return (
            win[section, slot, 0].astype(F32) * (1.0 / SCALE),
            win[section, slot, 1].astype(F32) * (1.0 / SCALE),
        )

    loads[3].wait()
    loads[4].wait()
    probe_real, probe_imag = probe[0].astype(F32), probe[1].astype(F32)
    for k in range(2):
        halo[k].wait_recv()
        halo.append(
            send(
                pad.at[:, inner_rows[k], past_cross], pad.at[:, outer_rows[k], past_cross],
                halo_sems, 6 + k, along[k],
            )
        )
    for k in range(2):
        halo[3 + k].wait_recv()
        halo.append(
            send(
                pad.at[:, outer_rows[k], near_mate], pad.at[:, outer_rows[k], past_cross],
                halo_sems, 8 + k, mate,
            )
        )
    for copy in (halo[2], *halo[5:]):
        copy.wait_recv()

    @pl.when(depth == 1)
    def _():
        for slot in range(2):
            extract(slot)
            swap(win.at[1], slot).start()

    @pl.when(depth == 0)
    def _():
        for slot in range(2):
            extract(slot)
            obj_real, obj_imag = patch_of(0, slot)
            wave_real, wave_imag = transform3(
                probe_real * obj_real - probe_imag * obj_imag,
                probe_real * obj_imag + probe_imag * obj_real,
                0,
            )
            wave[slot, 0] = wave_real.astype(BF16)
            wave[slot, 1] = wave_imag.astype(BF16)
            swap(wave, slot).start()

    spread = []
    for slot in range(2):
        @pl.when(depth == 0)
        def _():
            swap(win.at[1], slot).wait_recv()

        @pl.when(depth == 1)
        def _():
            swap(wave, slot).wait_recv()

        wave_real, wave_imag = wave[slot, 0].astype(F32), wave[slot, 1].astype(F32)
        obj_real, obj_imag = patch_of(1, slot)
        far_real, far_imag = transform3(
            wave_real * obj_real - wave_imag * obj_imag,
            wave_real * obj_imag + wave_imag * obj_real,
            1,
        )
        power = far_real * far_real + far_imag * far_imag
        weight = live[0, 0, slot].astype(F32)
        factor = weight * (
            1.0 - amp[slot].astype(F32) * lax.rsqrt(jnp.maximum(power, 0.0625))
        )
        back_real, back_imag = conjugate1(far_real * factor, far_imag * factor, 1)
        back_real = back_real.astype(BF16).astype(F32)
        back_imag = back_imag.astype(BF16).astype(F32)

        @pl.when(depth == 1)
        def _():
            grads[slot, 0] = (wave_real * back_real + wave_imag * back_imag).astype(BF16)
            grads[slot, 1] = (wave_real * back_imag - wave_imag * back_real).astype(BF16)

        @pl.when(depth == 0)
        def _():
            first_real, first_imag = conjugate1(
                obj_real * back_real + obj_imag * back_imag,
                obj_real * back_imag - obj_imag * back_real,
                0,
            )
            first_real = first_real.astype(BF16).astype(F32)
            first_imag = first_imag.astype(BF16).astype(F32)
            grads[slot, 0] = (probe_real * first_real + probe_imag * first_imag).astype(BF16)
            grads[slot, 1] = (probe_real * first_imag - probe_imag * first_real).astype(BF16)

        put_cols = (
            lax.broadcasted_iota(jnp.int32, (patch, full), 1)
            == lax.broadcasted_iota(jnp.int32, (patch, full), 0) + pos[0, 0, slot, 1]
        ).astype(F32).astype(BF16)
        spread.append([dot(grads[slot, part], put_cols).astype(BF16) for part in range(2)])

    put_rows = [
        (
            lax.broadcasted_iota(jnp.int32, (full, patch), 0)
            == lax.broadcasted_iota(jnp.int32, (full, patch), 1) + pos[0, 0, slot, 0]
        ).astype(F32).astype(BF16)
        for slot in range(2)
    ]
    place_rows = jnp.concatenate(put_rows, axis=1)
    spread = [jnp.concatenate((spread[0][part], spread[1][part]), axis=0) for part in range(2)]
    for part in range(2):
        sides = jnp.concatenate((spread[part][:, 0:rim], spread[part][:, rim + tile:]), axis=1)
        sides = dot(place_rows, sides).astype(BF16)
        gpad[part, :, 0:rim] = sides[:, 0:rim]
        gpad[part, :, rim + tile:] = sides[:, rim:]

    rim_sems = (rim_send, rim_recv)
    edge_rows = (pl.ds(0, rim), pl.ds(rim + tile, rim))
    rims = [
        send(gpad.at[:, edge_rows[k], past_cross], got_c.at[0, k], rim_sems, k, along[k])
        for k in range(2)
    ]
    rims += [
        send(gpad.at[:, edge_rows[k], past_mate], got_c.at[1, k], rim_sems, 2 + k, mate)
        for k in range(2)
    ]
    rims.append(
        send(
            gpad.at[:, pl.ds(2 * rim, tile - 2 * rim), past_cross],
            got_x.at[odd, :, pl.ds(rim, tile - 2 * rim)], rim_sems, 4, cross,
        )
    )
    rims.append(send(gpad.at[:, middle, past_mate], got_x.at[1 - odd], rim_sems, 5, mate))
    for part in range(2):
        ends = jnp.concatenate((place_rows[0:rim], place_rows[rim + tile:]), axis=0)
        ends = dot(ends, spread[part][:, rim:rim + tile]).astype(BF16)
        gpad[part, 0:rim, rim:rim + tile] = ends[0:rim]
        gpad[part, rim + tile:, rim:rim + tile] = ends[rim:]
    for k in range(2):
        rims[2 + k].wait_recv()
        for part in range(2):
            total = gpad[part, edge_rows[k], near_mate].astype(F32) + got_c[1, k, part].astype(F32)
            gpad[part, edge_rows[k], near_mate] = total.astype(BF16)
        rims.append(
            send(gpad.at[:, edge_rows[k], middle], got_y.at[k], rim_sems, 6 + k, along[k])
        )

    for part in range(2):
        center[part] = dot(place_rows[rim:rim + tile], spread[part][:, rim:rim + tile])

    for k in range(2):
        rims[k].wait_recv()
        rows = inner_rows[1 - k]
        for part in range(2):
            total = gpad[part, rows, past_cross].astype(F32) + got_c[0, k, part].astype(F32)
            gpad[part, rows, past_cross] = total.astype(BF16)
        rims.append(
            send(
                gpad.at[:, rows, past_cross], got_x.at[odd, :, pl.ds((1 - k) * (tile - rim), rim)],
                rim_sems, 8 + k, cross,
            )
        )
    for copy in rims[4:]:
        copy.wait_recv()
    starts = {1: (0, rim), 0: (rim, tile - 2 * rim), -1: (tile - rim, rim)}
    for down in (-1, 0, 1):
        for right in (-1, 0, 1):
            (top, height), (left, width) = starts[down], starts[right]
            rows, cols = pl.ds(top, height), pl.ds(left, width)
            for part in range(2):
                total = center[part, rows, cols]
                if right:
                    total = total + got_x[(1 + right) // 2, part, rows, :].astype(F32)
                if down:
                    total = total + got_y[(1 + down) // 2, part, :, cols].astype(F32)
                out[0, part, rows, cols] = total

    for copy in halo:
        copy.wait_send()
    for slot in range(2):
        swap(wave, slot).wait_send()
    for copy in rims:
        copy.wait_send()


def on_device(object_field, probe, amplitude, positions, live):
    tile = object_field.shape[2]
    patch = probe.shape[1]
    rim = patch // 2
    full = tile + patch
    packed = jnp.asarray(tables(patch))
    vmem = pl.BlockSpec(memory_space=pltpu.VMEM)
    smem = pl.BlockSpec(memory_space=pltpu.SMEM)
    hbm = pl.BlockSpec(memory_space=pl.ANY)
    dma = pltpu.SemaphoreType.DMA
    gradient = pl.pallas_call(
        functools.partial(
            kernel, tile, patch, lax.axis_size("row"), lax.axis_size("col")
        ),
        out_shape=pltpu.VMEM(object_field.shape, F32),
        in_specs=[smem, smem, hbm, hbm, hbm, hbm],
        out_specs=vmem,
        scratch_shapes=[
            pltpu.VMEM((2, tile, tile), F32),
            pltpu.VMEM((2, patch, patch), BF16),
            pltpu.VMEM((2, patch, patch), BF16),
            pltpu.VMEM(packed.shape, BF16),
            pltpu.VMEM((2, full, full), jnp.int16),
            pltpu.VMEM((2, 2, 2, patch, patch), jnp.int16),
            pltpu.VMEM((2, 2, patch, patch), BF16),
            pltpu.VMEM((2, 2, patch, patch), BF16),
            pltpu.VMEM((2, tile, tile), F32),
            pltpu.VMEM((2, full, full), BF16),
            pltpu.VMEM((2, 2, tile, rim), BF16),
            pltpu.VMEM((2, 2, rim, tile), BF16),
            pltpu.VMEM((2, 2, 2, rim, rim), BF16),
            pltpu.VMEM((2, 2 * patch, 6 * patch), BF16),
            pltpu.VMEM((2, 6 * patch, 2 * patch), BF16),
            pltpu.VMEM((6 * patch, patch), BF16),
            pltpu.VMEM((patch, 6 * patch), BF16),
            dma((5,)), dma((10,)), dma((10,)), dma((2,)), dma((2,)), dma((10,)), dma((10,)),
        ],
        compiler_params=pltpu.CompilerParams(
            collective_id=0, has_side_effects=True, vmem_limit_bytes=56 * 1024 * 1024
        ),
    )(positions, live, object_field, probe, amplitude, packed)
    return gradient


def solution(mesh):
    in_specs = (
        P("depth", None, "row", "col"),
        P(),
        P("row", "col", None, None, None),
        P("row", "col", None, None),
        P("row", "col", None),
    )
    out_specs = P("depth", None, "row", "col")
    return jax.shard_map(
        on_device, mesh=mesh, in_specs=in_specs, out_specs=out_specs, check_vma=False
    )
```

```python
import functools
import math

import jax
import jax.numpy as jnp
import ml_dtypes
import numpy as np
from jax import lax
from jax.experimental import pallas as pl
from jax.experimental.pallas import tpu as pltpu
from jax.sharding import PartitionSpec as P

MESH = pl.DeviceIdType.MESH
SCALE = 16384.0
F32 = jnp.float32
BF16 = jnp.bfloat16


def split(values):
    high = values.astype(ml_dtypes.bfloat16)
    low = (values - high.astype(np.float64)).astype(ml_dtypes.bfloat16)
    return high, low


def tables(size):
    steps = np.arange(size)
    angles = 2.0 * math.pi * ((steps[:, None] * steps[None, :]) % size) / size
    fourier = np.exp(-1j * angles) / math.sqrt(size)
    frequency = (steps + size // 2) % size - size // 2
    chirp = np.exp(-1j * math.pi * frequency.astype(np.float64) ** 2 / (2.0 * size))
    spread = fourier.conj() @ (chirp[:, None] * fourier)
    packed = []
    for table in (spread, fourier):
        real_high, real_low = split(table.real)
        imag_high, imag_low = split(table.imag)
        packed.append(np.stack((real_high, imag_high, real_low, imag_low)))
    return np.stack(packed)


def dot(left, right):
    return jnp.dot(left, right, preferred_element_type=F32)


def halves(values):
    high = values.astype(BF16)
    return high, (values - high.astype(F32)).astype(BF16)


def kernel(
    tile, patch, n_row, n_col,
    pos, live, obj_hbm, probe_hbm, amp_hbm, tab_hbm, out,
    obj, probe, amp, tab, pad, win, wave, grads, center, gpad, got_x, got_y, got_c,
    left3, right3, stack, wide, pick_rows, pick_cols, put_rows, put_cols, spread,
    in_sem, halo_send, halo_recv, swap_send, swap_recv, rim_send, rim_recv,
):
    rim = patch // 2
    full = tile + patch
    span = patch + rim
    depth, row, col = lax.axis_index("depth"), lax.axis_index("row"), lax.axis_index("col")
    partner = (1 - depth, row, col)

    odd = lax.rem(col, 2)
    away = 2 * odd - 1
    mate = (depth, row, col - away)
    cross = (depth, row, lax.rem(col + away + n_col, n_col))
    along = [(depth, lax.rem(row + step + n_row, n_row), col) for step in (-1, 1)]

    def send(source, target, sems, index, device):
        copy = pltpu.make_async_remote_copy(
            src_ref=source, dst_ref=target, send_sem=sems[0].at[index],
            recv_sem=sems[1].at[index], device_id=device, device_id_type=MESH,
        )
        copy.start()
        return copy

    barrier = pltpu.get_barrier_semaphore()
    for device in (mate, cross, *along, partner):
        pl.semaphore_signal(barrier, inc=1, device_id=device, device_id_type=MESH)
    loads = [
        pltpu.make_async_copy(source, target, in_sem.at[index])
        for index, (source, target) in enumerate((
            (obj_hbm.at[0, 0], obj.at[0]), (obj_hbm.at[0, 1], obj.at[1]),
            (tab_hbm, tab), (probe_hbm, probe), (amp_hbm.at[0, 0], amp),
        ))
    ]
    for load in loads:
        load.start()

    for part in range(2):
        loads[part].wait()
        pad[part, rim:rim + tile, rim:rim + tile] = (
            jnp.round(obj[part] * SCALE).astype(jnp.int32).astype(jnp.int16)
        )
    pl.semaphore_wait(barrier, 5)

    last = tile // rim
    near_mate, near_cross = pl.ds(rim * (last - (last - 1) * odd), rim), pl.ds(rim * (1 + (last - 1) * odd), rim)
    past_mate, past_cross = pl.ds(rim * ((last + 1) * (1 - odd)), rim), pl.ds(rim * ((last + 1) * odd), rim)
    middle = pl.ds(rim, tile)
    inner_rows = (pl.ds(rim, rim), pl.ds(tile, rim))
    outer_rows = (pl.ds(rim + tile, rim), pl.ds(0, rim))
    halo_sems = (halo_send, halo_recv)
    halo = [
        send(pad.at[:, rows, near_cross], pad.at[:, rows, past_mate], halo_sems, index, cross)
        for index, rows in enumerate((*inner_rows, pl.ds(2 * rim, tile - 2 * rim)))
    ]
    halo += [
        send(pad.at[:, inner_rows[k], middle], pad.at[:, outer_rows[k], middle], halo_sems, 3 + k, along[k])
        for k in range(2)
    ]
    halo.append(send(pad.at[:, middle, near_mate], pad.at[:, middle, past_cross], halo_sems, 5, mate))

    loads[2].wait()
    for which in range(2):
        for place, level in enumerate((0, 2, 0)):
            real, imag = tab[which, level], tab[which, level + 1]
            minus = -imag
            base = place * 2 * patch
            left3[which, 0:patch, base:base + patch] = real
            left3[which, 0:patch, base + patch:base + 2 * patch] = minus
            left3[which, patch:2 * patch, base:base + patch] = imag
            left3[which, patch:2 * patch, base + patch:base + 2 * patch] = real
            right3[which, base:base + patch, 0:patch] = real
            right3[which, base:base + patch, patch:2 * patch] = imag
            right3[which, base + patch:base + 2 * patch, 0:patch] = minus
            right3[which, base + patch:base + 2 * patch, patch:2 * patch] = real

    def transform3(real, imag, which):
        for part, values in enumerate((real, imag)):
            high, low = halves(values)
            at = part * patch
            stack[at:at + patch] = high
            stack[2 * patch + at:3 * patch + at] = high
            stack[4 * patch + at:5 * patch + at] = low
        mid = dot(left3[which], stack[...])
        for part in range(2):
            high, low = halves(mid[part * patch:(part + 1) * patch])
            at = part * patch
            wide[:, at:at + patch] = high
            wide[:, 2 * patch + at:3 * patch + at] = high
            wide[:, 4 * patch + at:5 * patch + at] = low
        end = dot(wide[...], right3[which])
        return end[:, :patch], end[:, patch:]

    def conjugate1(real, imag, which):
        stack[0:patch] = real.astype(BF16)
        stack[patch:2 * patch] = imag.astype(BF16)
        mid = dot(right3[which, 0:2 * patch], stack[0:2 * patch])
        wide[:, 0:patch] = mid[:patch].astype(BF16)
        wide[:, patch:2 * patch] = mid[patch:].astype(BF16)
        end = dot(wide[:, 0:2 * patch], left3[which, :, 0:2 * patch])
        return end[:, :patch], end[:, patch:]

    def one_hot(shape, axis, shift):
        hit = (
            lax.broadcasted_iota(jnp.int32, shape, axis)
            == lax.broadcasted_iota(jnp.int32, shape, 1 - axis) + shift
        )
        return hit.astype(F32).astype(BF16)

    blocks = []
    for slot in range(2):
        first, second = pos[0, 0, slot, 0], pos[0, 0, slot, 1]
        row_block = jnp.minimum(first >> 7, (full - span) // 128)
        col_block = jnp.minimum(second >> 7, (full - span) // 128)
        blocks.append((row_block, col_block))
        pick_rows[slot] = one_hot((patch, span), 1, first - row_block * 128)
        pick_cols[slot] = one_hot((span, patch), 0, second - col_block * 128)
        put_rows[:, slot * patch:(slot + 1) * patch] = one_hot((full, patch), 0, first)
        put_cols[slot] = one_hot((patch, full), 1, second)

    def extract(slot, part):
        row_block, col_block = blocks[slot]
        block = pad[part, pl.ds(row_block * 128, span), pl.ds(col_block * 128, span)]
        high, low = halves(block.astype(F32))
        rows = dot(pick_rows[slot], jnp.concatenate((high, low), axis=1)).astype(BF16)
        cells = dot(rows[:, :span], pick_cols[slot]) + dot(rows[:, span:], pick_cols[slot])
        win[depth, slot, part] = cells.astype(jnp.int32).astype(jnp.int16)

    def swap(buffer, index):
        return pltpu.make_async_remote_copy(
            src_ref=buffer, dst_ref=buffer,
            send_sem=swap_send.at[index], recv_sem=swap_recv.at[index],
            device_id=partner, device_id_type=MESH,
        )

    def patch_of(section, slot):
        return (
            win[section, slot, 0].astype(F32) * (1.0 / SCALE),
            win[section, slot, 1].astype(F32) * (1.0 / SCALE),
        )

    loads[3].wait()
    loads[4].wait()
    probe_real, probe_imag = probe[0].astype(F32), probe[1].astype(F32)
    for k in range(2):
        halo[k].wait_recv()
        halo.append(
            send(
                pad.at[:, inner_rows[k], past_cross], pad.at[:, outer_rows[k], past_cross],
                halo_sems, 6 + k, along[k],
            )
        )
    for k in range(2):
        halo[3 + k].wait_recv()
        halo.append(
            send(
                pad.at[:, outer_rows[k], near_mate], pad.at[:, outer_rows[k], past_cross],
                halo_sems, 8 + k, mate,
            )
        )
    for copy in (halo[2], *halo[5:]):
        copy.wait_recv()

    def propagate(slot):
        obj_real, obj_imag = patch_of(0, slot)
        wave_real, wave_imag = transform3(
            probe_real * obj_real - probe_imag * obj_imag,
            probe_real * obj_imag + probe_imag * obj_real,
            0,
        )
        wave[slot, 0] = wave_real.astype(BF16)
        wave[slot, 1] = wave_imag.astype(BF16)

    for part in range(2):
        extract(0, part)
        swap(win.at[depth, 0, part], part).start()
    for part in range(2):
        extract(1, part)

    @pl.when(depth == 0)
    def _():
        propagate(1)
        swap(wave.at[1], 2).start()

    @pl.when(depth == 1)
    def _():
        swap(win.at[1, 1], 2).start()
        for part in range(2):
            swap(win.at[1, 0, part], part).wait_recv()

    propagate(0)

    @pl.when(depth == 0)
    def _():
        for part in range(2):
            swap(win.at[0, 0, part], part).wait_recv()

    for slot in range(2):
        if slot == 1:
            swap(wave.at[1], 2).wait_recv()

        wave_real, wave_imag = wave[slot, 0].astype(F32), wave[slot, 1].astype(F32)
        obj_real, obj_imag = patch_of(1, slot)
        far_real, far_imag = transform3(
            wave_real * obj_real - wave_imag * obj_imag,
            wave_real * obj_imag + wave_imag * obj_real,
            1,
        )
        power = far_real * far_real + far_imag * far_imag
        weight = live[0, 0, slot].astype(F32)
        factor = weight * (
            1.0 - amp[slot].astype(F32) * lax.rsqrt(jnp.maximum(power, 0.0625))
        )
        back_real, back_imag = conjugate1(far_real * factor, far_imag * factor, 1)
        back_real = back_real.astype(BF16).astype(F32)
        back_imag = back_imag.astype(BF16).astype(F32)

        @pl.when(depth == 1)
        def _():
            grads[slot, 0] = (wave_real * back_real + wave_imag * back_imag).astype(BF16)
            grads[slot, 1] = (wave_real * back_imag - wave_imag * back_real).astype(BF16)

        @pl.when(depth == 0)
        def _():
            first_real, first_imag = conjugate1(
                obj_real * back_real + obj_imag * back_imag,
                obj_real * back_imag - obj_imag * back_real,
                0,
            )
            first_real = first_real.astype(BF16).astype(F32)
            first_imag = first_imag.astype(BF16).astype(F32)
            grads[slot, 0] = (probe_real * first_real + probe_imag * first_imag).astype(BF16)
            grads[slot, 1] = (probe_real * first_imag - probe_imag * first_real).astype(BF16)

        for part in range(2):
            spread[part, slot * patch:(slot + 1) * patch] = dot(
                grads[slot, part], put_cols[slot]
            ).astype(BF16)

    for part in range(2):
        sides = jnp.concatenate((spread[part, :, 0:rim], spread[part, :, rim + tile:]), axis=1)
        sides = dot(put_rows[...], sides).astype(BF16)
        gpad[part, :, 0:rim] = sides[:, 0:rim]
        gpad[part, :, rim + tile:] = sides[:, rim:]

    rim_sems = (rim_send, rim_recv)
    edge_rows = (pl.ds(0, rim), pl.ds(rim + tile, rim))
    rims = [
        send(gpad.at[:, edge_rows[k], past_cross], got_c.at[0, k], rim_sems, k, along[k])
        for k in range(2)
    ]
    rims += [
        send(gpad.at[:, edge_rows[k], past_mate], got_c.at[1, k], rim_sems, 2 + k, mate)
        for k in range(2)
    ]
    rims.append(
        send(
            gpad.at[:, pl.ds(2 * rim, tile - 2 * rim), past_cross],
            got_x.at[odd, :, pl.ds(rim, tile - 2 * rim)], rim_sems, 4, cross,
        )
    )
    rims.append(send(gpad.at[:, middle, past_mate], got_x.at[1 - odd], rim_sems, 5, mate))
    for part in range(2):
        ends = jnp.concatenate((put_rows[0:rim], put_rows[rim + tile:]), axis=0)
        ends = dot(ends, spread[part, :, rim:rim + tile]).astype(BF16)
        gpad[part, 0:rim, rim:rim + tile] = ends[0:rim]
        gpad[part, rim + tile:, rim:rim + tile] = ends[rim:]
    for k in range(2):
        rims[2 + k].wait_recv()
        for part in range(2):
            total = gpad[part, edge_rows[k], near_mate].astype(F32) + got_c[1, k, part].astype(F32)
            gpad[part, edge_rows[k], near_mate] = total.astype(BF16)
        rims.append(
            send(gpad.at[:, edge_rows[k], middle], got_y.at[k], rim_sems, 6 + k, along[k])
        )

    for part in range(2):
        center[part] = dot(put_rows[rim:rim + tile], spread[part, :, rim:rim + tile])

    for k in range(2):
        rims[k].wait_recv()
        rows = inner_rows[1 - k]
        for part in range(2):
            total = gpad[part, rows, past_cross].astype(F32) + got_c[0, k, part].astype(F32)
            gpad[part, rows, past_cross] = total.astype(BF16)
        rims.append(
            send(
                gpad.at[:, rows, past_cross], got_x.at[odd, :, pl.ds((1 - k) * (tile - rim), rim)],
                rim_sems, 8 + k, cross,
            )
        )
    for copy in rims[4:8]:
        copy.wait_recv()
    starts = {1: (0, rim), 0: (rim, tile - 2 * rim), -1: (tile - rim, rim)}
    for down in (0, -1, 1):
        if down:
            rims[8 + (1 + down) // 2].wait_recv()
        for right in (-1, 0, 1):
            (top, height), (left, width) = starts[down], starts[right]
            rows, cols = pl.ds(top, height), pl.ds(left, width)
            for part in range(2):
                total = center[part, rows, cols]
                if right:
                    total = total + got_x[(1 + right) // 2, part, rows, :].astype(F32)
                if down:
                    total = total + got_y[(1 + down) // 2, part, :, cols].astype(F32)
                out[0, part, rows, cols] = total

    for copy in halo:
        copy.wait_send()
    for part in range(2):
        swap(win.at[depth, 0, part], part).wait_send()
    swap(wave.at[1], 2).wait_send()
    for copy in rims:
        copy.wait_send()


def on_device(object_field, probe, amplitude, positions, live):
    tile = object_field.shape[2]
    patch = probe.shape[1]
    rim = patch // 2
    full = tile + patch
    packed = jnp.asarray(tables(patch))
    vmem = pl.BlockSpec(memory_space=pltpu.VMEM)
    smem = pl.BlockSpec(memory_space=pltpu.SMEM)
    hbm = pl.BlockSpec(memory_space=pl.ANY)
    dma = pltpu.SemaphoreType.DMA
    gradient = pl.pallas_call(
        functools.partial(
            kernel, tile, patch, lax.axis_size("row"), lax.axis_size("col")
        ),
        out_shape=pltpu.VMEM(object_field.shape, F32),
        in_specs=[smem, smem, hbm, hbm, hbm, hbm],
        out_specs=vmem,
        scratch_shapes=[
            pltpu.VMEM((2, tile, tile), F32),
            pltpu.VMEM((2, patch, patch), BF16),
            pltpu.VMEM((2, patch, patch), BF16),
            pltpu.VMEM(packed.shape, BF16),
            pltpu.VMEM((2, full, full), jnp.int16),
            pltpu.VMEM((2, 2, 2, patch, patch), jnp.int16),
            pltpu.VMEM((2, 2, patch, patch), BF16),
            pltpu.VMEM((2, 2, patch, patch), BF16),
            pltpu.VMEM((2, tile, tile), F32),
            pltpu.VMEM((2, full, full), BF16),
            pltpu.VMEM((2, 2, tile, rim), BF16),
            pltpu.VMEM((2, 2, rim, tile), BF16),
            pltpu.VMEM((2, 2, 2, rim, rim), BF16),
            pltpu.VMEM((2, 2 * patch, 6 * patch), BF16),
            pltpu.VMEM((2, 6 * patch, 2 * patch), BF16),
            pltpu.VMEM((6 * patch, patch), BF16),
            pltpu.VMEM((patch, 6 * patch), BF16),
            pltpu.VMEM((2, patch, patch + rim), BF16),
            pltpu.VMEM((2, patch + rim, patch), BF16),
            pltpu.VMEM((full, 2 * patch), BF16),
            pltpu.VMEM((2, patch, full), BF16),
            pltpu.VMEM((2, 2 * patch, full), BF16),
            dma((5,)), dma((10,)), dma((10,)), dma((3,)), dma((3,)), dma((10,)), dma((10,)),
        ],
        compiler_params=pltpu.CompilerParams(
            collective_id=0, has_side_effects=True, vmem_limit_bytes=56 * 1024 * 1024
        ),
    )(positions, live, object_field, probe, amplitude, packed)
    return gradient


def solution(mesh):
    in_specs = (
        P("depth", None, "row", "col"),
        P(),
        P("row", "col", None, None, None),
        P("row", "col", None, None),
        P("row", "col", None),
    )
    out_specs = P("depth", None, "row", "col")
    return jax.shard_map(
        on_device, mesh=mesh, in_specs=in_specs, out_specs=out_specs, check_vma=False
    )
```

```python
import functools
import math

import jax
import jax.numpy as jnp
import ml_dtypes
import numpy as np
from jax import lax
from jax.experimental import pallas as pl
from jax.experimental.pallas import tpu as pltpu
from jax.sharding import PartitionSpec as P

MESH = pl.DeviceIdType.MESH
SCALE = 16384.0
F32 = jnp.float32
BF16 = jnp.bfloat16


def split(values):
    high = values.astype(ml_dtypes.bfloat16)
    low = (values - high.astype(np.float64)).astype(ml_dtypes.bfloat16)
    return high, low


def tables(size):
    steps = np.arange(size)
    angles = 2.0 * math.pi * ((steps[:, None] * steps[None, :]) % size) / size
    fourier = np.exp(-1j * angles) / math.sqrt(size)
    frequency = (steps + size // 2) % size - size // 2
    chirp = np.exp(-1j * math.pi * frequency.astype(np.float64) ** 2 / (2.0 * size))
    spread = fourier.conj() @ (chirp[:, None] * fourier)
    packed = []
    for table in (spread, fourier):
        real_high, real_low = split(table.real)
        imag_high, imag_low = split(table.imag)
        packed.append(np.stack((real_high, imag_high, real_low, imag_low)))
    return np.stack(packed)


def dot(left, right):
    return jnp.dot(left, right, preferred_element_type=F32)


def halves(values):
    high = values.astype(BF16)
    return high, (values - high.astype(F32)).astype(BF16)


def kernel(
    tile, patch, n_row, n_col,
    pos, live, obj_hbm, probe_hbm, amp_hbm, tab_hbm, out,
    edge, obj, probe, amp, tab, pad, win, wave, grads, center, gpad, got_x, got_y, got_c,
    left3, right3, stack, wide, pick_rows, pick_cols, put_rows, put_cols, quad_rows, quad_cols, spread,
    in_sem, halo_send, halo_recv, swap_send, swap_recv, rim_send, rim_recv,
):
    rim = patch // 2
    full = tile + patch
    span = patch + rim
    depth, row, col = lax.axis_index("depth"), lax.axis_index("row"), lax.axis_index("col")
    partner = (1 - depth, row, col)

    odd = lax.rem(col, 2)
    away = 2 * odd - 1
    mate = (depth, row, col - away)
    cross = (depth, row, lax.rem(col + away + n_col, n_col))
    along = [(depth, lax.rem(row + step + n_row, n_row), col) for step in (-1, 1)]

    def send(source, target, sems, index, device):
        copy = pltpu.make_async_remote_copy(
            src_ref=source, dst_ref=target, send_sem=sems[0].at[index],
            recv_sem=sems[1].at[index], device_id=device, device_id_type=MESH,
        )
        copy.start()
        return copy

    barrier = pltpu.get_barrier_semaphore()
    for device in (mate, cross, *along, partner):
        pl.semaphore_signal(barrier, inc=1, device_id=device, device_id_type=MESH)
    last = tile // rim
    near_mate, near_cross = pl.ds(rim * (last - (last - 1) * odd), rim), pl.ds(rim * (1 + (last - 1) * odd), rim)
    past_mate, past_cross = pl.ds(rim * ((last + 1) * (1 - odd)), rim), pl.ds(rim * ((last + 1) * odd), rim)
    middle = pl.ds(rim, tile)
    inner_rows = (pl.ds(rim, rim), pl.ds(tile, rim))
    outer_rows = (pl.ds(rim + tile, rim), pl.ds(0, rim))
    halo_sems = (halo_send, halo_recv)
    edge_cross, edge_mate = pl.ds(rim * (last - 1) * odd, rim), pl.ds(rim * (last - 1) * (1 - odd), rim)
    loads = [
        pltpu.make_async_copy(source, target, in_sem.at[index])
        for index, (source, target) in enumerate((
            (obj_hbm.at[0, 0], obj.at[0]), (obj_hbm.at[0, 1], obj.at[1]),
            (tab_hbm, tab), (probe_hbm, probe), (amp_hbm.at[0, 0], amp),
            (obj_hbm.at[0, :, :, edge_cross], edge),
        ))
    ]
    for load in (loads[5], *loads[:5]):
        load.start()

    def fixed_point(values):
        return jnp.round(values * SCALE).astype(jnp.int32).astype(jnp.int16)

    loads[5].wait()
    for part in range(2):
        pad[part, middle, near_cross] = fixed_point(edge[part])
    pl.semaphore_wait(barrier, 5)
    halo = [
        send(pad.at[:, rows, near_cross], pad.at[:, rows, past_mate], halo_sems, index, cross)
        for index, rows in enumerate((*inner_rows, pl.ds(2 * rim, tile - 2 * rim)))
    ]
    for part in range(2):
        loads[part].wait()
        pad[part, middle, 2 * rim:tile] = fixed_point(obj[part, :, rim:tile - rim])
        pad[part, middle, near_mate] = fixed_point(obj[part, :, edge_mate])
    halo += [
        send(pad.at[:, inner_rows[k], middle], pad.at[:, outer_rows[k], middle], halo_sems, 3 + k, along[k])
        for k in range(2)
    ]
    halo.append(send(pad.at[:, middle, near_mate], pad.at[:, middle, past_cross], halo_sems, 5, mate))

    loads[2].wait()
    for which in range(2):
        for place, level in enumerate((0, 2, 0)):
            real, imag = tab[which, level], tab[which, level + 1]
            minus = -imag
            base = place * 2 * patch
            left3[which, 0:patch, base:base + patch] = real
            left3[which, 0:patch, base + patch:base + 2 * patch] = minus
            left3[which, patch:2 * patch, base:base + patch] = imag
            left3[which, patch:2 * patch, base + patch:base + 2 * patch] = real
            right3[which, base:base + patch, 0:patch] = real
            right3[which, base:base + patch, patch:2 * patch] = imag
            right3[which, base + patch:base + 2 * patch, 0:patch] = minus
            right3[which, base + patch:base + 2 * patch, patch:2 * patch] = real

    def transform3(real, imag, which):
        for part, values in enumerate((real, imag)):
            high, low = halves(values)
            at = part * patch
            stack[at:at + patch] = high
            stack[2 * patch + at:3 * patch + at] = high
            stack[4 * patch + at:5 * patch + at] = low
        mid = dot(left3[which], stack[...])
        for part in range(2):
            high, low = halves(mid[part * patch:(part + 1) * patch])
            at = part * patch
            wide[:, at:at + patch] = high
            wide[:, 2 * patch + at:3 * patch + at] = high
            wide[:, 4 * patch + at:5 * patch + at] = low
        end = dot(wide[...], right3[which])
        return end[:, :patch], end[:, patch:]

    def conjugate1(real, imag, which):
        stack[0:patch] = real.astype(BF16)
        stack[patch:2 * patch] = imag.astype(BF16)
        mid = dot(right3[which, 0:2 * patch], stack[0:2 * patch])
        wide[:, 0:patch] = mid[:patch].astype(BF16)
        wide[:, patch:2 * patch] = mid[patch:].astype(BF16)
        end = dot(wide[:, 0:2 * patch], left3[which, :, 0:2 * patch])
        return end[:, :patch], end[:, patch:]

    def one_hot(shape, axis, shift, turn=None):
        index = lax.broadcasted_iota(jnp.int32, shape, 1 - axis)
        if turn is not None:
            index = index + turn
            index = jnp.where(index >= patch, index - patch, index)
        hit = lax.broadcasted_iota(jnp.int32, shape, axis) == index + shift
        return hit.astype(F32).astype(BF16)

    blocks, quads, turned = [], [], []
    for slot in range(2):
        corner = [pos[0, 0, slot, axis] for axis in range(2)]
        turned.append([start < patch for start in corner])
        turns = [jnp.where(flag, rim, 0) for flag in turned[slot]]
        block = [jnp.minimum(start >> 7, (full - span) // 128) for start in corner]
        blocks.append(block)
        pick_rows[slot] = one_hot((patch, span), 1, corner[0] - block[0] * 128, turns[0])
        pick_cols[slot] = one_hot((span, patch), 0, corner[1] - block[1] * 128, turns[1])
        put_rows[:, slot * patch:(slot + 1) * patch] = one_hot((full, patch), 0, corner[0])
        put_cols[slot] = one_hot((patch, full), 1, corner[1])
        first = [start - rim + turn for start, turn in zip(corner, turns)]
        quad = [jnp.minimum(start >> 7, (tile - patch) // 128) for start in first]
        quads.append(quad)
        quad_rows[slot] = one_hot((rim, patch), 1, first[0] - quad[0] * 128)
        quad_cols[slot] = one_hot((patch, rim), 0, first[1] - quad[1] * 128)

    def select(codes, rows, cols):
        width = codes.shape[1]
        high, low = halves(codes)
        picked = dot(rows, jnp.concatenate((high, low), axis=1)).astype(BF16)
        cells = dot(picked[:, :width], cols) + dot(picked[:, width:], cols)
        return cells.astype(jnp.int32).astype(jnp.int16)

    for slot in range(2):
        for part in range(2):
            block = obj[part, pl.ds(quads[slot][0] * 128, patch), pl.ds(quads[slot][1] * 128, patch)]
            win[depth, slot, part, 0:rim, 0:rim] = select(
                jnp.round(block * SCALE), quad_rows[slot], quad_cols[slot]
            )

    def extract(slot, part):
        block = pad[
            part, pl.ds(blocks[slot][0] * 128, span), pl.ds(blocks[slot][1] * 128, span)
        ]
        cells = select(block.astype(F32), pick_rows[slot], pick_cols[slot])
        win[depth, slot, part, 0:rim, rim:] = cells[0:rim, rim:]
        win[depth, slot, part, rim:, :] = cells[rim:, :]

    def swap(buffer, index):
        return pltpu.make_async_remote_copy(
            src_ref=buffer, dst_ref=buffer,
            send_sem=swap_send.at[index], recv_sem=swap_recv.at[index],
            device_id=partner, device_id_type=MESH,
        )

    def patch_of(section, slot):
        parts = []
        for part in range(2):
            codes = win[section, slot, part].astype(F32) * (1.0 / SCALE)
            for axis in range(2):
                front, back = (codes[0:rim], codes[rim:]) if axis == 0 else (codes[:, 0:rim], codes[:, rim:])
                flag = turned[slot][axis]
                codes = jnp.concatenate(
                    (jnp.where(flag, back, front), jnp.where(flag, front, back)), axis=axis
                )
            parts.append(codes)
        return parts

    def quadrant(slot, section):
        return swap(win.at[section, slot, :, 0:rim, 0:rim], slot)

    def remainder(slot, section, part=None):
        parts = pl.ds(0, 2) if part is None else pl.ds(part, 1)
        base = 2 if part is None else 4 + 2 * part
        return (
            swap(win.at[section, slot, parts, 0:rim, rim:patch], base),
            swap(win.at[section, slot, parts, rim:patch], base + 1),
        )

    loads[3].wait()
    loads[4].wait()
    probe_real, probe_imag = probe[0].astype(F32), probe[1].astype(F32)
    for k in range(2):
        halo[k].wait_recv()
        halo.append(
            send(
                pad.at[:, inner_rows[k], past_cross], pad.at[:, outer_rows[k], past_cross],
                halo_sems, 6 + k, along[k],
            )
        )
    quadrant(0, depth).start()

    @pl.when(depth == 1)
    def _():
        quadrant(1, 1).start()

    for k in range(2):
        halo[3 + k].wait_recv()
        halo.append(
            send(
                pad.at[:, outer_rows[k], near_mate], pad.at[:, outer_rows[k], past_cross],
                halo_sems, 8 + k, mate,
            )
        )
    for copy in (halo[2], *halo[5:]):
        copy.wait_recv()

    def propagate(slot):
        obj_real, obj_imag = patch_of(0, slot)
        wave_real, wave_imag = transform3(
            probe_real * obj_real - probe_imag * obj_imag,
            probe_real * obj_imag + probe_imag * obj_real,
            0,
        )
        wave[slot, 0] = wave_real.astype(BF16)
        wave[slot, 1] = wave_imag.astype(BF16)

    for part in range(2):
        extract(0, part)
        for copy in remainder(0, depth, part):
            copy.start()
    for part in range(2):
        extract(1, part)

    @pl.when(depth == 0)
    def _():
        propagate(1)
        swap(wave.at[1], 8).start()

    @pl.when(depth == 1)
    def _():
        for copy in remainder(1, 1):
            copy.start()
        quadrant(0, 0).wait_recv()
        for part in range(2):
            for copy in remainder(0, 0, part):
                copy.wait_recv()

    propagate(0)

    @pl.when(depth == 0)
    def _():
        quadrant(0, 1).wait_recv()
        for part in range(2):
            for copy in remainder(0, 1, part):
                copy.wait_recv()

    for slot in range(2):
        if slot == 1:
            @pl.when(depth == 0)
            def _():
                for copy in (quadrant(1, 1), *remainder(1, 1)):
                    copy.wait_recv()

            @pl.when(depth == 1)
            def _():
                swap(wave.at[1], 8).wait_recv()

        wave_real, wave_imag = wave[slot, 0].astype(F32), wave[slot, 1].astype(F32)
        obj_real, obj_imag = patch_of(1, slot)
        far_real, far_imag = transform3(
            wave_real * obj_real - wave_imag * obj_imag,
            wave_real * obj_imag + wave_imag * obj_real,
            1,
        )
        power = far_real * far_real + far_imag * far_imag
        weight = live[0, 0, slot].astype(F32)
        factor = weight * (
            1.0 - amp[slot].astype(F32) * lax.rsqrt(jnp.maximum(power, 0.0625))
        )
        back_real, back_imag = conjugate1(far_real * factor, far_imag * factor, 1)
        back_real = back_real.astype(BF16).astype(F32)
        back_imag = back_imag.astype(BF16).astype(F32)

        @pl.when(depth == 1)
        def _():
            grads[slot, 0] = (wave_real * back_real + wave_imag * back_imag).astype(BF16)
            grads[slot, 1] = (wave_real * back_imag - wave_imag * back_real).astype(BF16)

        @pl.when(depth == 0)
        def _():
            first_real, first_imag = conjugate1(
                obj_real * back_real + obj_imag * back_imag,
                obj_real * back_imag - obj_imag * back_real,
                0,
            )
            first_real = first_real.astype(BF16).astype(F32)
            first_imag = first_imag.astype(BF16).astype(F32)
            grads[slot, 0] = (probe_real * first_real + probe_imag * first_imag).astype(BF16)
            grads[slot, 1] = (probe_real * first_imag - probe_imag * first_real).astype(BF16)

        for part in range(2):
            spread[part, slot * patch:(slot + 1) * patch] = dot(
                grads[slot, part], put_cols[slot]
            ).astype(BF16)

    for part in range(2):
        sides = jnp.concatenate((spread[part, :, 0:rim], spread[part, :, rim + tile:]), axis=1)
        sides = dot(put_rows[...], sides).astype(BF16)
        gpad[part, :, 0:rim] = sides[:, 0:rim]
        gpad[part, :, rim + tile:] = sides[:, rim:]

    rim_sems = (rim_send, rim_recv)
    edge_rows = (pl.ds(0, rim), pl.ds(rim + tile, rim))
    rims = [
        send(gpad.at[:, edge_rows[k], past_cross], got_c.at[0, k], rim_sems, k, along[k])
        for k in range(2)
    ]
    rims += [
        send(gpad.at[:, edge_rows[k], past_mate], got_c.at[1, k], rim_sems, 2 + k, mate)
        for k in range(2)
    ]
    rims.append(
        send(
            gpad.at[:, pl.ds(2 * rim, tile - 2 * rim), past_cross],
            got_x.at[odd, :, pl.ds(rim, tile - 2 * rim)], rim_sems, 4, cross,
        )
    )
    rims.append(send(gpad.at[:, middle, past_mate], got_x.at[1 - odd], rim_sems, 5, mate))
    for part in range(2):
        ends = jnp.concatenate((put_rows[0:rim], put_rows[rim + tile:]), axis=0)
        ends = dot(ends, spread[part, :, rim:rim + tile]).astype(BF16)
        gpad[part, 0:rim, rim:rim + tile] = ends[0:rim]
        gpad[part, rim + tile:, rim:rim + tile] = ends[rim:]
    for k in range(2):
        rims[2 + k].wait_recv()
        for part in range(2):
            total = gpad[part, edge_rows[k], near_mate].astype(F32) + got_c[1, k, part].astype(F32)
            gpad[part, edge_rows[k], near_mate] = total.astype(BF16)
        rims.append(
            send(gpad.at[:, edge_rows[k], middle], got_y.at[k], rim_sems, 6 + k, along[k])
        )

    for part in range(2):
        center[part] = dot(put_rows[rim:rim + tile], spread[part, :, rim:rim + tile])

    for k in range(2):
        rims[k].wait_recv()
        rows = inner_rows[1 - k]
        for part in range(2):
            total = gpad[part, rows, past_cross].astype(F32) + got_c[0, k, part].astype(F32)
            gpad[part, rows, past_cross] = total.astype(BF16)
        rims.append(
            send(
                gpad.at[:, rows, past_cross], got_x.at[odd, :, pl.ds((1 - k) * (tile - rim), rim)],
                rim_sems, 8 + k, cross,
            )
        )
    for copy in rims[4:8]:
        copy.wait_recv()
    starts = {1: (0, rim), 0: (rim, tile - 2 * rim), -1: (tile - rim, rim)}
    for down in (0, -1, 1):
        if down:
            rims[8 + (1 + down) // 2].wait_recv()
        for right in (-1, 0, 1):
            (top, height), (left, width) = starts[down], starts[right]
            rows, cols = pl.ds(top, height), pl.ds(left, width)
            for part in range(2):
                total = center[part, rows, cols]
                if right:
                    total = total + got_x[(1 + right) // 2, part, rows, :].astype(F32)
                if down:
                    total = total + got_y[(1 + down) // 2, part, :, cols].astype(F32)
                out[0, part, rows, cols] = total

    for copy in halo:
        copy.wait_send()
    quadrant(0, depth).wait_send()
    for part in range(2):
        for copy in remainder(0, depth, part):
            copy.wait_send()

    @pl.when(depth == 0)
    def _():
        swap(wave.at[1], 8).wait_send()

    @pl.when(depth == 1)
    def _():
        for copy in (quadrant(1, 1), *remainder(1, 1)):
            copy.wait_send()

    for copy in rims:
        copy.wait_send()


def on_device(object_field, probe, amplitude, positions, live):
    tile = object_field.shape[2]
    patch = probe.shape[1]
    rim = patch // 2
    full = tile + patch
    packed = jnp.asarray(tables(patch))
    vmem = pl.BlockSpec(memory_space=pltpu.VMEM)
    smem = pl.BlockSpec(memory_space=pltpu.SMEM)
    hbm = pl.BlockSpec(memory_space=pl.ANY)
    dma = pltpu.SemaphoreType.DMA
    gradient = pl.pallas_call(
        functools.partial(
            kernel, tile, patch, lax.axis_size("row"), lax.axis_size("col")
        ),
        out_shape=pltpu.VMEM(object_field.shape, F32),
        in_specs=[smem, smem, hbm, hbm, hbm, hbm],
        out_specs=vmem,
        scratch_shapes=[
            pltpu.VMEM((2, tile, rim), F32),
            pltpu.VMEM((2, tile, tile), F32),
            pltpu.VMEM((2, patch, patch), BF16),
            pltpu.VMEM((2, patch, patch), BF16),
            pltpu.VMEM(packed.shape, BF16),
            pltpu.VMEM((2, full, full), jnp.int16),
            pltpu.VMEM((2, 2, 2, patch, patch), jnp.int16),
            pltpu.VMEM((2, 2, patch, patch), BF16),
            pltpu.VMEM((2, 2, patch, patch), BF16),
            pltpu.VMEM((2, tile, tile), F32),
            pltpu.VMEM((2, full, full), BF16),
            pltpu.VMEM((2, 2, tile, rim), BF16),
            pltpu.VMEM((2, 2, rim, tile), BF16),
            pltpu.VMEM((2, 2, 2, rim, rim), BF16),
            pltpu.VMEM((2, 2 * patch, 6 * patch), BF16),
            pltpu.VMEM((2, 6 * patch, 2 * patch), BF16),
            pltpu.VMEM((6 * patch, patch), BF16),
            pltpu.VMEM((patch, 6 * patch), BF16),
            pltpu.VMEM((2, patch, patch + rim), BF16),
            pltpu.VMEM((2, patch + rim, patch), BF16),
            pltpu.VMEM((full, 2 * patch), BF16),
            pltpu.VMEM((2, patch, full), BF16),
            pltpu.VMEM((2, rim, patch), BF16),
            pltpu.VMEM((2, patch, rim), BF16),
            pltpu.VMEM((2, 2 * patch, full), BF16),
            dma((6,)), dma((10,)), dma((10,)), dma((9,)), dma((9,)), dma((10,)), dma((10,)),
        ],
        compiler_params=pltpu.CompilerParams(
            collective_id=0, has_side_effects=True, vmem_limit_bytes=56 * 1024 * 1024
        ),
    )(positions, live, object_field, probe, amplitude, packed)
    return gradient


def solution(mesh):
    in_specs = (
        P("depth", None, "row", "col"),
        P(),
        P("row", "col", None, None, None),
        P("row", "col", None, None),
        P("row", "col", None),
    )
    out_specs = P("depth", None, "row", "col")
    return jax.shard_map(
        on_device, mesh=mesh, in_specs=in_specs, out_specs=out_specs, check_vma=False
    )
```

```python
import functools
import math

import jax
import jax.numpy as jnp
import ml_dtypes
import numpy as np
from jax import lax
from jax.experimental import pallas as pl
from jax.experimental.pallas import tpu as pltpu
from jax.sharding import PartitionSpec as P

MESH = pl.DeviceIdType.MESH
SCALE = 16384.0
F32 = jnp.float32
BF16 = jnp.bfloat16


def split(values):
    high = values.astype(ml_dtypes.bfloat16)
    low = (values - high.astype(np.float64)).astype(ml_dtypes.bfloat16)
    return high, low


def tables(size):
    steps = np.arange(size)
    angles = 2.0 * math.pi * ((steps[:, None] * steps[None, :]) % size) / size
    fourier = np.exp(-1j * angles) / math.sqrt(size)
    frequency = (steps + size // 2) % size - size // 2
    chirp = np.exp(-1j * math.pi * frequency.astype(np.float64) ** 2 / (2.0 * size))
    spread = fourier.conj() @ (chirp[:, None] * fourier)
    half = size // 2
    same, swapped = spread[:half, :half], spread[:half, half:]
    left, right = [], []
    for table in (fourier[0::2, :half], fourier[1::2, :half], (same + swapped) / 2, (same - swapped) / 2):
        whole = np.block([[table.real, -table.imag], [table.imag, table.real]])
        high, low = split(whole)
        left.append(np.concatenate((high, low, high), axis=1))
        right.append(np.concatenate((high.T, low.T, high.T), axis=0))
    return np.stack(left), np.stack(right)


def dot(left, right):
    return jnp.dot(left, right, preferred_element_type=F32)


def halves(values):
    high = values.astype(BF16)
    return high, (values - high.astype(F32)).astype(BF16)


def kernel(
    tile, patch, n_row, n_col,
    pos, live, obj_hbm, probe_hbm, amp_hbm, left_hbm, right_hbm, out,
    edge, obj, probe, amp, turned_amp, pad, win, wave, grads, center, gpad, got_x, got_y, got_c,
    left3, right3, pick_rows, pick_cols, put_rows, put_cols, quad_rows, quad_cols, spread,
    in_sem, halo_send, halo_recv, swap_send, swap_recv, rim_send, rim_recv,
):
    rim = patch // 2
    full = tile + patch
    span = patch + rim
    depth, row, col = lax.axis_index("depth"), lax.axis_index("row"), lax.axis_index("col")
    partner = (1 - depth, row, col)

    odd = lax.rem(col, 2)
    away = 2 * odd - 1
    mate = (depth, row, col - away)
    cross = (depth, row, lax.rem(col + away + n_col, n_col))
    along = [(depth, lax.rem(row + step + n_row, n_row), col) for step in (-1, 1)]

    def send(source, target, sems, index, device):
        copy = pltpu.make_async_remote_copy(
            src_ref=source, dst_ref=target, send_sem=sems[0].at[index],
            recv_sem=sems[1].at[index], device_id=device, device_id_type=MESH,
        )
        copy.start()
        return copy

    barrier = pltpu.get_barrier_semaphore()
    for device in (mate, cross, *along, partner):
        pl.semaphore_signal(barrier, inc=1, device_id=device, device_id_type=MESH)
    last = tile // rim
    near_mate, near_cross = pl.ds(rim * (last - (last - 1) * odd), rim), pl.ds(rim * (1 + (last - 1) * odd), rim)
    past_mate, past_cross = pl.ds(rim * ((last + 1) * (1 - odd)), rim), pl.ds(rim * ((last + 1) * odd), rim)
    middle = pl.ds(rim, tile)
    inner_rows = (pl.ds(rim, rim), pl.ds(tile, rim))
    outer_rows = (pl.ds(rim + tile, rim), pl.ds(0, rim))
    halo_sems = (halo_send, halo_recv)
    edge_cross, edge_mate = pl.ds(rim * (last - 1) * odd, rim), pl.ds(rim * (last - 1) * (1 - odd), rim)
    loads = [
        pltpu.make_async_copy(source, target, in_sem.at[index])
        for index, (source, target) in enumerate((
            (obj_hbm.at[0, 0], obj.at[0]), (obj_hbm.at[0, 1], obj.at[1]),
            (left_hbm, left3), (probe_hbm, probe), (amp_hbm.at[0, 0], amp),
            (obj_hbm.at[0, :, :, edge_cross], edge), (right_hbm, right3),
        ))
    ]
    for load in (loads[5], *loads[:5], loads[6]):
        load.start()

    def fixed_point(values):
        return jnp.round(values * SCALE).astype(jnp.int32).astype(jnp.int16)

    loads[5].wait()
    for part in range(2):
        pad[part, middle, near_cross] = fixed_point(edge[part])
    pl.semaphore_wait(barrier, 5)
    halo = [
        send(pad.at[:, rows, near_cross], pad.at[:, rows, past_mate], halo_sems, index, cross)
        for index, rows in enumerate((*inner_rows, pl.ds(2 * rim, tile - 2 * rim)))
    ]
    for part in range(2):
        loads[part].wait()
        pad[part, middle, 2 * rim:tile] = fixed_point(obj[part, :, rim:tile - rim])
        pad[part, middle, near_mate] = fixed_point(obj[part, :, edge_mate])
    halo += [
        send(pad.at[:, inner_rows[k], middle], pad.at[:, outer_rows[k], middle], halo_sems, 3 + k, along[k])
        for k in range(2)
    ]
    halo.append(send(pad.at[:, middle, near_mate], pad.at[:, middle, past_cross], halo_sems, 5, mate))

    def halved(values, axis):
        if axis == 0:
            return values[0:rim], values[rim:]
        return values[:, 0:rim], values[:, rim:]

    def stacked(real, imag, axis, mix):
        (real0, real1), (imag0, imag1) = halved(real, axis), halved(imag, axis)
        if mix:
            real0, real1 = real0 + real1, real0 - real1
            imag0, imag1 = imag0 + imag1, imag0 - imag1
        return [jnp.concatenate(pair, axis=axis) for pair in ((real0, imag0), (real1, imag1))]

    def unstacked(first, second, axis, mix):
        (real0, imag0), (real1, imag1) = halved(first, axis), halved(second, axis)
        if mix:
            real0, real1 = real0 + real1, real0 - real1
            imag0, imag1 = imag0 + imag1, imag0 - imag1
        return [jnp.concatenate(pair, axis=axis) for pair in ((real0, real1), (imag0, imag1))]

    def transform3(real, imag, base, mix_after):
        for axis in range(2):
            sides = []
            for place, values in enumerate(stacked(real, imag, axis, True)):
                high, low = halves(values)
                values = jnp.concatenate((high, high, low), axis=axis)
                if axis == 0:
                    sides.append(dot(left3[base + place], values))
                else:
                    sides.append(dot(values, right3[base + place]))
            real, imag = unstacked(*sides, axis, mix_after)
        return real, imag

    def conjugate1(real, imag, base, mix_before):
        for axis in range(2):
            sides = []
            for place, values in enumerate(stacked(real, imag, axis, mix_before)):
                values = values.astype(BF16)
                if axis == 0:
                    sides.append(dot(right3[base + place, 0:patch], values))
                else:
                    sides.append(dot(values, left3[base + place, :, 0:patch]))
            real, imag = unstacked(*sides, axis, True)
        return real, imag

    def one_hot(shape, axis, shift, turn=None):
        index = lax.broadcasted_iota(jnp.int32, shape, 1 - axis)
        if turn is not None:
            index = index + turn
            index = jnp.where(index >= patch, index - patch, index)
        hit = lax.broadcasted_iota(jnp.int32, shape, axis) == index + shift
        return hit.astype(F32).astype(BF16)

    blocks, quads, turned = [], [], []
    for slot in range(2):
        corner = [pos[0, 0, slot, axis] for axis in range(2)]
        turned.append([start < patch for start in corner])
        turns = [jnp.where(flag, rim, 0) for flag in turned[slot]]
        block = [jnp.minimum(start >> 7, (full - span) // 128) for start in corner]
        blocks.append(block)
        pick_rows[slot] = one_hot((patch, span), 1, corner[0] - block[0] * 128, turns[0])
        pick_cols[slot] = one_hot((span, patch), 0, corner[1] - block[1] * 128, turns[1])
        put_rows[:, slot * patch:(slot + 1) * patch] = one_hot((full, patch), 0, corner[0])
        put_cols[slot] = one_hot((patch, full), 1, corner[1])
        first = [start - rim + turn for start, turn in zip(corner, turns)]
        quad = [jnp.minimum(start >> 7, (tile - patch) // 128) for start in first]
        quads.append(quad)
        quad_rows[slot] = one_hot((rim, patch), 1, first[0] - quad[0] * 128)
        quad_cols[slot] = one_hot((patch, rim), 0, first[1] - quad[1] * 128)

    def select(codes, rows, cols):
        width = codes.shape[1]
        high, low = halves(codes)
        picked = dot(rows, jnp.concatenate((high, low), axis=1)).astype(BF16)
        cells = dot(picked[:, :width], cols) + dot(picked[:, width:], cols)
        return cells.astype(jnp.int32).astype(jnp.int16)

    for slot in range(2):
        for part in range(2):
            block = obj[part, pl.ds(quads[slot][0] * 128, patch), pl.ds(quads[slot][1] * 128, patch)]
            win[depth, slot, part, 0:rim, 0:rim] = select(
                jnp.round(block * SCALE), quad_rows[slot], quad_cols[slot]
            )

    def extract(slot, part):
        block = pad[
            part, pl.ds(blocks[slot][0] * 128, span), pl.ds(blocks[slot][1] * 128, span)
        ]
        cells = select(block.astype(F32), pick_rows[slot], pick_cols[slot])
        win[depth, slot, part, 0:rim, rim:] = cells[0:rim, rim:]
        win[depth, slot, part, rim:, :] = cells[rim:, :]

    def swap(buffer, index):
        return pltpu.make_async_remote_copy(
            src_ref=buffer, dst_ref=buffer,
            send_sem=swap_send.at[index], recv_sem=swap_recv.at[index],
            device_id=partner, device_id_type=MESH,
        )

    def patch_of(section, slot):
        parts = []
        for part in range(2):
            codes = win[section, slot, part].astype(F32) * (1.0 / SCALE)
            for axis in range(2):
                front, back = (codes[0:rim], codes[rim:]) if axis == 0 else (codes[:, 0:rim], codes[:, rim:])
                flag = turned[slot][axis]
                codes = jnp.concatenate(
                    (jnp.where(flag, back, front), jnp.where(flag, front, back)), axis=axis
                )
            parts.append(codes)
        return parts

    def quadrant(slot, section):
        return swap(win.at[section, slot, :, 0:rim, 0:rim], slot)

    def remainder(slot, section, part=None):
        parts = pl.ds(0, 2) if part is None else pl.ds(part, 1)
        base = 2 if part is None else 4 + 2 * part
        return (
            swap(win.at[section, slot, parts, 0:rim, rim:patch], base),
            swap(win.at[section, slot, parts, rim:patch], base + 1),
        )

    loads[2].wait()
    loads[3].wait()
    loads[4].wait()
    loads[6].wait()
    place = lax.broadcasted_iota(jnp.int32, (patch, patch), 0)
    order = (
        lax.broadcasted_iota(jnp.int32, (patch, patch), 1)
        == 2 * place - jnp.where(place >= rim, patch - 1, 0)
    ).astype(F32).astype(BF16)
    for slot in range(2):
        rows = dot(order, amp[slot]).astype(BF16)
        turned_amp[slot] = lax.dot_general(
            rows, order, (((1,), (1,)), ((), ())), preferred_element_type=F32
        ).astype(BF16)
    probe_real, probe_imag = probe[0].astype(F32), probe[1].astype(F32)
    for k in range(2):
        halo[k].wait_recv()
        halo.append(
            send(
                pad.at[:, inner_rows[k], past_cross], pad.at[:, outer_rows[k], past_cross],
                halo_sems, 6 + k, along[k],
            )
        )
    quadrant(0, depth).start()

    @pl.when(depth == 1)
    def _():
        quadrant(1, 1).start()

    for k in range(2):
        halo[3 + k].wait_recv()
        halo.append(
            send(
                pad.at[:, outer_rows[k], near_mate], pad.at[:, outer_rows[k], past_cross],
                halo_sems, 8 + k, mate,
            )
        )
    for copy in (halo[2], *halo[5:]):
        copy.wait_recv()

    def propagate(slot):
        obj_real, obj_imag = patch_of(0, slot)
        wave_real, wave_imag = transform3(
            probe_real * obj_real - probe_imag * obj_imag,
            probe_real * obj_imag + probe_imag * obj_real,
            2, True,
        )
        wave[slot, 0] = wave_real.astype(BF16)
        wave[slot, 1] = wave_imag.astype(BF16)

    for part in range(2):
        extract(0, part)
        for copy in remainder(0, depth, part):
            copy.start()
    for part in range(2):
        extract(1, part)

    @pl.when(depth == 0)
    def _():
        propagate(1)
        swap(wave.at[1], 8).start()

    @pl.when(depth == 1)
    def _():
        for copy in remainder(1, 1):
            copy.start()
        quadrant(0, 0).wait_recv()
        for part in range(2):
            for copy in remainder(0, 0, part):
                copy.wait_recv()

    propagate(0)

    @pl.when(depth == 0)
    def _():
        quadrant(0, 1).wait_recv()
        for part in range(2):
            for copy in remainder(0, 1, part):
                copy.wait_recv()

    for slot in range(2):
        if slot == 1:
            @pl.when(depth == 0)
            def _():
                for copy in (quadrant(1, 1), *remainder(1, 1)):
                    copy.wait_recv()

            @pl.when(depth == 1)
            def _():
                swap(wave.at[1], 8).wait_recv()

        wave_real, wave_imag = wave[slot, 0].astype(F32), wave[slot, 1].astype(F32)
        obj_real, obj_imag = patch_of(1, slot)
        far_real, far_imag = transform3(
            wave_real * obj_real - wave_imag * obj_imag,
            wave_real * obj_imag + wave_imag * obj_real,
            0, False,
        )
        power = far_real * far_real + far_imag * far_imag
        weight = live[0, 0, slot].astype(F32)
        factor = weight * (
            1.0 - turned_amp[slot].astype(F32) * lax.rsqrt(jnp.maximum(power, 0.0625))
        )
        back_real, back_imag = conjugate1(far_real * factor, far_imag * factor, 0, False)
        back_real = back_real.astype(BF16).astype(F32)
        back_imag = back_imag.astype(BF16).astype(F32)

        @pl.when(depth == 1)
        def _():
            grads[slot, 0] = (wave_real * back_real + wave_imag * back_imag).astype(BF16)
            grads[slot, 1] = (wave_real * back_imag - wave_imag * back_real).astype(BF16)

        @pl.when(depth == 0)
        def _():
            first_real, first_imag = conjugate1(
                obj_real * back_real + obj_imag * back_imag,
                obj_real * back_imag - obj_imag * back_real,
                2, True,
            )
            first_real = first_real.astype(BF16).astype(F32)
            first_imag = first_imag.astype(BF16).astype(F32)
            grads[slot, 0] = (probe_real * first_real + probe_imag * first_imag).astype(BF16)
            grads[slot, 1] = (probe_real * first_imag - probe_imag * first_real).astype(BF16)

        if slot == 0:
            for part in range(2):
                spread[part, 0:patch] = dot(grads[slot, part], put_cols[slot]).astype(BF16)

    def outside(values):
        return jnp.concatenate((values[:, 0:rim], values[:, rim + tile:]), axis=1)

    outer_cols = outside(put_cols[1])
    outer_ends = jnp.concatenate((put_rows[0:rim], put_rows[rim + tile:]), axis=0)
    for part in range(2):
        cells = dot(grads[1, part], outer_cols).astype(BF16)
        spread[part, patch:, 0:rim] = cells[:, 0:rim]
        spread[part, patch:, rim + tile:] = cells[:, rim:]
    for part in range(2):
        cells = dot(outer_ends, spread[part, :, past_cross]).astype(BF16)
        gpad[part, 0:rim, past_cross] = cells[0:rim]
        gpad[part, rim + tile:, past_cross] = cells[rim:]

    rim_sems = (rim_send, rim_recv)
    edge_rows = (pl.ds(0, rim), pl.ds(rim + tile, rim))
    rims = [
        send(gpad.at[:, edge_rows[k], past_cross], got_c.at[0, k], rim_sems, k, along[k])
        for k in range(2)
    ]
    for part in range(2):
        sides = jnp.concatenate((spread[part, :, past_cross], spread[part, :, past_mate]), axis=1)
        sides = dot(put_rows[...], sides).astype(BF16)
        gpad[part, middle, past_cross] = sides[rim:rim + tile, 0:rim]
        gpad[part, :, past_mate] = sides[:, rim:]
    rims += [
        send(gpad.at[:, edge_rows[k], past_mate], got_c.at[1, k], rim_sems, 2 + k, mate)
        for k in range(2)
    ]
    rims.append(
        send(
            gpad.at[:, pl.ds(2 * rim, tile - 2 * rim), past_cross],
            got_x.at[odd, :, pl.ds(rim, tile - 2 * rim)], rim_sems, 4, cross,
        )
    )
    rims.append(send(gpad.at[:, middle, past_mate], got_x.at[1 - odd], rim_sems, 5, mate))
    for part in range(2):
        spread[part, patch:, middle] = dot(grads[1, part], put_cols[1, :, middle]).astype(BF16)
        ends = dot(outer_ends, spread[part, :, rim:rim + tile]).astype(BF16)
        gpad[part, 0:rim, rim:rim + tile] = ends[0:rim]
        gpad[part, rim + tile:, rim:rim + tile] = ends[rim:]
    for k in range(2):
        rims[2 + k].wait_recv()
        for part in range(2):
            total = gpad[part, edge_rows[k], near_mate].astype(F32) + got_c[1, k, part].astype(F32)
            gpad[part, edge_rows[k], near_mate] = total.astype(BF16)
        rims.append(
            send(gpad.at[:, edge_rows[k], middle], got_y.at[k], rim_sems, 6 + k, along[k])
        )

    for part in range(2):
        center[part] = dot(put_rows[rim:rim + tile], spread[part, :, rim:rim + tile])

    for k in range(2):
        rims[k].wait_recv()
        rows = inner_rows[1 - k]
        for part in range(2):
            total = gpad[part, rows, past_cross].astype(F32) + got_c[0, k, part].astype(F32)
            gpad[part, rows, past_cross] = total.astype(BF16)
        rims.append(
            send(
                gpad.at[:, rows, past_cross], got_x.at[odd, :, pl.ds((1 - k) * (tile - rim), rim)],
                rim_sems, 8 + k, cross,
            )
        )
    for copy in rims[4:8]:
        copy.wait_recv()
    starts = {1: (0, rim), 0: (rim, tile - 2 * rim), -1: (tile - rim, rim)}
    for down in (0, -1, 1):
        if down:
            rims[8 + (1 + down) // 2].wait_recv()
        for right in (-1, 0, 1):
            (top, height), (left, width) = starts[down], starts[right]
            rows, cols = pl.ds(top, height), pl.ds(left, width)
            for part in range(2):
                total = center[part, rows, cols]
                if right:
                    total = total + got_x[(1 + right) // 2, part, rows, :].astype(F32)
                if down:
                    total = total + got_y[(1 + down) // 2, part, :, cols].astype(F32)
                out[0, part, rows, cols] = total

    for copy in halo:
        copy.wait_send()
    quadrant(0, depth).wait_send()
    for part in range(2):
        for copy in remainder(0, depth, part):
            copy.wait_send()

    @pl.when(depth == 0)
    def _():
        swap(wave.at[1], 8).wait_send()

    @pl.when(depth == 1)
    def _():
        for copy in (quadrant(1, 1), *remainder(1, 1)):
            copy.wait_send()

    for copy in rims:
        copy.wait_send()


def on_device(object_field, probe, amplitude, positions, live):
    tile = object_field.shape[2]
    patch = probe.shape[1]
    rim = patch // 2
    full = tile + patch
    left, right = tables(patch)
    vmem = pl.BlockSpec(memory_space=pltpu.VMEM)
    smem = pl.BlockSpec(memory_space=pltpu.SMEM)
    hbm = pl.BlockSpec(memory_space=pl.ANY)
    dma = pltpu.SemaphoreType.DMA
    gradient = pl.pallas_call(
        functools.partial(
            kernel, tile, patch, lax.axis_size("row"), lax.axis_size("col")
        ),
        out_shape=pltpu.VMEM(object_field.shape, F32),
        in_specs=[smem, smem, hbm, hbm, hbm, hbm, hbm],
        out_specs=vmem,
        scratch_shapes=[
            pltpu.VMEM((2, tile, rim), F32),
            pltpu.VMEM((2, tile, tile), F32),
            pltpu.VMEM((2, patch, patch), BF16),
            pltpu.VMEM((2, patch, patch), BF16),
            pltpu.VMEM((2, patch, patch), BF16),
            pltpu.VMEM((2, full, full), jnp.int16),
            pltpu.VMEM((2, 2, 2, patch, patch), jnp.int16),
            pltpu.VMEM((2, 2, patch, patch), BF16),
            pltpu.VMEM((2, 2, patch, patch), BF16),
            pltpu.VMEM((2, tile, tile), F32),
            pltpu.VMEM((2, full, full), BF16),
            pltpu.VMEM((2, 2, tile, rim), BF16),
            pltpu.VMEM((2, 2, rim, tile), BF16),
            pltpu.VMEM((2, 2, 2, rim, rim), BF16),
            pltpu.VMEM(left.shape, BF16),
            pltpu.VMEM(right.shape, BF16),
            pltpu.VMEM((2, patch, patch + rim), BF16),
            pltpu.VMEM((2, patch + rim, patch), BF16),
            pltpu.VMEM((full, 2 * patch), BF16),
            pltpu.VMEM((2, patch, full), BF16),
            pltpu.VMEM((2, rim, patch), BF16),
            pltpu.VMEM((2, patch, rim), BF16),
            pltpu.VMEM((2, 2 * patch, full), BF16),
            dma((7,)), dma((10,)), dma((10,)), dma((9,)), dma((9,)), dma((10,)), dma((10,)),
        ],
        compiler_params=pltpu.CompilerParams(
            collective_id=0, has_side_effects=True, vmem_limit_bytes=56 * 1024 * 1024
        ),
    )(positions, live, object_field, probe, amplitude, jnp.asarray(left), jnp.asarray(right))
    return gradient


def solution(mesh):
    in_specs = (
        P("depth", None, "row", "col"),
        P(),
        P("row", "col", None, None, None),
        P("row", "col", None, None),
        P("row", "col", None),
    )
    out_specs = P("depth", None, "row", "col")
    return jax.shard_map(
        on_device, mesh=mesh, in_specs=in_specs, out_specs=out_specs, check_vma=False
    )
```

```python
import functools
import math

import jax
import jax.numpy as jnp
import ml_dtypes
import numpy as np
from jax import lax
from jax.experimental import pallas as pl
from jax.experimental.pallas import tpu as pltpu
from jax.sharding import PartitionSpec as P

MESH = pl.DeviceIdType.MESH
SCALE = 16384.0
F32 = jnp.float32
BF16 = jnp.bfloat16


def split(values):
    high = values.astype(ml_dtypes.bfloat16)
    low = (values - high.astype(np.float64)).astype(ml_dtypes.bfloat16)
    return high, low


def tables(size):
    steps = np.arange(size)
    angles = 2.0 * math.pi * ((steps[:, None] * steps[None, :]) % size) / size
    fourier = np.exp(-1j * angles) / math.sqrt(size)
    frequency = (steps + size // 2) % size - size // 2
    chirp = np.exp(-1j * math.pi * frequency.astype(np.float64) ** 2 / (2.0 * size))
    spread = fourier.conj() @ (chirp[:, None] * fourier)
    half = size // 2
    same, swapped = spread[:half, :half], spread[:half, half:]
    left, right = [], []
    for table in (fourier[0::2, :half], fourier[1::2, :half], (same + swapped) / 2, (same - swapped) / 2):
        whole = np.block([[table.real, -table.imag], [table.imag, table.real]])
        high, low = split(whole)
        left.append(np.concatenate((high, low, high), axis=1))
        right.append(np.concatenate((high.T, low.T, high.T), axis=0))
    return np.stack(left), np.stack(right)


def dot(left, right):
    return jnp.dot(left, right, preferred_element_type=F32)


def halves(values):
    high = values.astype(BF16)
    return high, (values - high.astype(F32)).astype(BF16)


def kernel(
    tile, patch, n_row, n_col,
    pos, live, obj_hbm, probe_hbm, amp_hbm, left_hbm, right_hbm, out,
    edge, obj, probe, amp, turned_amp, pad, ring, win, wave, grads, center, gpad, got_x, got_y, got_c,
    left3, right3, pick_rows, pick_cols, put_rows, put_cols, quad_rows, quad_cols, spread,
    in_sem, halo_send, halo_recv, swap_send, swap_recv, rim_send, rim_recv,
):
    rim = patch // 2
    full = tile + patch
    span = patch + rim
    depth, row, col = lax.axis_index("depth"), lax.axis_index("row"), lax.axis_index("col")
    partner = (1 - depth, row, col)

    odd = lax.rem(col, 2)
    away = 2 * odd - 1
    mate = (depth, row, col - away)
    cross = (depth, row, lax.rem(col + away + n_col, n_col))
    along = [(depth, lax.rem(row + step + n_row, n_row), col) for step in (-1, 1)]

    def send(source, target, sems, index, device):
        copy = pltpu.make_async_remote_copy(
            src_ref=source, dst_ref=target, send_sem=sems[0].at[index],
            recv_sem=sems[1].at[index], device_id=device, device_id_type=MESH,
        )
        copy.start()
        return copy

    barrier = pltpu.get_barrier_semaphore()
    for device in (mate, cross, *along, partner):
        pl.semaphore_signal(barrier, inc=1, device_id=device, device_id_type=MESH)
    last = tile // rim
    near_mate, near_cross = pl.ds(rim * (last - (last - 1) * odd), rim), pl.ds(rim * (1 + (last - 1) * odd), rim)
    past_mate, past_cross = pl.ds(rim * ((last + 1) * (1 - odd)), rim), pl.ds(rim * ((last + 1) * odd), rim)
    middle = pl.ds(rim, tile)
    inner_rows = (pl.ds(rim, rim), pl.ds(tile, rim))
    outer_rows = (pl.ds(rim + tile, rim), pl.ds(0, rim))
    halo_sems = (halo_send, halo_recv)
    edge_cross, edge_mate = pl.ds(rim * (last - 1) * odd, rim), pl.ds(rim * (last - 1) * (1 - odd), rim)
    loads = [
        pltpu.make_async_copy(source, target, in_sem.at[index])
        for index, (source, target) in enumerate((
            (obj_hbm.at[0, 0], obj.at[0]), (obj_hbm.at[0, 1], obj.at[1]),
            (left_hbm, left3), (probe_hbm, probe), (amp_hbm.at[0, 0], amp),
            (obj_hbm.at[0, :, :, edge_cross], edge), (right_hbm, right3),
        ))
    ]
    for load in (loads[5], *loads[:5], loads[6]):
        load.start()

    def fixed_point(values):
        return jnp.round(values * SCALE).astype(jnp.int32).astype(jnp.int16)

    loads[5].wait()
    for part in range(2):
        pad[part, middle, near_cross] = fixed_point(edge[part])
    pl.semaphore_wait(barrier, 5)
    halo = [
        send(pad.at[:, rows, near_cross], pad.at[:, rows, past_mate], halo_sems, index, cross)
        for index, rows in enumerate((*inner_rows, pl.ds(2 * rim, tile - 2 * rim)))
    ]
    for part in range(2):
        loads[part].wait()
        pad[part, middle, 2 * rim:tile] = fixed_point(obj[part, :, rim:tile - rim])
        pad[part, middle, near_mate] = fixed_point(obj[part, :, edge_mate])
    halo += [
        send(pad.at[:, inner_rows[k], middle], ring.at[k, :, :, middle], halo_sems, 3 + k, along[k])
        for k in range(2)
    ]
    halo.append(send(pad.at[:, middle, near_mate], pad.at[:, middle, past_cross], halo_sems, 5, mate))

    def halved(values, axis):
        if axis == 0:
            return values[0:rim], values[rim:]
        return values[:, 0:rim], values[:, rim:]

    def stacked(real, imag, axis, mix):
        (real0, real1), (imag0, imag1) = halved(real, axis), halved(imag, axis)
        if mix:
            real0, real1 = real0 + real1, real0 - real1
            imag0, imag1 = imag0 + imag1, imag0 - imag1
        return [jnp.concatenate(pair, axis=axis) for pair in ((real0, imag0), (real1, imag1))]

    def unstacked(first, second, axis, mix):
        (real0, imag0), (real1, imag1) = halved(first, axis), halved(second, axis)
        if mix:
            real0, real1 = real0 + real1, real0 - real1
            imag0, imag1 = imag0 + imag1, imag0 - imag1
        return [jnp.concatenate(pair, axis=axis) for pair in ((real0, real1), (imag0, imag1))]

    def transform3(real, imag, base, mix_after):
        for axis in range(2):
            sides = []
            for place, values in enumerate(stacked(real, imag, axis, True)):
                high, low = halves(values)
                values = jnp.concatenate((high, high, low), axis=axis)
                if axis == 0:
                    sides.append(dot(left3[base + place], values))
                else:
                    sides.append(dot(values, right3[base + place]))
            real, imag = unstacked(*sides, axis, mix_after)
        return real, imag

    def conjugate1(real, imag, base, mix_before):
        for axis in range(2):
            sides = []
            for place, values in enumerate(stacked(real, imag, axis, mix_before)):
                values = values.astype(BF16)
                if axis == 0:
                    sides.append(dot(right3[base + place, 0:patch], values))
                else:
                    sides.append(dot(values, left3[base + place, :, 0:patch]))
            real, imag = unstacked(*sides, axis, True)
        return real, imag

    def one_hot(shape, axis, shift, turn=None):
        index = lax.broadcasted_iota(jnp.int32, shape, 1 - axis)
        if turn is not None:
            index = index + turn
            index = jnp.where(index >= patch, index - patch, index)
        hit = lax.broadcasted_iota(jnp.int32, shape, axis) == index + shift
        return hit.astype(F32).astype(BF16)

    blocks, quads, turned = [], [], []
    for slot in range(2):
        corner = [pos[0, 0, slot, axis] for axis in range(2)]
        turned.append([start < patch for start in corner])
        turns = [jnp.where(flag, rim, 0) for flag in turned[slot]]
        block = [jnp.minimum(start >> 7, (full - span) // 128) for start in corner]
        blocks.append(block)
        pick_rows[slot] = one_hot((rim, span), 1, corner[0] - block[0] * 128, turns[0] + rim)
        pick_cols[slot] = one_hot((span, patch), 0, corner[1] - block[1] * 128, turns[1])
        put_rows[:, slot * patch:(slot + 1) * patch] = one_hot((full, patch), 0, corner[0])
        put_cols[slot] = one_hot((patch, full), 1, corner[1])
        first = [start - rim + turn for start, turn in zip(corner, turns)]
        quad = [jnp.minimum(start >> 7, (tile - patch) // 128) for start in first]
        quads.append(quad)
        quad_rows[slot] = one_hot((rim, patch), 1, first[0] - quad[0] * 128)
        quad_cols[slot] = one_hot((patch, rim), 0, first[1] - quad[1] * 128)

    def select(codes, rows, cols):
        width = codes.shape[1]
        high, low = halves(codes)
        picked = dot(rows, jnp.concatenate((high, low), axis=1)).astype(BF16)
        cells = dot(picked[:, :width], cols) + dot(picked[:, width:], cols)
        return cells.astype(jnp.int32).astype(jnp.int16)

    for slot in range(2):
        for part in range(2):
            block = obj[part, pl.ds(quads[slot][0] * 128, patch), pl.ds(quads[slot][1] * 128, patch)]
            win[depth, slot, part, 0:rim, 0:rim] = select(
                jnp.round(block * SCALE), quad_rows[slot], quad_cols[slot]
            )

    def extract_front(slot, part):
        block = pad[
            part, pl.ds((quads[slot][0] + 1) * 128, patch), pl.ds(blocks[slot][1] * 128, span)
        ]
        cells = select(block.astype(F32), quad_rows[slot], pick_cols[slot, :, rim:])
        win[depth, slot, part, 0:rim, rim:] = cells

    def extract_back(slot, part):
        block = pad[
            part, pl.ds(blocks[slot][0] * 128, span), pl.ds(blocks[slot][1] * 128, span)
        ]
        win[depth, slot, part, rim:] = select(block.astype(F32), pick_rows[slot], pick_cols[slot])

    def swap(buffer, index):
        return pltpu.make_async_remote_copy(
            src_ref=buffer, dst_ref=buffer,
            send_sem=swap_send.at[index], recv_sem=swap_recv.at[index],
            device_id=partner, device_id_type=MESH,
        )

    def patch_of(section, slot):
        parts = []
        for part in range(2):
            codes = win[section, slot, part].astype(F32) * (1.0 / SCALE)
            for axis in range(2):
                front, back = (codes[0:rim], codes[rim:]) if axis == 0 else (codes[:, 0:rim], codes[:, rim:])
                flag = turned[slot][axis]
                codes = jnp.concatenate(
                    (jnp.where(flag, back, front), jnp.where(flag, front, back)), axis=axis
                )
            parts.append(codes)
        return parts

    def swap_piece(slot, section, piece):
        source = win.at[section, slot]
        if piece < 2:
            source = source.at[:, 0:rim, piece * rim:(piece + 1) * rim]
        else:
            source = source.at[pl.ds(piece - 2, 1), rim:patch]
        return swap(source, 4 * slot + piece)

    loads[2].wait()
    loads[3].wait()
    loads[4].wait()
    loads[6].wait()
    place = lax.broadcasted_iota(jnp.int32, (patch, patch), 0)
    order = (
        lax.broadcasted_iota(jnp.int32, (patch, patch), 1)
        == 2 * place - jnp.where(place >= rim, patch - 1, 0)
    ).astype(F32).astype(BF16)
    for slot in range(2):
        rows = dot(order, amp[slot]).astype(BF16)
        turned_amp[slot] = lax.dot_general(
            rows, order, (((1,), (1,)), ((), ())), preferred_element_type=F32
        ).astype(BF16)
    probe_real, probe_imag = probe[0].astype(F32), probe[1].astype(F32)
    for k in range(2):
        halo[k].wait_recv()
        halo.append(
            send(
                pad.at[:, inner_rows[k], past_cross], ring.at[k, :, :, past_cross],
                halo_sems, 6 + k, along[k],
            )
        )
    for slot in range(2):
        swap_piece(slot, depth, 0).start()
    for k in range(2):
        halo[3 + k].wait_recv()
        halo.append(
            send(
                ring.at[k, :, :, near_mate], ring.at[k, :, :, past_cross],
                halo_sems, 8 + k, mate,
            )
        )
    halo[5].wait_recv()
    halo[2].wait_recv()
    for slot in range(2):
        for part in range(2):
            extract_front(slot, part)
        swap_piece(slot, depth, 1).start()
    for copy in halo[6:]:
        copy.wait_recv()
    for k in range(2):
        for part in range(2):
            pad[part, outer_rows[k]] = ring[k, part]

    def propagate(slot):
        obj_real, obj_imag = patch_of(0, slot)
        wave_real, wave_imag = transform3(
            probe_real * obj_real - probe_imag * obj_imag,
            probe_real * obj_imag + probe_imag * obj_real,
            2, True,
        )
        wave[slot, 0] = wave_real.astype(BF16)
        wave[slot, 1] = wave_imag.astype(BF16)

    for slot in range(2):
        for part in range(2):
            extract_back(slot, part)
            swap_piece(slot, depth, 2 + part).start()

    @pl.when(depth == 0)
    def _():
        for slot in range(2):
            propagate(slot)

    for slot in range(2):
        for piece in range(4):
            swap_piece(slot, 1 - depth, piece).wait_recv()

        @pl.when(depth == 1)
        def _():
            propagate(slot)

        wave_real, wave_imag = wave[slot, 0].astype(F32), wave[slot, 1].astype(F32)
        obj_real, obj_imag = patch_of(1, slot)
        far_real, far_imag = transform3(
            wave_real * obj_real - wave_imag * obj_imag,
            wave_real * obj_imag + wave_imag * obj_real,
            0, False,
        )
        power = far_real * far_real + far_imag * far_imag
        weight = live[0, 0, slot].astype(F32)
        factor = weight * (
            1.0 - turned_amp[slot].astype(F32) * lax.rsqrt(jnp.maximum(power, 0.0625))
        )
        back_real, back_imag = conjugate1(far_real * factor, far_imag * factor, 0, False)
        back_real = back_real.astype(BF16).astype(F32)
        back_imag = back_imag.astype(BF16).astype(F32)

        @pl.when(depth == 1)
        def _():
            grads[slot, 0] = (wave_real * back_real + wave_imag * back_imag).astype(BF16)
            grads[slot, 1] = (wave_real * back_imag - wave_imag * back_real).astype(BF16)

        @pl.when(depth == 0)
        def _():
            first_real, first_imag = conjugate1(
                obj_real * back_real + obj_imag * back_imag,
                obj_real * back_imag - obj_imag * back_real,
                2, True,
            )
            first_real = first_real.astype(BF16).astype(F32)
            first_imag = first_imag.astype(BF16).astype(F32)
            grads[slot, 0] = (probe_real * first_real + probe_imag * first_imag).astype(BF16)
            grads[slot, 1] = (probe_real * first_imag - probe_imag * first_real).astype(BF16)

        if slot == 0:
            for part in range(2):
                spread[part, 0:patch] = dot(grads[slot, part], put_cols[slot]).astype(BF16)

    def outside(values):
        return jnp.concatenate((values[:, 0:rim], values[:, rim + tile:]), axis=1)

    outer_cols = outside(put_cols[1])
    outer_ends = jnp.concatenate((put_rows[0:rim], put_rows[rim + tile:]), axis=0)
    for part in range(2):
        cells = dot(grads[1, part], outer_cols).astype(BF16)
        spread[part, patch:, 0:rim] = cells[:, 0:rim]
        spread[part, patch:, rim + tile:] = cells[:, rim:]
    for part in range(2):
        cells = dot(outer_ends, spread[part, :, past_cross]).astype(BF16)
        gpad[part, 0:rim, past_cross] = cells[0:rim]
        gpad[part, rim + tile:, past_cross] = cells[rim:]

    rim_sems = (rim_send, rim_recv)
    edge_rows = (pl.ds(0, rim), pl.ds(rim + tile, rim))
    rims = [
        send(gpad.at[:, edge_rows[k], past_cross], got_c.at[0, k], rim_sems, k, along[k])
        for k in range(2)
    ]
    for part in range(2):
        sides = jnp.concatenate((spread[part, :, past_cross], spread[part, :, past_mate]), axis=1)
        sides = dot(put_rows[...], sides).astype(BF16)
        gpad[part, middle, past_cross] = sides[rim:rim + tile, 0:rim]
        gpad[part, :, past_mate] = sides[:, rim:]
    rims += [
        send(gpad.at[:, edge_rows[k], past_mate], got_c.at[1, k], rim_sems, 2 + k, mate)
        for k in range(2)
    ]
    rims.append(
        send(
            gpad.at[:, pl.ds(2 * rim, tile - 2 * rim), past_cross],
            got_x.at[odd, :, pl.ds(rim, tile - 2 * rim)], rim_sems, 4, cross,
        )
    )
    rims.append(send(gpad.at[:, middle, past_mate], got_x.at[1 - odd], rim_sems, 5, mate))
    for part in range(2):
        spread[part, patch:, middle] = dot(grads[1, part], put_cols[1, :, middle]).astype(BF16)
        ends = dot(outer_ends, spread[part, :, rim:rim + tile]).astype(BF16)
        gpad[part, 0:rim, rim:rim + tile] = ends[0:rim]
        gpad[part, rim + tile:, rim:rim + tile] = ends[rim:]
    for k in range(2):
        rims[2 + k].wait_recv()
        for part in range(2):
            total = gpad[part, edge_rows[k], near_mate].astype(F32) + got_c[1, k, part].astype(F32)
            gpad[part, edge_rows[k], near_mate] = total.astype(BF16)
        rims.append(
            send(gpad.at[:, edge_rows[k], middle], got_y.at[k], rim_sems, 6 + k, along[k])
        )

    for part in range(2):
        center[part] = dot(put_rows[rim:rim + tile], spread[part, :, rim:rim + tile])

    for k in range(2):
        rims[k].wait_recv()
        rows = inner_rows[1 - k]
        for part in range(2):
            total = gpad[part, rows, past_cross].astype(F32) + got_c[0, k, part].astype(F32)
            gpad[part, rows, past_cross] = total.astype(BF16)
        rims.append(
            send(
                gpad.at[:, rows, past_cross], got_x.at[odd, :, pl.ds((1 - k) * (tile - rim), rim)],
                rim_sems, 8 + k, cross,
            )
        )
    for copy in rims[4:8]:
        copy.wait_recv()
    starts = {1: (0, rim), 0: (rim, tile - 2 * rim), -1: (tile - rim, rim)}
    for down in (0, -1, 1):
        if down:
            rims[8 + (1 + down) // 2].wait_recv()
        for right in (-1, 0, 1):
            (top, height), (left, width) = starts[down], starts[right]
            rows, cols = pl.ds(top, height), pl.ds(left, width)
            for part in range(2):
                total = center[part, rows, cols]
                if right:
                    total = total + got_x[(1 + right) // 2, part, rows, :].astype(F32)
                if down:
                    total = total + got_y[(1 + down) // 2, part, :, cols].astype(F32)
                out[0, part, rows, cols] = total

    for copy in halo:
        copy.wait_send()
    for slot in range(2):
        for piece in range(4):
            swap_piece(slot, depth, piece).wait_send()
    for copy in rims:
        copy.wait_send()


def on_device(object_field, probe, amplitude, positions, live):
    tile = object_field.shape[2]
    patch = probe.shape[1]
    rim = patch // 2
    full = tile + patch
    left, right = tables(patch)
    vmem = pl.BlockSpec(memory_space=pltpu.VMEM)
    smem = pl.BlockSpec(memory_space=pltpu.SMEM)
    hbm = pl.BlockSpec(memory_space=pl.ANY)
    dma = pltpu.SemaphoreType.DMA
    gradient = pl.pallas_call(
        functools.partial(
            kernel, tile, patch, lax.axis_size("row"), lax.axis_size("col")
        ),
        out_shape=pltpu.VMEM(object_field.shape, F32),
        in_specs=[smem, smem, hbm, hbm, hbm, hbm, hbm],
        out_specs=vmem,
        scratch_shapes=[
            pltpu.VMEM((2, tile, rim), F32),
            pltpu.VMEM((2, tile, tile), F32),
            pltpu.VMEM((2, patch, patch), BF16),
            pltpu.VMEM((2, patch, patch), BF16),
            pltpu.VMEM((2, patch, patch), BF16),
            pltpu.VMEM((2, full, full), jnp.int16),
            pltpu.VMEM((2, 2, rim, full), jnp.int16),
            pltpu.VMEM((2, 2, 2, patch, patch), jnp.int16),
            pltpu.VMEM((2, 2, patch, patch), BF16),
            pltpu.VMEM((2, 2, patch, patch), BF16),
            pltpu.VMEM((2, tile, tile), F32),
            pltpu.VMEM((2, full, full), BF16),
            pltpu.VMEM((2, 2, tile, rim), BF16),
            pltpu.VMEM((2, 2, rim, tile), BF16),
            pltpu.VMEM((2, 2, 2, rim, rim), BF16),
            pltpu.VMEM(left.shape, BF16),
            pltpu.VMEM(right.shape, BF16),
            pltpu.VMEM((2, rim, patch + rim), BF16),
            pltpu.VMEM((2, patch + rim, patch), BF16),
            pltpu.VMEM((full, 2 * patch), BF16),
            pltpu.VMEM((2, patch, full), BF16),
            pltpu.VMEM((2, rim, patch), BF16),
            pltpu.VMEM((2, patch, rim), BF16),
            pltpu.VMEM((2, 2 * patch, full), BF16),
            dma((7,)), dma((10,)), dma((10,)), dma((8,)), dma((8,)), dma((10,)), dma((10,)),
        ],
        compiler_params=pltpu.CompilerParams(
            collective_id=0, has_side_effects=True, vmem_limit_bytes=56 * 1024 * 1024
        ),
    )(positions, live, object_field, probe, amplitude, jnp.asarray(left), jnp.asarray(right))
    return gradient


def solution(mesh):
    in_specs = (
        P("depth", None, "row", "col"),
        P(),
        P("row", "col", None, None, None),
        P("row", "col", None, None),
        P("row", "col", None),
    )
    out_specs = P("depth", None, "row", "col")
    return jax.shard_map(
        on_device, mesh=mesh, in_specs=in_specs, out_specs=out_specs, check_vma=False
    )
```

```python
import functools
import math

import jax
import jax.numpy as jnp
import ml_dtypes
import numpy as np
from jax import lax
from jax.experimental import pallas as pl
from jax.experimental.pallas import tpu as pltpu
from jax.sharding import PartitionSpec as P

MESH = pl.DeviceIdType.MESH
SCALE = 16384.0
F32 = jnp.float32
BF16 = jnp.bfloat16


def split(values):
    high = values.astype(ml_dtypes.bfloat16)
    low = (values - high.astype(np.float64)).astype(ml_dtypes.bfloat16)
    return high, low


def tables(size):
    steps = np.arange(size)
    angles = 2.0 * math.pi * ((steps[:, None] * steps[None, :]) % size) / size
    fourier = np.exp(-1j * angles) / math.sqrt(size)
    frequency = (steps + size // 2) % size - size // 2
    chirp = np.exp(-1j * math.pi * frequency.astype(np.float64) ** 2 / (2.0 * size))
    spread = fourier.conj() @ (chirp[:, None] * fourier)
    half = size // 2
    same, swapped = spread[:half, :half], spread[:half, half:]
    left, right = [], []
    for table in (fourier[0::2, :half], fourier[1::2, :half], (same + swapped) / 2, (same - swapped) / 2):
        whole = np.block([[table.real, -table.imag], [table.imag, table.real]])
        high, low = split(whole)
        left.append(np.concatenate((high, low, high), axis=1))
        right.append(np.concatenate((high.T, low.T, high.T), axis=0))
    return np.stack(left), np.stack(right)


def dot(left, right):
    return jnp.dot(left, right, preferred_element_type=F32)


def halves(values):
    high = values.astype(BF16)
    return high, (values - high.astype(F32)).astype(BF16)


def kernel(
    tile, patch, n_row, n_col,
    pos, live, obj_hbm, probe_hbm, amp_hbm, left_hbm, right_hbm, out,
    edge, obj, probe, amp, turned_amp, pad, ring, win, wave, grads, gpad, got_x, got_y, got_c,
    left3, right3, pick_rows, pick_cols, put_rows, put_cols, quad_rows, quad_cols, spread,
    in_sem, halo_send, halo_recv, swap_send, swap_recv, rim_send, rim_recv,
):
    rim = patch // 2
    full = tile + patch
    span = patch + rim
    depth, row, col = lax.axis_index("depth"), lax.axis_index("row"), lax.axis_index("col")
    partner = (1 - depth, row, col)

    odd = lax.rem(col, 2)
    away = 2 * odd - 1
    mate = (depth, row, col - away)
    cross = (depth, row, lax.rem(col + away + n_col, n_col))
    along = [(depth, lax.rem(row + step + n_row, n_row), col) for step in (-1, 1)]

    def send(source, target, sems, index, device):
        copy = pltpu.make_async_remote_copy(
            src_ref=source, dst_ref=target, send_sem=sems[0].at[index],
            recv_sem=sems[1].at[index], device_id=device, device_id_type=MESH,
        )
        copy.start()
        return copy

    barrier = pltpu.get_barrier_semaphore()
    for device in (mate, cross, *along, partner):
        pl.semaphore_signal(barrier, inc=1, device_id=device, device_id_type=MESH)
    last = tile // rim
    near_mate, near_cross = pl.ds(rim * (last - (last - 1) * odd), rim), pl.ds(rim * (1 + (last - 1) * odd), rim)
    past_mate, past_cross = pl.ds(rim * ((last + 1) * (1 - odd)), rim), pl.ds(rim * ((last + 1) * odd), rim)
    middle = pl.ds(rim, tile)
    inner_rows = (pl.ds(rim, rim), pl.ds(tile, rim))
    outer_rows = (pl.ds(rim + tile, rim), pl.ds(0, rim))
    halo_sems = (halo_send, halo_recv)
    edge_cross, edge_mate = pl.ds(rim * (last - 1) * odd, rim), pl.ds(rim * (last - 1) * (1 - odd), rim)
    loads = [
        pltpu.make_async_copy(source, target, in_sem.at[index])
        for index, (source, target) in enumerate((
            (obj_hbm.at[0, 0], obj.at[0]), (obj_hbm.at[0, 1], obj.at[1]),
            (left_hbm, left3), (probe_hbm, probe), (amp_hbm.at[0, 0], amp),
            (obj_hbm.at[0, :, :, edge_cross], edge), (right_hbm, right3),
        ))
    ]
    for load in (loads[5], *loads[:5], loads[6]):
        load.start()

    def fixed_point(values):
        return jnp.round(values * SCALE).astype(jnp.int32).astype(jnp.int16)

    loads[5].wait()
    for part in range(2):
        pad[part, middle, near_cross] = fixed_point(edge[part])
    pl.semaphore_wait(barrier, 5)
    halo = [
        send(pad.at[:, rows, near_cross], pad.at[:, rows, past_mate], halo_sems, index, cross)
        for index, rows in enumerate((*inner_rows, pl.ds(2 * rim, tile - 2 * rim)))
    ]
    for part in range(2):
        loads[part].wait()
        pad[part, middle, 2 * rim:tile] = fixed_point(obj[part, :, rim:tile - rim])
        pad[part, middle, near_mate] = fixed_point(obj[part, :, edge_mate])
    halo += [
        send(pad.at[:, inner_rows[k], middle], ring.at[k, :, :, middle], halo_sems, 3 + k, along[k])
        for k in range(2)
    ]
    halo.append(send(pad.at[:, middle, near_mate], pad.at[:, middle, past_cross], halo_sems, 5, mate))

    def halved(values, axis):
        if axis == 0:
            return values[0:rim], values[rim:]
        return values[:, 0:rim], values[:, rim:]

    def stacked(real, imag, axis, mix):
        (real0, real1), (imag0, imag1) = halved(real, axis), halved(imag, axis)
        if mix:
            real0, real1 = real0 + real1, real0 - real1
            imag0, imag1 = imag0 + imag1, imag0 - imag1
        return [jnp.concatenate(pair, axis=axis) for pair in ((real0, imag0), (real1, imag1))]

    def unstacked(first, second, axis, mix):
        (real0, imag0), (real1, imag1) = halved(first, axis), halved(second, axis)
        if mix:
            real0, real1 = real0 + real1, real0 - real1
            imag0, imag1 = imag0 + imag1, imag0 - imag1
        return [jnp.concatenate(pair, axis=axis) for pair in ((real0, real1), (imag0, imag1))]

    def transform3(real, imag, base, mix_after):
        for axis in range(2):
            sides = []
            for place, values in enumerate(stacked(real, imag, axis, True)):
                high, low = halves(values)
                values = jnp.concatenate((high, high, low), axis=axis)
                if axis == 0:
                    sides.append(dot(left3[base + place], values))
                else:
                    sides.append(dot(values, right3[base + place]))
            real, imag = unstacked(*sides, axis, mix_after)
        return real, imag

    def conjugate1(real, imag, base, mix_before):
        for axis in range(2):
            sides = []
            for place, values in enumerate(stacked(real, imag, axis, mix_before)):
                values = values.astype(BF16)
                if axis == 0:
                    sides.append(dot(right3[base + place, 0:patch], values))
                else:
                    sides.append(dot(values, left3[base + place, :, 0:patch]))
            real, imag = unstacked(*sides, axis, True)
        return real, imag

    def one_hot(shape, axis, shift, turn=None):
        index = lax.broadcasted_iota(jnp.int32, shape, 1 - axis)
        if turn is not None:
            index = index + turn
            index = jnp.where(index >= patch, index - patch, index)
        hit = lax.broadcasted_iota(jnp.int32, shape, axis) == index + shift
        return hit.astype(F32).astype(BF16)

    blocks, quads, turned = [], [], []
    for slot in range(2):
        corner = [pos[0, 0, slot, axis] for axis in range(2)]
        turned.append([start < patch for start in corner])
        turns = [jnp.where(flag, rim, 0) for flag in turned[slot]]
        block = [jnp.minimum(start >> 7, (full - span) // 128) for start in corner]
        blocks.append(block)
        pick_rows[slot] = one_hot((rim, span), 1, corner[0] - block[0] * 128, turns[0] + rim)
        pick_cols[slot] = one_hot((span, patch), 0, corner[1] - block[1] * 128, turns[1])
        put_rows[:, slot * patch:(slot + 1) * patch] = one_hot((full, patch), 0, corner[0])
        put_cols[slot] = one_hot((patch, full), 1, corner[1])
        first = [start - rim + turn for start, turn in zip(corner, turns)]
        quad = [jnp.minimum(start >> 7, (tile - patch) // 128) for start in first]
        quads.append(quad)
        quad_rows[slot] = one_hot((rim, patch), 1, first[0] - quad[0] * 128)
        quad_cols[slot] = one_hot((patch, rim), 0, first[1] - quad[1] * 128)

    def select(codes, rows, cols):
        width = codes.shape[1]
        high, low = halves(codes)
        picked = dot(rows, jnp.concatenate((high, low), axis=1)).astype(BF16)
        cells = dot(picked[:, :width], cols) + dot(picked[:, width:], cols)
        return cells.astype(jnp.int32).astype(jnp.int16)

    for slot in range(2):
        for part in range(2):
            block = obj[part, pl.ds(quads[slot][0] * 128, patch), pl.ds(quads[slot][1] * 128, patch)]
            win[depth, slot, part, 0:rim, 0:rim] = select(
                jnp.round(block * SCALE), quad_rows[slot], quad_cols[slot]
            )

    def extract_front(slot, part):
        block = pad[
            part, pl.ds((quads[slot][0] + 1) * 128, patch), pl.ds(blocks[slot][1] * 128, span)
        ]
        cells = select(block.astype(F32), quad_rows[slot], pick_cols[slot, :, rim:])
        win[depth, slot, part, 0:rim, rim:] = cells

    def extract_back(slot, part):
        block = pad[
            part, pl.ds(blocks[slot][0] * 128, span), pl.ds(blocks[slot][1] * 128, span)
        ]
        win[depth, slot, part, rim:] = select(block.astype(F32), pick_rows[slot], pick_cols[slot])

    def swap(buffer, index):
        return pltpu.make_async_remote_copy(
            src_ref=buffer, dst_ref=buffer,
            send_sem=swap_send.at[index], recv_sem=swap_recv.at[index],
            device_id=partner, device_id_type=MESH,
        )

    def patch_of(section, slot):
        parts = []
        for part in range(2):
            codes = win[section, slot, part].astype(F32) * (1.0 / SCALE)
            for axis in range(2):
                front, back = (codes[0:rim], codes[rim:]) if axis == 0 else (codes[:, 0:rim], codes[:, rim:])
                flag = turned[slot][axis]
                codes = jnp.concatenate(
                    (jnp.where(flag, back, front), jnp.where(flag, front, back)), axis=axis
                )
            parts.append(codes)
        return parts

    def swap_piece(slot, section, piece):
        source = win.at[section, slot]
        if piece < 2:
            source = source.at[:, 0:rim, piece * rim:(piece + 1) * rim]
        else:
            source = source.at[pl.ds(piece - 2, 1), rim:patch]
        return swap(source, 4 * slot + piece)

    loads[2].wait()
    loads[3].wait()
    loads[4].wait()
    loads[6].wait()
    place = lax.broadcasted_iota(jnp.int32, (patch, patch), 0)
    order = (
        lax.broadcasted_iota(jnp.int32, (patch, patch), 1)
        == 2 * place - jnp.where(place >= rim, patch - 1, 0)
    ).astype(F32).astype(BF16)
    for slot in range(2):
        rows = dot(order, amp[slot]).astype(BF16)
        turned_amp[slot] = lax.dot_general(
            rows, order, (((1,), (1,)), ((), ())), preferred_element_type=F32
        ).astype(BF16)
    probe_real, probe_imag = probe[0].astype(F32), probe[1].astype(F32)
    for k in range(2):
        halo[k].wait_recv()
        halo.append(
            send(
                pad.at[:, inner_rows[k], past_cross], ring.at[k, :, :, past_cross],
                halo_sems, 6 + k, along[k],
            )
        )
    for slot in range(2):
        swap_piece(slot, depth, 0).start()
    for k in range(2):
        halo[3 + k].wait_recv()
        halo.append(
            send(
                ring.at[k, :, :, near_mate], ring.at[k, :, :, past_cross],
                halo_sems, 8 + k, mate,
            )
        )
    halo[5].wait_recv()
    halo[2].wait_recv()
    for slot in range(2):
        for part in range(2):
            extract_front(slot, part)
        swap_piece(slot, depth, 1).start()
    for copy in halo[6:]:
        copy.wait_recv()
    for k in range(2):
        for part in range(2):
            pad[part, outer_rows[k]] = ring[k, part]

    def propagate(slot):
        obj_real, obj_imag = patch_of(0, slot)
        wave_real, wave_imag = transform3(
            probe_real * obj_real - probe_imag * obj_imag,
            probe_real * obj_imag + probe_imag * obj_real,
            2, True,
        )
        wave[slot, 0] = wave_real.astype(BF16)
        wave[slot, 1] = wave_imag.astype(BF16)

    for slot in range(2):
        for part in range(2):
            extract_back(slot, part)
            swap_piece(slot, depth, 2 + part).start()

    @pl.when(depth == 0)
    def _():
        for slot in range(2):
            propagate(slot)

    for slot in range(2):
        for piece in range(4):
            swap_piece(slot, 1 - depth, piece).wait_recv()

        @pl.when(depth == 1)
        def _():
            propagate(slot)

        wave_real, wave_imag = wave[slot, 0].astype(F32), wave[slot, 1].astype(F32)
        obj_real, obj_imag = patch_of(1, slot)
        far_real, far_imag = transform3(
            wave_real * obj_real - wave_imag * obj_imag,
            wave_real * obj_imag + wave_imag * obj_real,
            0, False,
        )
        power = far_real * far_real + far_imag * far_imag
        weight = live[0, 0, slot].astype(F32)
        factor = weight * (
            1.0 - turned_amp[slot].astype(F32) * lax.rsqrt(jnp.maximum(power, 0.0625))
        )
        back_real, back_imag = conjugate1(far_real * factor, far_imag * factor, 0, False)
        back_real = back_real.astype(BF16).astype(F32)
        back_imag = back_imag.astype(BF16).astype(F32)

        @pl.when(depth == 1)
        def _():
            grads[slot, 0] = (wave_real * back_real + wave_imag * back_imag).astype(BF16)
            grads[slot, 1] = (wave_real * back_imag - wave_imag * back_real).astype(BF16)

        @pl.when(depth == 0)
        def _():
            first_real, first_imag = conjugate1(
                obj_real * back_real + obj_imag * back_imag,
                obj_real * back_imag - obj_imag * back_real,
                2, True,
            )
            first_real = first_real.astype(BF16).astype(F32)
            first_imag = first_imag.astype(BF16).astype(F32)
            grads[slot, 0] = (probe_real * first_real + probe_imag * first_imag).astype(BF16)
            grads[slot, 1] = (probe_real * first_imag - probe_imag * first_real).astype(BF16)

        if slot == 0:
            cells = dot(grads[0].reshape(2 * patch, patch), put_cols[0]).astype(BF16)
            for part in range(2):
                spread[part, 0:patch] = cells[part * patch:(part + 1) * patch]

    outer_cols = jnp.concatenate((put_cols[1, :, 0:rim], put_cols[1, :, rim + tile:]), axis=1)
    outer_ends = jnp.concatenate((put_rows[0:rim], put_rows[rim + tile:]), axis=0)
    last_grads = grads[1].reshape(2 * patch, patch)
    cells = dot(last_grads, outer_cols).astype(BF16)
    for part in range(2):
        spread[part, patch:, 0:rim] = cells[part * patch:(part + 1) * patch, 0:rim]
        spread[part, patch:, rim + tile:] = cells[part * patch:(part + 1) * patch, rim:]
    sides = [(part, place) for place in (past_cross, past_mate) for part in range(2)]
    lanes = jnp.concatenate([spread[part, :, place] for part, place in sides], axis=1)
    cells = dot(outer_ends, lanes).astype(BF16)
    for index, (part, place) in enumerate(sides):
        gpad[part, 0:rim, place] = cells[0:rim, index * rim:(index + 1) * rim]
        gpad[part, rim + tile:, place] = cells[rim:, index * rim:(index + 1) * rim]
    rim_sems = (rim_send, rim_recv)
    edge_rows = (pl.ds(0, rim), pl.ds(rim + tile, rim))
    rims = [
        send(gpad.at[:, edge_rows[k], past_cross], got_c.at[0, k], rim_sems, k, along[k])
        for k in range(2)
    ]
    rims += [
        send(gpad.at[:, edge_rows[k], past_mate], got_c.at[1, k], rim_sems, 2 + k, mate)
        for k in range(2)
    ]
    cells = dot(put_rows[rim:rim + tile], lanes).astype(BF16)
    for index, (part, place) in enumerate(sides):
        gpad[part, middle, place] = cells[:, index * rim:(index + 1) * rim]
    rims.append(
        send(
            gpad.at[:, pl.ds(2 * rim, tile - 2 * rim), past_cross],
            got_x.at[odd, :, pl.ds(rim, tile - 2 * rim)], rim_sems, 4, cross,
        )
    )
    rims.append(send(gpad.at[:, middle, past_mate], got_x.at[1 - odd], rim_sems, 5, mate))

    cells = dot(last_grads, put_cols[1, :, rim:rim + tile]).astype(BF16)
    for part in range(2):
        spread[part, patch:, rim:rim + tile] = cells[part * patch:(part + 1) * patch]
    lanes = jnp.concatenate([spread[part, :, rim:rim + tile] for part in range(2)], axis=1)
    cells = dot(outer_ends, lanes).astype(BF16)
    for part in range(2):
        gpad[part, 0:rim, rim:rim + tile] = cells[0:rim, part * tile:(part + 1) * tile]
        gpad[part, rim + tile:, rim:rim + tile] = cells[rim:, part * tile:(part + 1) * tile]
    rims += [
        send(
            gpad.at[:, edge_rows[k], pl.ds(rim * (1 + odd), tile - rim)],
            got_y.at[k, :, :, pl.ds(rim * odd, tile - rim)], rim_sems, 6 + k, along[k],
        )
        for k in range(2)
    ]
    for k in range(2):
        rims[2 + k].wait_recv()
        for part in range(2):
            total = gpad[part, edge_rows[k], near_mate].astype(F32) + got_c[1, k, part].astype(F32)
            gpad[part, edge_rows[k], near_mate] = total.astype(BF16)
        rims.append(
            send(
                gpad.at[:, edge_rows[k], near_mate], got_y.at[k, :, :, edge_mate],
                rim_sems, 8 + k, along[k],
            )
        )

    for part in range(2):
        out[0, part] = dot(put_rows[rim:rim + tile], spread[part, :, rim:rim + tile])

    tile_rows = (pl.ds(tile - rim, rim), pl.ds(0, rim))
    for k in range(2):
        rims[k].wait_recv()
        rows = inner_rows[1 - k]
        for part in range(2):
            total = gpad[part, rows, past_cross].astype(F32) + got_c[0, k, part].astype(F32)
            gpad[part, rows, past_cross] = total.astype(BF16)
        rims.append(
            send(
                gpad.at[:, rows, past_cross], got_x.at[odd, :, tile_rows[k]],
                rim_sems, 10 + k, cross,
            )
        )
    for copy in rims[4:10]:
        copy.wait_recv()
    core = pl.ds(rim, tile - 2 * rim)
    for part in range(2):
        out[0, part, :, edge_mate] += got_x[odd, part].astype(F32)
        out[0, part, core, edge_cross] += got_x[1 - odd, part, core].astype(F32)
        for k in range(2):
            out[0, part, tile_rows[k]] += got_y[k, part].astype(F32)
    for k in range(2):
        rims[10 + k].wait_recv()
        for part in range(2):
            out[0, part, tile_rows[k], edge_cross] += got_x[1 - odd, part, tile_rows[k]].astype(F32)

    for copy in halo:
        copy.wait_send()
    for slot in range(2):
        for piece in range(4):
            swap_piece(slot, depth, piece).wait_send()
    for copy in rims:
        copy.wait_send()


def on_device(object_field, probe, amplitude, positions, live):
    tile = object_field.shape[2]
    patch = probe.shape[1]
    rim = patch // 2
    full = tile + patch
    left, right = tables(patch)
    vmem = pl.BlockSpec(memory_space=pltpu.VMEM)
    smem = pl.BlockSpec(memory_space=pltpu.SMEM)
    hbm = pl.BlockSpec(memory_space=pl.ANY)
    dma = pltpu.SemaphoreType.DMA
    gradient = pl.pallas_call(
        functools.partial(
            kernel, tile, patch, lax.axis_size("row"), lax.axis_size("col")
        ),
        out_shape=pltpu.VMEM(object_field.shape, F32),
        in_specs=[smem, smem, hbm, hbm, hbm, hbm, hbm],
        out_specs=vmem,
        scratch_shapes=[
            pltpu.VMEM((2, tile, rim), F32),
            pltpu.VMEM((2, tile, tile), F32),
            pltpu.VMEM((2, patch, patch), BF16),
            pltpu.VMEM((2, patch, patch), BF16),
            pltpu.VMEM((2, patch, patch), BF16),
            pltpu.VMEM((2, full, full), jnp.int16),
            pltpu.VMEM((2, 2, rim, full), jnp.int16),
            pltpu.VMEM((2, 2, 2, patch, patch), jnp.int16),
            pltpu.VMEM((2, 2, patch, patch), BF16),
            pltpu.VMEM((2, 2, patch, patch), BF16),
            pltpu.VMEM((2, full, full), BF16),
            pltpu.VMEM((2, 2, tile, rim), BF16),
            pltpu.VMEM((2, 2, rim, tile), BF16),
            pltpu.VMEM((2, 2, 2, rim, rim), BF16),
            pltpu.VMEM(left.shape, BF16),
            pltpu.VMEM(right.shape, BF16),
            pltpu.VMEM((2, rim, patch + rim), BF16),
            pltpu.VMEM((2, patch + rim, patch), BF16),
            pltpu.VMEM((full, 2 * patch), BF16),
            pltpu.VMEM((2, patch, full), BF16),
            pltpu.VMEM((2, rim, patch), BF16),
            pltpu.VMEM((2, patch, rim), BF16),
            pltpu.VMEM((2, 2 * patch, full), BF16),
            dma((7,)), dma((10,)), dma((10,)), dma((8,)), dma((8,)), dma((12,)), dma((12,)),
        ],
        compiler_params=pltpu.CompilerParams(
            collective_id=0, has_side_effects=True, vmem_limit_bytes=56 * 1024 * 1024
        ),
    )(positions, live, object_field, probe, amplitude, jnp.asarray(left), jnp.asarray(right))
    return gradient


def solution(mesh):
    in_specs = (
        P("depth", None, "row", "col"),
        P(),
        P("row", "col", None, None, None),
        P("row", "col", None, None),
        P("row", "col", None),
    )
    out_specs = P("depth", None, "row", "col")
    return jax.shard_map(
        on_device, mesh=mesh, in_specs=in_specs, out_specs=out_specs, check_vma=False
    )
```

```python
import functools
import math

import jax
import jax.numpy as jnp
import ml_dtypes
import numpy as np
from jax import lax
from jax.experimental import pallas as pl
from jax.experimental.pallas import tpu as pltpu
from jax.sharding import PartitionSpec as P

MESH = pl.DeviceIdType.MESH
SCALE = 16384.0
F32 = jnp.float32
BF16 = jnp.bfloat16


def split(values):
    high = values.astype(ml_dtypes.bfloat16)
    low = (values - high.astype(np.float64)).astype(ml_dtypes.bfloat16)
    return high, low


def tables(size):
    steps = np.arange(size)
    angles = 2.0 * math.pi * ((steps[:, None] * steps[None, :]) % size) / size
    fourier = np.exp(-1j * angles) / math.sqrt(size)
    frequency = (steps + size // 2) % size - size // 2
    chirp = np.exp(-1j * math.pi * frequency.astype(np.float64) ** 2 / (2.0 * size))
    spread = fourier.conj() @ (chirp[:, None] * fourier)
    half = size // 2
    same, swapped = spread[:half, :half], spread[:half, half:]
    left, right = [], []
    for table in (fourier[0::2, :half], fourier[1::2, :half], (same + swapped) / 2, (same - swapped) / 2):
        whole = np.block([[table.real, -table.imag], [table.imag, table.real]])
        high, low = split(whole)
        left.append(np.concatenate((high, low, high), axis=1))
        right.append(np.concatenate((high.T, low.T, high.T), axis=0))
    return np.stack(left), np.stack(right)


def dot(left, right):
    return jnp.dot(left, right, preferred_element_type=F32)


def halves(values):
    high = values.astype(BF16)
    return high, (values - high.astype(F32)).astype(BF16)


def kernel(
    tile, patch, n_row, n_col,
    pos, live, obj_hbm, probe_hbm, amp_hbm, left_hbm, right_hbm, out,
    edge, obj, probe, amp, turned_amp, pad, ring, win, wave, grads, gpad, got_x, got_y, got_c,
    left3, right3, pick_rows, pick_cols, put_rows, put_cols, quad_rows, quad_cols, spread,
    in_sem, halo_send, halo_recv, swap_send, swap_recv, rim_send, rim_recv,
):
    rim = patch // 2
    full = tile + patch
    span = patch + rim
    depth, row, col = lax.axis_index("depth"), lax.axis_index("row"), lax.axis_index("col")
    partner = (1 - depth, row, col)

    odd = lax.rem(col, 2)
    away = 2 * odd - 1
    mate = (depth, row, col - away)
    cross = (depth, row, lax.rem(col + away + n_col, n_col))
    along = [(depth, lax.rem(row + step + n_row, n_row), col) for step in (-1, 1)]

    def send(source, target, sems, index, device):
        copy = pltpu.make_async_remote_copy(
            src_ref=source, dst_ref=target, send_sem=sems[0].at[index],
            recv_sem=sems[1].at[index], device_id=device, device_id_type=MESH,
        )
        copy.start()
        return copy

    barrier = pltpu.get_barrier_semaphore()
    for device in (mate, cross, *along, partner):
        pl.semaphore_signal(barrier, inc=1, device_id=device, device_id_type=MESH)
    last = tile // rim
    near_mate, near_cross = pl.ds(rim * (last - (last - 1) * odd), rim), pl.ds(rim * (1 + (last - 1) * odd), rim)
    past_mate, past_cross = pl.ds(rim * ((last + 1) * (1 - odd)), rim), pl.ds(rim * ((last + 1) * odd), rim)
    middle = pl.ds(rim, tile)
    inner_rows = (pl.ds(rim, rim), pl.ds(tile, rim))
    outer_rows = (pl.ds(rim + tile, rim), pl.ds(0, rim))
    halo_sems = (halo_send, halo_recv)
    edge_cross, edge_mate = pl.ds(rim * (last - 1) * odd, rim), pl.ds(rim * (last - 1) * (1 - odd), rim)
    loads = [
        pltpu.make_async_copy(source, target, in_sem.at[index])
        for index, (source, target) in enumerate((
            (obj_hbm.at[0, 0], obj.at[0]), (obj_hbm.at[0, 1], obj.at[1]),
            (left_hbm, left3), (probe_hbm, probe), (amp_hbm.at[0, 0], amp),
            (obj_hbm.at[0, :, :, edge_cross], edge), (right_hbm, right3),
        ))
    ]
    for load in (loads[5], *loads[:5], loads[6]):
        load.start()

    def fixed_point(values):
        return jnp.round(values * SCALE).astype(jnp.int32).astype(jnp.int16)

    loads[5].wait()
    for part in range(2):
        pad[part, middle, near_cross] = fixed_point(edge[part])
    pl.semaphore_wait(barrier, 5)
    halo = [
        send(pad.at[:, rows, near_cross], pad.at[:, rows, past_mate], halo_sems, index, cross)
        for index, rows in enumerate((*inner_rows, pl.ds(2 * rim, tile - 2 * rim)))
    ]
    for part in range(2):
        loads[part].wait()
        pad[part, middle, 2 * rim:tile] = fixed_point(obj[part, :, rim:tile - rim])
        pad[part, middle, near_mate] = fixed_point(obj[part, :, edge_mate])
    halo += [
        send(pad.at[:, inner_rows[k], middle], ring.at[k, :, :, middle], halo_sems, 3 + k, along[k])
        for k in range(2)
    ]
    halo.append(send(pad.at[:, middle, near_mate], pad.at[:, middle, past_cross], halo_sems, 5, mate))

    def halved(values, axis):
        if axis == 0:
            return values[0:rim], values[rim:]
        return values[:, 0:rim], values[:, rim:]

    def stacked(real, imag, axis, mix):
        (real0, real1), (imag0, imag1) = halved(real, axis), halved(imag, axis)
        if mix:
            real0, real1 = real0 + real1, real0 - real1
            imag0, imag1 = imag0 + imag1, imag0 - imag1
        return [jnp.concatenate(pair, axis=axis) for pair in ((real0, imag0), (real1, imag1))]

    def unstacked(first, second, axis, mix):
        (real0, imag0), (real1, imag1) = halved(first, axis), halved(second, axis)
        if mix:
            real0, real1 = real0 + real1, real0 - real1
            imag0, imag1 = imag0 + imag1, imag0 - imag1
        return [jnp.concatenate(pair, axis=axis) for pair in ((real0, real1), (imag0, imag1))]

    def transform3(real, imag, base, mix_after):
        for axis in range(2):
            sides = []
            for place, values in enumerate(stacked(real, imag, axis, True)):
                high, low = halves(values)
                values = jnp.concatenate((high, high, low), axis=axis)
                if axis == 0:
                    sides.append(dot(left3[base + place], values))
                else:
                    sides.append(dot(values, right3[base + place]))
            real, imag = unstacked(*sides, axis, mix_after)
        return real, imag

    def conjugate1(real, imag, base, mix_before):
        for axis in range(2):
            sides = []
            for place, values in enumerate(stacked(real, imag, axis, mix_before)):
                values = values.astype(BF16)
                if axis == 0:
                    sides.append(dot(right3[base + place, 0:patch], values))
                else:
                    sides.append(dot(values, left3[base + place, :, 0:patch]))
            real, imag = unstacked(*sides, axis, True)
        return real, imag

    def one_hot(shape, axis, shift, turn=None):
        index = lax.broadcasted_iota(jnp.int32, shape, 1 - axis)
        if turn is not None:
            index = index + turn
            index = jnp.where(index >= patch, index - patch, index)
        hit = lax.broadcasted_iota(jnp.int32, shape, axis) == index + shift
        return hit.astype(F32).astype(BF16)

    blocks, quads, turned = [], [], []
    for slot in range(2):
        corner = [pos[0, 0, slot, axis] for axis in range(2)]
        turned.append([start < patch for start in corner])
        turns = [jnp.where(flag, rim, 0) for flag in turned[slot]]
        block = [jnp.minimum(start >> 7, (full - span) // 128) for start in corner]
        blocks.append(block)
        pick_rows[slot] = one_hot((rim, span), 1, corner[0] - block[0] * 128, turns[0] + rim)
        pick_cols[slot] = one_hot((span, patch), 0, corner[1] - block[1] * 128, turns[1])
        put_rows[:, slot * patch:(slot + 1) * patch] = one_hot((full, patch), 0, corner[0])
        put_cols[slot] = one_hot((patch, full), 1, corner[1])
        first = [start - rim + turn for start, turn in zip(corner, turns)]
        quad = [jnp.minimum(start >> 7, (tile - patch) // 128) for start in first]
        quads.append(quad)
        quad_rows[slot] = one_hot((rim, patch), 1, first[0] - quad[0] * 128)
        quad_cols[slot] = one_hot((patch, rim), 0, first[1] - quad[1] * 128)

    def select(codes, rows, cols):
        width = codes.shape[1]
        high, low = halves(codes)
        picked = dot(rows, jnp.concatenate((high, low), axis=1)).astype(BF16)
        cells = dot(picked[:, :width], cols) + dot(picked[:, width:], cols)
        return cells.astype(jnp.int32).astype(jnp.int16)

    for slot in range(2):
        for part in range(2):
            block = obj[part, pl.ds(quads[slot][0] * 128, patch), pl.ds(quads[slot][1] * 128, patch)]
            win[depth, slot, part, 0:rim, 0:rim] = select(
                jnp.round(block * SCALE), quad_rows[slot], quad_cols[slot]
            )

    def extract_front(slot, part):
        block = pad[
            part, pl.ds((quads[slot][0] + 1) * 128, patch), pl.ds(blocks[slot][1] * 128, span)
        ]
        cells = select(block.astype(F32), quad_rows[slot], pick_cols[slot, :, rim:])
        win[depth, slot, part, 0:rim, rim:] = cells

    def extract_back(slot, part):
        block = pad[
            part, pl.ds(blocks[slot][0] * 128, span), pl.ds(blocks[slot][1] * 128, span)
        ]
        win[depth, slot, part, rim:] = select(block.astype(F32), pick_rows[slot], pick_cols[slot])

    def swap(buffer, index):
        return pltpu.make_async_remote_copy(
            src_ref=buffer, dst_ref=buffer,
            send_sem=swap_send.at[index], recv_sem=swap_recv.at[index],
            device_id=partner, device_id_type=MESH,
        )

    def patch_of(section, slot):
        parts = []
        for part in range(2):
            codes = win[section, slot, part].astype(F32) * (1.0 / SCALE)
            for axis in range(2):
                front, back = (codes[0:rim], codes[rim:]) if axis == 0 else (codes[:, 0:rim], codes[:, rim:])
                flag = turned[slot][axis]
                codes = jnp.concatenate(
                    (jnp.where(flag, back, front), jnp.where(flag, front, back)), axis=axis
                )
            parts.append(codes)
        return parts

    def swap_piece(slot, section, piece):
        source = win.at[section, slot]
        if piece < 2:
            source = source.at[:, 0:rim, piece * rim:(piece + 1) * rim]
        else:
            source = source.at[pl.ds(piece - 2, 1), rim:patch]
        return swap(source, 4 * slot + piece)

    loads[2].wait()
    loads[3].wait()
    loads[4].wait()
    loads[6].wait()
    place = lax.broadcasted_iota(jnp.int32, (patch, patch), 0)
    order = (
        lax.broadcasted_iota(jnp.int32, (patch, patch), 1)
        == 2 * place - jnp.where(place >= rim, patch - 1, 0)
    ).astype(F32).astype(BF16)
    for slot in range(2):
        rows = dot(order, amp[slot]).astype(BF16)
        turned_amp[slot] = lax.dot_general(
            rows, order, (((1,), (1,)), ((), ())), preferred_element_type=F32
        ).astype(BF16)
    probe_real, probe_imag = probe[0].astype(F32), probe[1].astype(F32)
    halo[2].wait_send()
    for slot in range(2):
        swap_piece(slot, depth, 0).start()
    for k in range(2):
        halo[k].wait_recv()
        halo.append(
            send(
                pad.at[:, inner_rows[k], past_cross], ring.at[k, :, :, past_cross],
                halo_sems, 6 + k, along[k],
            )
        )
    for k in range(2):
        halo[3 + k].wait_recv()
        halo.append(
            send(
                ring.at[k, :, :, near_mate], ring.at[k, :, :, past_cross],
                halo_sems, 8 + k, mate,
            )
        )
    halo[5].wait_recv()
    halo[2].wait_recv()
    for part in range(2):
        extract_front(0, part)
    swap_piece(0, depth, 1).start()
    for copy in halo[6:]:
        copy.wait_recv()
    for k in range(2):
        for part in range(2):
            pad[part, outer_rows[k]] = ring[k, part]

    def propagate(slot):
        obj_real, obj_imag = patch_of(0, slot)
        wave_real, wave_imag = transform3(
            probe_real * obj_real - probe_imag * obj_imag,
            probe_real * obj_imag + probe_imag * obj_real,
            2, True,
        )
        wave[slot, 0] = wave_real.astype(BF16)
        wave[slot, 1] = wave_imag.astype(BF16)

    for slot in range(2):
        if slot == 1:
            for part in range(2):
                extract_front(1, part)
            swap_piece(1, depth, 1).start()
        for part in range(2):
            extract_back(slot, part)
            swap_piece(slot, depth, 2 + part).start()

    @pl.when(depth == 0)
    def _():
        for slot in range(2):
            propagate(slot)

    for slot in range(2):
        for piece in range(4):
            swap_piece(slot, 1 - depth, piece).wait_recv()

        @pl.when(depth == 1)
        def _():
            propagate(slot)

        wave_real, wave_imag = wave[slot, 0].astype(F32), wave[slot, 1].astype(F32)
        obj_real, obj_imag = patch_of(1, slot)
        far_real, far_imag = transform3(
            wave_real * obj_real - wave_imag * obj_imag,
            wave_real * obj_imag + wave_imag * obj_real,
            0, False,
        )
        power = far_real * far_real + far_imag * far_imag
        weight = live[0, 0, slot].astype(F32)
        factor = weight * (
            1.0 - turned_amp[slot].astype(F32) * lax.rsqrt(jnp.maximum(power, 0.0625))
        )
        back_real, back_imag = conjugate1(far_real * factor, far_imag * factor, 0, False)
        back_real = back_real.astype(BF16).astype(F32)
        back_imag = back_imag.astype(BF16).astype(F32)

        @pl.when(depth == 1)
        def _():
            grads[slot, 0] = (wave_real * back_real + wave_imag * back_imag).astype(BF16)
            grads[slot, 1] = (wave_real * back_imag - wave_imag * back_real).astype(BF16)

        @pl.when(depth == 0)
        def _():
            first_real, first_imag = conjugate1(
                obj_real * back_real + obj_imag * back_imag,
                obj_real * back_imag - obj_imag * back_real,
                2, True,
            )
            first_real = first_real.astype(BF16).astype(F32)
            first_imag = first_imag.astype(BF16).astype(F32)
            grads[slot, 0] = (probe_real * first_real + probe_imag * first_imag).astype(BF16)
            grads[slot, 1] = (probe_real * first_imag - probe_imag * first_real).astype(BF16)

        if slot == 0:
            cells = dot(grads[0].reshape(2 * patch, patch), put_cols[0]).astype(BF16)
            for part in range(2):
                spread[part, 0:patch] = cells[part * patch:(part + 1) * patch]

    outer_cols = jnp.concatenate((put_cols[1, :, 0:rim], put_cols[1, :, rim + tile:]), axis=1)
    outer_ends = jnp.concatenate((put_rows[0:rim], put_rows[rim + tile:]), axis=0)
    last_grads = grads[1].reshape(2 * patch, patch)
    cells = dot(last_grads, outer_cols).astype(BF16)
    for part in range(2):
        spread[part, patch:, 0:rim] = cells[part * patch:(part + 1) * patch, 0:rim]
        spread[part, patch:, rim + tile:] = cells[part * patch:(part + 1) * patch, rim:]
    sides = [(part, place) for place in (past_cross, past_mate) for part in range(2)]
    lanes = jnp.concatenate([spread[part, :, place] for part, place in sides], axis=1)
    cells = dot(outer_ends, lanes).astype(BF16)
    for index, (part, place) in enumerate(sides):
        gpad[part, 0:rim, place] = cells[0:rim, index * rim:(index + 1) * rim]
        gpad[part, rim + tile:, place] = cells[rim:, index * rim:(index + 1) * rim]
    rim_sems = (rim_send, rim_recv)
    edge_rows = (pl.ds(0, rim), pl.ds(rim + tile, rim))
    rims = [
        send(gpad.at[:, edge_rows[k], past_cross], got_c.at[0, k], rim_sems, k, along[k])
        for k in range(2)
    ]
    rims += [
        send(gpad.at[:, edge_rows[k], past_mate], got_c.at[1, k], rim_sems, 2 + k, mate)
        for k in range(2)
    ]
    cells = dot(put_rows[rim:rim + tile], lanes).astype(BF16)
    for index, (part, place) in enumerate(sides):
        gpad[part, middle, place] = cells[:, index * rim:(index + 1) * rim]
    rims.append(
        send(
            gpad.at[:, pl.ds(2 * rim, tile - 2 * rim), past_cross],
            got_x.at[odd, :, pl.ds(rim, tile - 2 * rim)], rim_sems, 4, cross,
        )
    )
    rims.append(send(gpad.at[:, middle, past_mate], got_x.at[1 - odd], rim_sems, 5, mate))

    cells = dot(last_grads, put_cols[1, :, rim:rim + tile]).astype(BF16)
    for part in range(2):
        spread[part, patch:, rim:rim + tile] = cells[part * patch:(part + 1) * patch]
    lanes = jnp.concatenate([spread[part, :, rim:rim + tile] for part in range(2)], axis=1)
    cells = dot(outer_ends, lanes).astype(BF16)
    for part in range(2):
        gpad[part, 0:rim, rim:rim + tile] = cells[0:rim, part * tile:(part + 1) * tile]
        gpad[part, rim + tile:, rim:rim + tile] = cells[rim:, part * tile:(part + 1) * tile]
    rims += [
        send(
            gpad.at[:, edge_rows[k], pl.ds(rim * (1 + odd), tile - rim)],
            got_y.at[k, :, :, pl.ds(rim * odd, tile - rim)], rim_sems, 6 + k, along[k],
        )
        for k in range(2)
    ]
    for k in range(2):
        rims[2 + k].wait_recv()
        for part in range(2):
            total = gpad[part, edge_rows[k], near_mate].astype(F32) + got_c[1, k, part].astype(F32)
            gpad[part, edge_rows[k], near_mate] = total.astype(BF16)
        rims.append(
            send(
                gpad.at[:, edge_rows[k], near_mate], got_y.at[k, :, :, edge_mate],
                rim_sems, 8 + k, along[k],
            )
        )

    for part in range(2):
        out[0, part] = dot(put_rows[rim:rim + tile], spread[part, :, rim:rim + tile])

    tile_rows = (pl.ds(tile - rim, rim), pl.ds(0, rim))
    for k in range(2):
        rims[k].wait_recv()
        rows = inner_rows[1 - k]
        for part in range(2):
            total = gpad[part, rows, past_cross].astype(F32) + got_c[0, k, part].astype(F32)
            gpad[part, rows, past_cross] = total.astype(BF16)
        rims.append(
            send(
                gpad.at[:, rows, past_cross], got_x.at[odd, :, tile_rows[k]],
                rim_sems, 10 + k, cross,
            )
        )
    for copy in rims[4:10]:
        copy.wait_recv()
    core = pl.ds(rim, tile - 2 * rim)
    for part in range(2):
        out[0, part, :, edge_mate] += got_x[odd, part].astype(F32)
        out[0, part, core, edge_cross] += got_x[1 - odd, part, core].astype(F32)
        for k in range(2):
            out[0, part, tile_rows[k]] += got_y[k, part].astype(F32)
    for k in range(2):
        rims[10 + k].wait_recv()
        for part in range(2):
            out[0, part, tile_rows[k], edge_cross] += got_x[1 - odd, part, tile_rows[k]].astype(F32)

    for copy in (*halo[0:2], *halo[3:]):
        copy.wait_send()
    for slot in range(2):
        for piece in range(4):
            swap_piece(slot, depth, piece).wait_send()
    for copy in rims:
        copy.wait_send()


def on_device(object_field, probe, amplitude, positions, live):
    tile = object_field.shape[2]
    patch = probe.shape[1]
    rim = patch // 2
    full = tile + patch
    left, right = tables(patch)
    vmem = pl.BlockSpec(memory_space=pltpu.VMEM)
    smem = pl.BlockSpec(memory_space=pltpu.SMEM)
    hbm = pl.BlockSpec(memory_space=pl.ANY)
    dma = pltpu.SemaphoreType.DMA
    gradient = pl.pallas_call(
        functools.partial(
            kernel, tile, patch, lax.axis_size("row"), lax.axis_size("col")
        ),
        out_shape=pltpu.VMEM(object_field.shape, F32),
        in_specs=[smem, smem, hbm, hbm, hbm, hbm, hbm],
        out_specs=vmem,
        scratch_shapes=[
            pltpu.VMEM((2, tile, rim), F32),
            pltpu.VMEM((2, tile, tile), F32),
            pltpu.VMEM((2, patch, patch), BF16),
            pltpu.VMEM((2, patch, patch), BF16),
            pltpu.VMEM((2, patch, patch), BF16),
            pltpu.VMEM((2, full, full), jnp.int16),
            pltpu.VMEM((2, 2, rim, full), jnp.int16),
            pltpu.VMEM((2, 2, 2, patch, patch), jnp.int16),
            pltpu.VMEM((2, 2, patch, patch), BF16),
            pltpu.VMEM((2, 2, patch, patch), BF16),
            pltpu.VMEM((2, full, full), BF16),
            pltpu.VMEM((2, 2, tile, rim), BF16),
            pltpu.VMEM((2, 2, rim, tile), BF16),
            pltpu.VMEM((2, 2, 2, rim, rim), BF16),
            pltpu.VMEM(left.shape, BF16),
            pltpu.VMEM(right.shape, BF16),
            pltpu.VMEM((2, rim, patch + rim), BF16),
            pltpu.VMEM((2, patch + rim, patch), BF16),
            pltpu.VMEM((full, 2 * patch), BF16),
            pltpu.VMEM((2, patch, full), BF16),
            pltpu.VMEM((2, rim, patch), BF16),
            pltpu.VMEM((2, patch, rim), BF16),
            pltpu.VMEM((2, 2 * patch, full), BF16),
            dma((7,)), dma((10,)), dma((10,)), dma((8,)), dma((8,)), dma((12,)), dma((12,)),
        ],
        compiler_params=pltpu.CompilerParams(
            collective_id=0, has_side_effects=True, vmem_limit_bytes=56 * 1024 * 1024
        ),
    )(positions, live, object_field, probe, amplitude, jnp.asarray(left), jnp.asarray(right))
    return gradient


def solution(mesh):
    in_specs = (
        P("depth", None, "row", "col"),
        P(),
        P("row", "col", None, None, None),
        P("row", "col", None, None),
        P("row", "col", None),
    )
    out_specs = P("depth", None, "row", "col")
    return jax.shard_map(
        on_device, mesh=mesh, in_specs=in_specs, out_specs=out_specs, check_vma=False
    )
```

```python
import functools
import math

import jax
import jax.numpy as jnp
import ml_dtypes
import numpy as np
from jax import lax
from jax.experimental import pallas as pl
from jax.experimental.pallas import tpu as pltpu
from jax.sharding import PartitionSpec as P

MESH = pl.DeviceIdType.MESH
SCALE = 16384.0
F32 = jnp.float32
BF16 = jnp.bfloat16


def split(values):
    high = values.astype(ml_dtypes.bfloat16)
    low = (values - high.astype(np.float64)).astype(ml_dtypes.bfloat16)
    return high, low


def tables(size):
    steps = np.arange(size)
    angles = 2.0 * math.pi * ((steps[:, None] * steps[None, :]) % size) / size
    fourier = np.exp(-1j * angles) / math.sqrt(size)
    frequency = (steps + size // 2) % size - size // 2
    chirp = np.exp(-1j * math.pi * frequency.astype(np.float64) ** 2 / (2.0 * size))
    spread = fourier.conj() @ (chirp[:, None] * fourier)
    half = size // 2
    same, swapped = spread[:half, :half], spread[:half, half:]
    left, right = [], []
    for table in (fourier[0::2, :half], fourier[1::2, :half], (same + swapped) / 2, (same - swapped) / 2):
        whole = np.block([[table.real, -table.imag], [table.imag, table.real]])
        high, low = split(whole)
        left.append(np.concatenate((high, low, high), axis=1))
        right.append(np.concatenate((high.T, low.T, high.T), axis=0))
    return np.stack(left), np.stack(right)


def dot(left, right):
    return jnp.dot(left, right, preferred_element_type=F32)


def halves(values):
    high = values.astype(BF16)
    return high, (values - high.astype(F32)).astype(BF16)


def kernel(
    tile, patch, n_row, n_col,
    pos, live, obj_hbm, probe_hbm, amp_hbm, left_hbm, right_hbm, out,
    edge, obj, probe, amp, turned_amp, pad, ring, win, wave, grads, gpad, got_x, got_y, got_c,
    left3, right3, pick_rows, pick_cols, put_rows, put_cols, quad_rows, quad_cols, spread,
    in_sem, halo_send, halo_recv, swap_send, swap_recv, rim_send, rim_recv,
):
    rim = patch // 2
    full = tile + patch
    span = patch + rim
    depth, row, col = lax.axis_index("depth"), lax.axis_index("row"), lax.axis_index("col")
    partner = (1 - depth, row, col)

    odd = lax.rem(col, 2)
    away = 2 * odd - 1
    mate = (depth, row, col - away)
    cross = (depth, row, lax.rem(col + away + n_col, n_col))
    along = [(depth, lax.rem(row + step + n_row, n_row), col) for step in (-1, 1)]

    def send(source, target, sems, index, device):
        copy = pltpu.make_async_remote_copy(
            src_ref=source, dst_ref=target, send_sem=sems[0].at[index],
            recv_sem=sems[1].at[index], device_id=device, device_id_type=MESH,
        )
        copy.start()
        return copy

    barrier = pltpu.get_barrier_semaphore()
    for device in (mate, cross, *along, partner):
        pl.semaphore_signal(barrier, inc=1, device_id=device, device_id_type=MESH)
    last = tile // rim
    near_mate, near_cross = pl.ds(rim * (last - (last - 1) * odd), rim), pl.ds(rim * (1 + (last - 1) * odd), rim)
    past_mate, past_cross = pl.ds(rim * ((last + 1) * (1 - odd)), rim), pl.ds(rim * ((last + 1) * odd), rim)
    middle = pl.ds(rim, tile)
    inner_rows = (pl.ds(rim, rim), pl.ds(tile, rim))
    outer_rows = (pl.ds(rim + tile, rim), pl.ds(0, rim))
    halo_sems = (halo_send, halo_recv)
    edge_cross, edge_mate = pl.ds(rim * (last - 1) * odd, rim), pl.ds(rim * (last - 1) * (1 - odd), rim)
    loads = [
        pltpu.make_async_copy(source, target, in_sem.at[index])
        for index, (source, target) in enumerate((
            (obj_hbm.at[0, 0], obj.at[0]), (obj_hbm.at[0, 1], obj.at[1]),
            (left_hbm, left3), (probe_hbm, probe), (amp_hbm.at[0, 0], amp),
            (obj_hbm.at[0, :, :, edge_cross], edge), (right_hbm, right3),
        ))
    ]
    for load in (loads[5], loads[0], loads[1]):
        load.start()

    def fixed_point(values):
        return jnp.round(values * SCALE).astype(jnp.int32).astype(jnp.int16)

    loads[5].wait()
    for part in range(2):
        pad[part, middle, near_cross] = fixed_point(edge[part])
    pl.semaphore_wait(barrier, 5)
    halo = [
        send(pad.at[:, rows, near_cross], pad.at[:, rows, past_mate], halo_sems, index, cross)
        for index, rows in enumerate((*inner_rows, pl.ds(2 * rim, tile - 2 * rim)))
    ]
    for load in (*loads[2:5], loads[6]):
        load.start()
    for part in range(2):
        loads[part].wait()
        pad[part, middle, 2 * rim:tile] = fixed_point(obj[part, :, rim:tile - rim])
        pad[part, middle, near_mate] = fixed_point(obj[part, :, edge_mate])
    halo += [
        send(pad.at[:, inner_rows[k], middle], ring.at[k, :, :, middle], halo_sems, 3 + k, along[k])
        for k in range(2)
    ]
    halo.append(send(pad.at[:, middle, near_mate], pad.at[:, middle, past_cross], halo_sems, 5, mate))

    def halved(values, axis):
        if axis == 0:
            return values[0:rim], values[rim:]
        return values[:, 0:rim], values[:, rim:]

    def stacked(real, imag, axis, mix):
        (real0, real1), (imag0, imag1) = halved(real, axis), halved(imag, axis)
        if mix:
            real0, real1 = real0 + real1, real0 - real1
            imag0, imag1 = imag0 + imag1, imag0 - imag1
        return [jnp.concatenate(pair, axis=axis) for pair in ((real0, imag0), (real1, imag1))]

    def unstacked(first, second, axis, mix):
        (real0, imag0), (real1, imag1) = halved(first, axis), halved(second, axis)
        if mix:
            real0, real1 = real0 + real1, real0 - real1
            imag0, imag1 = imag0 + imag1, imag0 - imag1
        return [jnp.concatenate(pair, axis=axis) for pair in ((real0, real1), (imag0, imag1))]

    def transform3(real, imag, base, mix_after):
        for axis in range(2):
            sides = []
            for place, values in enumerate(stacked(real, imag, axis, True)):
                high, low = halves(values)
                values = jnp.concatenate((high, high, low), axis=axis)
                if axis == 0:
                    sides.append(dot(left3[base + place], values))
                else:
                    sides.append(dot(values, right3[base + place]))
            real, imag = unstacked(*sides, axis, mix_after)
        return real, imag

    def conjugate1(real, imag, base, mix_before):
        for axis in range(2):
            sides = []
            for place, values in enumerate(stacked(real, imag, axis, mix_before)):
                values = values.astype(BF16)
                if axis == 0:
                    sides.append(dot(right3[base + place, 0:patch], values))
                else:
                    sides.append(dot(values, left3[base + place, :, 0:patch]))
            real, imag = unstacked(*sides, axis, True)
        return real, imag

    def one_hot(shape, axis, shift, turn=None):
        index = lax.broadcasted_iota(jnp.int32, shape, 1 - axis)
        if turn is not None:
            index = index + turn
            index = jnp.where(index >= patch, index - patch, index)
        hit = lax.broadcasted_iota(jnp.int32, shape, axis) == index + shift
        return hit.astype(F32).astype(BF16)

    blocks, quads, turned = [], [], []
    for slot in range(2):
        corner = [pos[0, 0, slot, axis] for axis in range(2)]
        turned.append([start < patch for start in corner])
        turns = [jnp.where(flag, rim, 0) for flag in turned[slot]]
        block = [jnp.minimum(start >> 7, (full - span) // 128) for start in corner]
        blocks.append(block)
        pick_rows[slot] = one_hot((rim, span), 1, corner[0] - block[0] * 128, turns[0] + rim)
        pick_cols[slot] = one_hot((span, patch), 0, corner[1] - block[1] * 128, turns[1])
        put_rows[:, slot * patch:(slot + 1) * patch] = one_hot((full, patch), 0, corner[0])
        put_cols[slot] = one_hot((patch, full), 1, corner[1])
        first = [start - rim + turn for start, turn in zip(corner, turns)]
        quad = [jnp.minimum(start >> 7, (tile - patch) // 128) for start in first]
        quads.append(quad)
        quad_rows[slot] = one_hot((rim, patch), 1, first[0] - quad[0] * 128)
        quad_cols[slot] = one_hot((patch, rim), 0, first[1] - quad[1] * 128)

    def select(codes, rows, cols):
        width = codes.shape[1]
        high, low = halves(codes)
        picked = dot(rows, jnp.concatenate((high, low), axis=1)).astype(BF16)
        cells = dot(picked[:, :width], cols) + dot(picked[:, width:], cols)
        return cells.astype(jnp.int32).astype(jnp.int16)

    for slot in range(2):
        for part in range(2):
            block = obj[part, pl.ds(quads[slot][0] * 128, patch), pl.ds(quads[slot][1] * 128, patch)]
            win[depth, slot, part, 0:rim, 0:rim] = select(
                jnp.round(block * SCALE), quad_rows[slot], quad_cols[slot]
            )

    def extract_front(slot, part):
        block = pad[
            part, pl.ds((quads[slot][0] + 1) * 128, patch), pl.ds(blocks[slot][1] * 128, span)
        ]
        cells = select(block.astype(F32), quad_rows[slot], pick_cols[slot, :, rim:])
        win[depth, slot, part, 0:rim, rim:] = cells

    def extract_back(slot, part):
        block = pad[
            part, pl.ds(blocks[slot][0] * 128, span), pl.ds(blocks[slot][1] * 128, span)
        ]
        win[depth, slot, part, rim:] = select(block.astype(F32), pick_rows[slot], pick_cols[slot])

    def swap(buffer, index):
        return pltpu.make_async_remote_copy(
            src_ref=buffer, dst_ref=buffer,
            send_sem=swap_send.at[index], recv_sem=swap_recv.at[index],
            device_id=partner, device_id_type=MESH,
        )

    def patch_of(section, slot):
        parts = []
        for part in range(2):
            codes = win[section, slot, part].astype(F32) * (1.0 / SCALE)
            for axis in range(2):
                front, back = (codes[0:rim], codes[rim:]) if axis == 0 else (codes[:, 0:rim], codes[:, rim:])
                flag = turned[slot][axis]
                codes = jnp.concatenate(
                    (jnp.where(flag, back, front), jnp.where(flag, front, back)), axis=axis
                )
            parts.append(codes)
        return parts

    def swap_piece(slot, section, piece):
        source = win.at[section, slot]
        if piece < 2:
            source = source.at[:, 0:rim, piece * rim:(piece + 1) * rim]
        else:
            source = source.at[pl.ds(piece - 2, 1), rim:patch]
        return swap(source, 4 * slot + piece)

    loads[2].wait()
    loads[3].wait()
    loads[4].wait()
    loads[6].wait()
    place = lax.broadcasted_iota(jnp.int32, (patch, patch), 0)
    order = (
        lax.broadcasted_iota(jnp.int32, (patch, patch), 1)
        == 2 * place - jnp.where(place >= rim, patch - 1, 0)
    ).astype(F32).astype(BF16)
    for slot in range(2):
        rows = dot(order, amp[slot]).astype(BF16)
        turned_amp[slot] = lax.dot_general(
            rows, order, (((1,), (1,)), ((), ())), preferred_element_type=F32
        ).astype(BF16)
    probe_real, probe_imag = probe[0].astype(F32), probe[1].astype(F32)
    for k in range(2):
        halo[k].wait_recv()
        halo.append(
            send(
                pad.at[:, inner_rows[k], past_cross], ring.at[k, :, :, past_cross],
                halo_sems, 6 + k, along[k],
            )
        )
    for slot in range(2):
        swap_piece(slot, depth, 0).start()
    for k in range(2):
        halo[3 + k].wait_recv()
        halo.append(
            send(
                ring.at[k, :, :, near_mate], ring.at[k, :, :, past_cross],
                halo_sems, 8 + k, mate,
            )
        )
    halo[5].wait_recv()
    halo[2].wait_recv()
    for slot in range(2):
        for part in range(2):
            extract_front(slot, part)
        swap_piece(slot, depth, 1).start()
    for copy in halo[6:]:
        copy.wait_recv()
    for k in range(2):
        for part in range(2):
            pad[part, outer_rows[k]] = ring[k, part]

    def propagate(slot):
        obj_real, obj_imag = patch_of(0, slot)
        wave_real, wave_imag = transform3(
            probe_real * obj_real - probe_imag * obj_imag,
            probe_real * obj_imag + probe_imag * obj_real,
            2, True,
        )
        wave[slot, 0] = wave_real.astype(BF16)
        wave[slot, 1] = wave_imag.astype(BF16)

    for slot in range(2):
        for part in range(2):
            extract_back(slot, part)
            swap_piece(slot, depth, 2 + part).start()

    @pl.when(depth == 0)
    def _():
        for slot in range(2):
            propagate(slot)

    for slot in range(2):
        for piece in range(4):
            swap_piece(slot, 1 - depth, piece).wait_recv()

        @pl.when(depth == 1)
        def _():
            propagate(slot)

        wave_real, wave_imag = wave[slot, 0].astype(F32), wave[slot, 1].astype(F32)
        obj_real, obj_imag = patch_of(1, slot)
        far_real, far_imag = transform3(
            wave_real * obj_real - wave_imag * obj_imag,
            wave_real * obj_imag + wave_imag * obj_real,
            0, False,
        )
        power = far_real * far_real + far_imag * far_imag
        weight = live[0, 0, slot].astype(F32)
        factor = weight * (
            1.0 - turned_amp[slot].astype(F32) * lax.rsqrt(jnp.maximum(power, 0.0625))
        )
        back_real, back_imag = conjugate1(far_real * factor, far_imag * factor, 0, False)
        back_real = back_real.astype(BF16).astype(F32)
        back_imag = back_imag.astype(BF16).astype(F32)

        @pl.when(depth == 1)
        def _():
            grads[slot, 0] = (wave_real * back_real + wave_imag * back_imag).astype(BF16)
            grads[slot, 1] = (wave_real * back_imag - wave_imag * back_real).astype(BF16)

        @pl.when(depth == 0)
        def _():
            first_real, first_imag = conjugate1(
                obj_real * back_real + obj_imag * back_imag,
                obj_real * back_imag - obj_imag * back_real,
                2, True,
            )
            first_real = first_real.astype(BF16).astype(F32)
            first_imag = first_imag.astype(BF16).astype(F32)
            grads[slot, 0] = (probe_real * first_real + probe_imag * first_imag).astype(BF16)
            grads[slot, 1] = (probe_real * first_imag - probe_imag * first_real).astype(BF16)

        if slot == 0:
            cells = dot(grads[0].reshape(2 * patch, patch), put_cols[0]).astype(BF16)
            for part in range(2):
                spread[part, 0:patch] = cells[part * patch:(part + 1) * patch]

    outer_cols = jnp.concatenate((put_cols[1, :, 0:rim], put_cols[1, :, rim + tile:]), axis=1)
    outer_ends = jnp.concatenate((put_rows[0:rim], put_rows[rim + tile:]), axis=0)
    last_grads = grads[1].reshape(2 * patch, patch)
    cells = dot(last_grads, outer_cols).astype(BF16)
    for part in range(2):
        spread[part, patch:, 0:rim] = cells[part * patch:(part + 1) * patch, 0:rim]
        spread[part, patch:, rim + tile:] = cells[part * patch:(part + 1) * patch, rim:]
    sides = [(part, place) for place in (past_cross, past_mate) for part in range(2)]
    lanes = jnp.concatenate([spread[part, :, place] for part, place in sides], axis=1)
    cells = dot(outer_ends, lanes).astype(BF16)
    for index, (part, place) in enumerate(sides):
        gpad[part, 0:rim, place] = cells[0:rim, index * rim:(index + 1) * rim]
        gpad[part, rim + tile:, place] = cells[rim:, index * rim:(index + 1) * rim]
    rim_sems = (rim_send, rim_recv)
    edge_rows = (pl.ds(0, rim), pl.ds(rim + tile, rim))
    rims = [
        send(gpad.at[:, edge_rows[k], past_cross], got_c.at[0, k], rim_sems, k, along[k])
        for k in range(2)
    ]
    rims += [
        send(gpad.at[:, edge_rows[k], past_mate], got_c.at[1, k], rim_sems, 2 + k, mate)
        for k in range(2)
    ]
    cells = dot(put_rows[rim:rim + tile], lanes).astype(BF16)
    for index, (part, place) in enumerate(sides):
        gpad[part, middle, place] = cells[:, index * rim:(index + 1) * rim]
    rims.append(
        send(
            gpad.at[:, pl.ds(2 * rim, tile - 2 * rim), past_cross],
            got_x.at[odd, :, pl.ds(rim, tile - 2 * rim)], rim_sems, 4, cross,
        )
    )
    rims.append(send(gpad.at[:, middle, past_mate], got_x.at[1 - odd], rim_sems, 5, mate))

    cells = dot(last_grads, put_cols[1, :, rim:rim + tile]).astype(BF16)
    for part in range(2):
        spread[part, patch:, rim:rim + tile] = cells[part * patch:(part + 1) * patch]
    lanes = jnp.concatenate([spread[part, :, rim:rim + tile] for part in range(2)], axis=1)
    cells = dot(outer_ends, lanes).astype(BF16)
    for part in range(2):
        gpad[part, 0:rim, rim:rim + tile] = cells[0:rim, part * tile:(part + 1) * tile]
        gpad[part, rim + tile:, rim:rim + tile] = cells[rim:, part * tile:(part + 1) * tile]
    rims += [
        send(
            gpad.at[:, edge_rows[k], pl.ds(rim * (1 + odd), tile - rim)],
            got_y.at[k, :, :, pl.ds(rim * odd, tile - rim)], rim_sems, 6 + k, along[k],
        )
        for k in range(2)
    ]
    for k in range(2):
        rims[2 + k].wait_recv()
        for part in range(2):
            total = gpad[part, edge_rows[k], near_mate].astype(F32) + got_c[1, k, part].astype(F32)
            gpad[part, edge_rows[k], near_mate] = total.astype(BF16)
        rims.append(
            send(
                gpad.at[:, edge_rows[k], near_mate], got_y.at[k, :, :, edge_mate],
                rim_sems, 8 + k, along[k],
            )
        )

    for part in range(2):
        out[0, part] = dot(put_rows[rim:rim + tile], spread[part, :, rim:rim + tile])

    tile_rows = (pl.ds(tile - rim, rim), pl.ds(0, rim))
    for k in range(2):
        rims[k].wait_recv()
        rows = inner_rows[1 - k]
        for part in range(2):
            total = gpad[part, rows, past_cross].astype(F32) + got_c[0, k, part].astype(F32)
            gpad[part, rows, past_cross] = total.astype(BF16)
        rims.append(
            send(
                gpad.at[:, rows, past_cross], got_x.at[odd, :, tile_rows[k]],
                rim_sems, 10 + k, cross,
            )
        )
    for copy in rims[4:10]:
        copy.wait_recv()
    core = pl.ds(rim, tile - 2 * rim)
    for part in range(2):
        out[0, part, :, edge_mate] += got_x[odd, part].astype(F32)
        out[0, part, core, edge_cross] += got_x[1 - odd, part, core].astype(F32)
        for k in range(2):
            out[0, part, tile_rows[k]] += got_y[k, part].astype(F32)
    for k in range(2):
        rims[10 + k].wait_recv()
        for part in range(2):
            out[0, part, tile_rows[k], edge_cross] += got_x[1 - odd, part, tile_rows[k]].astype(F32)

    for copy in halo:
        copy.wait_send()
    for slot in range(2):
        for piece in range(4):
            swap_piece(slot, depth, piece).wait_send()
    for copy in rims:
        copy.wait_send()


def on_device(object_field, probe, amplitude, positions, live):
    tile = object_field.shape[2]
    patch = probe.shape[1]
    rim = patch // 2
    full = tile + patch
    left, right = tables(patch)
    vmem = pl.BlockSpec(memory_space=pltpu.VMEM)
    smem = pl.BlockSpec(memory_space=pltpu.SMEM)
    hbm = pl.BlockSpec(memory_space=pl.ANY)
    dma = pltpu.SemaphoreType.DMA
    gradient = pl.pallas_call(
        functools.partial(
            kernel, tile, patch, lax.axis_size("row"), lax.axis_size("col")
        ),
        out_shape=pltpu.VMEM(object_field.shape, F32),
        in_specs=[smem, smem, hbm, hbm, hbm, hbm, hbm],
        out_specs=vmem,
        scratch_shapes=[
            pltpu.VMEM((2, tile, rim), F32),
            pltpu.VMEM((2, tile, tile), F32),
            pltpu.VMEM((2, patch, patch), BF16),
            pltpu.VMEM((2, patch, patch), BF16),
            pltpu.VMEM((2, patch, patch), BF16),
            pltpu.VMEM((2, full, full), jnp.int16),
            pltpu.VMEM((2, 2, rim, full), jnp.int16),
            pltpu.VMEM((2, 2, 2, patch, patch), jnp.int16),
            pltpu.VMEM((2, 2, patch, patch), BF16),
            pltpu.VMEM((2, 2, patch, patch), BF16),
            pltpu.VMEM((2, full, full), BF16),
            pltpu.VMEM((2, 2, tile, rim), BF16),
            pltpu.VMEM((2, 2, rim, tile), BF16),
            pltpu.VMEM((2, 2, 2, rim, rim), BF16),
            pltpu.VMEM(left.shape, BF16),
            pltpu.VMEM(right.shape, BF16),
            pltpu.VMEM((2, rim, patch + rim), BF16),
            pltpu.VMEM((2, patch + rim, patch), BF16),
            pltpu.VMEM((full, 2 * patch), BF16),
            pltpu.VMEM((2, patch, full), BF16),
            pltpu.VMEM((2, rim, patch), BF16),
            pltpu.VMEM((2, patch, rim), BF16),
            pltpu.VMEM((2, 2 * patch, full), BF16),
            dma((7,)), dma((10,)), dma((10,)), dma((8,)), dma((8,)), dma((12,)), dma((12,)),
        ],
        compiler_params=pltpu.CompilerParams(
            collective_id=0, has_side_effects=True, vmem_limit_bytes=56 * 1024 * 1024
        ),
    )(positions, live, object_field, probe, amplitude, jnp.asarray(left), jnp.asarray(right))
    return gradient


def solution(mesh):
    in_specs = (
        P("depth", None, "row", "col"),
        P(),
        P("row", "col", None, None, None),
        P("row", "col", None, None),
        P("row", "col", None),
    )
    out_specs = P("depth", None, "row", "col")
    return jax.shard_map(
        on_device, mesh=mesh, in_specs=in_specs, out_specs=out_specs, check_vma=False
    )
```

```python
import functools
import math

import jax
import jax.numpy as jnp
import ml_dtypes
import numpy as np
from jax import lax
from jax.experimental import pallas as pl
from jax.experimental.pallas import tpu as pltpu
from jax.sharding import PartitionSpec as P

MESH = pl.DeviceIdType.MESH
SCALE = 16384.0
F32 = jnp.float32
BF16 = jnp.bfloat16


def split(values):
    high = values.astype(ml_dtypes.bfloat16)
    low = (values - high.astype(np.float64)).astype(ml_dtypes.bfloat16)
    return high, low


def tables(size):
    steps = np.arange(size)
    angles = 2.0 * math.pi * ((steps[:, None] * steps[None, :]) % size) / size
    fourier = np.exp(-1j * angles) / math.sqrt(size)
    frequency = (steps + size // 2) % size - size // 2
    chirp = np.exp(-1j * math.pi * frequency.astype(np.float64) ** 2 / (2.0 * size))
    spread = fourier.conj() @ (chirp[:, None] * fourier)
    half = size // 2
    same, swapped = spread[:half, :half], spread[:half, half:]
    left, right = [], []
    for table in (fourier[0::2, :half], fourier[1::2, :half], (same + swapped) / 2, (same - swapped) / 2):
        whole = np.block([[table.real, -table.imag], [table.imag, table.real]])
        high, low = split(whole)
        left.append(np.concatenate((high, low, high), axis=1))
        right.append(np.concatenate((high.T, low.T, high.T), axis=0))
    return np.stack(left), np.stack(right)


def dot(left, right):
    return jnp.dot(left, right, preferred_element_type=F32)


def halves(values):
    high = values.astype(BF16)
    return high, (values - high.astype(F32)).astype(BF16)


def kernel(
    tile, patch, n_row, n_col,
    pos, live, obj_hbm, probe_hbm, amp_hbm, left_hbm, right_hbm, out,
    edge, obj, probe, amp, turned_amp, pad, ring, win, wave, grads, gpad, got_x, got_y, got_c,
    left3, right3, pick_rows, pick_cols, put_rows, put_cols, quad_rows, quad_cols, spread,
    in_sem, halo_send, halo_recv, swap_send, swap_recv, rim_send, rim_recv,
):
    rim = patch // 2
    full = tile + patch
    span = patch + rim
    depth, row, col = lax.axis_index("depth"), lax.axis_index("row"), lax.axis_index("col")
    partner = (1 - depth, row, col)

    odd = lax.rem(col, 2)
    away = 2 * odd - 1
    mate = (depth, row, col - away)
    cross = (depth, row, lax.rem(col + away + n_col, n_col))
    along = [(depth, lax.rem(row + step + n_row, n_row), col) for step in (-1, 1)]

    def send(source, target, sems, index, device):
        copy = pltpu.make_async_remote_copy(
            src_ref=source, dst_ref=target, send_sem=sems[0].at[index],
            recv_sem=sems[1].at[index], device_id=device, device_id_type=MESH,
        )
        copy.start()
        return copy

    barrier = pltpu.get_barrier_semaphore()
    for device in (mate, cross, *along, partner):
        pl.semaphore_signal(barrier, inc=1, device_id=device, device_id_type=MESH)
    last = tile // rim
    near_mate, near_cross = pl.ds(rim * (last - (last - 1) * odd), rim), pl.ds(rim * (1 + (last - 1) * odd), rim)
    past_mate, past_cross = pl.ds(rim * ((last + 1) * (1 - odd)), rim), pl.ds(rim * ((last + 1) * odd), rim)
    middle = pl.ds(rim, tile)
    inner_rows = (pl.ds(rim, rim), pl.ds(tile, rim))
    outer_rows = (pl.ds(rim + tile, rim), pl.ds(0, rim))
    halo_sems = (halo_send, halo_recv)
    edge_cross, edge_mate = pl.ds(rim * (last - 1) * odd, rim), pl.ds(rim * (last - 1) * (1 - odd), rim)
    loads = [
        pltpu.make_async_copy(source, target, in_sem.at[index])
        for index, (source, target) in enumerate((
            (obj_hbm.at[0, 0], obj.at[0]), (obj_hbm.at[0, 1], obj.at[1]),
            (left_hbm, left3), (probe_hbm, probe), (amp_hbm.at[0, 0], amp),
            (obj_hbm.at[0, :, :, edge_cross], edge), (right_hbm, right3),
        ))
    ]
    for load in (loads[5], loads[0], loads[1]):
        load.start()

    def fixed_point(values):
        return jnp.round(values * SCALE).astype(jnp.int32).astype(jnp.int16)

    loads[5].wait()
    for part in range(2):
        pad[part, middle, near_cross] = fixed_point(edge[part])
    pl.semaphore_wait(barrier, 5)
    halo = [
        send(pad.at[:, rows, near_cross], pad.at[:, rows, past_mate], halo_sems, index, cross)
        for index, rows in enumerate((*inner_rows, pl.ds(2 * rim, tile - 2 * rim)))
    ]
    for load in (*loads[2:5], loads[6]):
        load.start()
    for part in range(2):
        loads[part].wait()
        pad[part, middle, 2 * rim:tile] = fixed_point(obj[part, :, rim:tile - rim])
        pad[part, middle, near_mate] = fixed_point(obj[part, :, edge_mate])
    halo += [
        send(pad.at[:, inner_rows[k], middle], ring.at[k, :, :, middle], halo_sems, 3 + k, along[k])
        for k in range(2)
    ]
    halo.append(send(pad.at[:, middle, near_mate], pad.at[:, middle, past_cross], halo_sems, 5, mate))

    def halved(values, axis):
        if axis == 0:
            return values[0:rim], values[rim:]
        return values[:, 0:rim], values[:, rim:]

    def stacked(real, imag, axis, mix):
        (real0, real1), (imag0, imag1) = halved(real, axis), halved(imag, axis)
        if mix:
            real0, real1 = real0 + real1, real0 - real1
            imag0, imag1 = imag0 + imag1, imag0 - imag1
        return [jnp.concatenate(pair, axis=axis) for pair in ((real0, imag0), (real1, imag1))]

    def unstacked(first, second, axis, mix):
        (real0, imag0), (real1, imag1) = halved(first, axis), halved(second, axis)
        if mix:
            real0, real1 = real0 + real1, real0 - real1
            imag0, imag1 = imag0 + imag1, imag0 - imag1
        return [jnp.concatenate(pair, axis=axis) for pair in ((real0, real1), (imag0, imag1))]

    def transform3(real, imag, base, mix_after):
        for axis in range(2):
            sides = []
            for place, values in enumerate(stacked(real, imag, axis, True)):
                high, low = halves(values)
                values = jnp.concatenate((high, high, low), axis=axis)
                if axis == 0:
                    sides.append(dot(left3[base + place], values))
                else:
                    sides.append(dot(values, right3[base + place]))
            real, imag = unstacked(*sides, axis, mix_after)
        return real, imag

    def conjugate1(real, imag, base, mix_before):
        for axis in range(2):
            sides = []
            for place, values in enumerate(stacked(real, imag, axis, mix_before)):
                values = values.astype(BF16)
                if axis == 0:
                    sides.append(dot(right3[base + place, 0:patch], values))
                else:
                    sides.append(dot(values, left3[base + place, :, 0:patch]))
            real, imag = unstacked(*sides, axis, True)
        return real, imag

    def one_hot(shape, axis, shift, turn=None):
        index = lax.broadcasted_iota(jnp.int32, shape, 1 - axis)
        if turn is not None:
            index = index + turn
            index = jnp.where(index >= patch, index - patch, index)
        hit = lax.broadcasted_iota(jnp.int32, shape, axis) == index + shift
        return hit.astype(F32).astype(BF16)

    blocks, quads, turned = [], [], []
    for slot in range(2):
        corner = [pos[0, 0, slot, axis] for axis in range(2)]
        turned.append([start < patch for start in corner])
        turns = [jnp.where(flag, rim, 0) for flag in turned[slot]]
        block = [jnp.minimum(start >> 7, (full - span) // 128) for start in corner]
        blocks.append(block)
        pick_rows[slot] = one_hot((rim, span), 1, corner[0] - block[0] * 128, turns[0] + rim)
        pick_cols[slot] = one_hot((span, patch), 0, corner[1] - block[1] * 128, turns[1])
        put_rows[:, slot * patch:(slot + 1) * patch] = one_hot((full, patch), 0, corner[0])
        put_cols[slot] = one_hot((patch, full), 1, corner[1])
        first = [start - rim + turn for start, turn in zip(corner, turns)]
        quad = [jnp.minimum(start >> 7, (tile - patch) // 128) for start in first]
        quads.append(quad)
        quad_rows[slot] = one_hot((rim, patch), 1, first[0] - quad[0] * 128)
        quad_cols[slot] = one_hot((patch, rim), 0, first[1] - quad[1] * 128)

    def select(codes, rows, cols):
        width = codes.shape[1]
        high, low = halves(codes)
        picked = dot(rows, jnp.concatenate((high, low), axis=1)).astype(BF16)
        cells = dot(picked[:, :width], cols) + dot(picked[:, width:], cols)
        return cells.astype(jnp.int32).astype(jnp.int16)

    for slot in range(2):
        for part in range(2):
            block = obj[part, pl.ds(quads[slot][0] * 128, patch), pl.ds(quads[slot][1] * 128, patch)]
            win[depth, slot, part, 0:rim, 0:rim] = select(
                jnp.round(block * SCALE), quad_rows[slot], quad_cols[slot]
            )

    def extract_front(slot, part):
        block = pad[
            part, pl.ds((quads[slot][0] + 1) * 128, patch), pl.ds(blocks[slot][1] * 128, span)
        ]
        cells = select(block.astype(F32), quad_rows[slot], pick_cols[slot, :, rim:])
        win[depth, slot, part, 0:rim, rim:] = cells

    def extract_back(slot, part):
        block = pad[
            part, pl.ds(blocks[slot][0] * 128, span), pl.ds(blocks[slot][1] * 128, span)
        ]
        win[depth, slot, part, rim:] = select(block.astype(F32), pick_rows[slot], pick_cols[slot])

    def swap(buffer, index):
        return pltpu.make_async_remote_copy(
            src_ref=buffer, dst_ref=buffer,
            send_sem=swap_send.at[index], recv_sem=swap_recv.at[index],
            device_id=partner, device_id_type=MESH,
        )

    def patch_of(section, slot):
        parts = []
        for part in range(2):
            codes = win[section, slot, part].astype(F32) * (1.0 / SCALE)
            for axis in range(2):
                front, back = (codes[0:rim], codes[rim:]) if axis == 0 else (codes[:, 0:rim], codes[:, rim:])
                flag = turned[slot][axis]
                codes = jnp.concatenate(
                    (jnp.where(flag, back, front), jnp.where(flag, front, back)), axis=axis
                )
            parts.append(codes)
        return parts

    def swap_piece(slot, section, piece):
        source = win.at[section, slot]
        if piece < 2:
            source = source.at[:, 0:rim, piece * rim:(piece + 1) * rim]
        else:
            source = source.at[pl.ds(piece - 2, 1), rim:patch]
        return swap(source, 4 * slot + piece)

    loads[2].wait()
    loads[3].wait()
    loads[4].wait()
    loads[6].wait()
    place = lax.broadcasted_iota(jnp.int32, (patch, patch), 0)
    order = (
        lax.broadcasted_iota(jnp.int32, (patch, patch), 1)
        == 2 * place - jnp.where(place >= rim, patch - 1, 0)
    ).astype(F32).astype(BF16)
    for slot in range(2):
        rows = dot(order, amp[slot]).astype(BF16)
        turned_amp[slot] = lax.dot_general(
            rows, order, (((1,), (1,)), ((), ())), preferred_element_type=F32
        ).astype(BF16)
    probe_real, probe_imag = probe[0].astype(F32), probe[1].astype(F32)
    for k in range(2):
        halo[k].wait_recv()
        halo.append(
            send(
                pad.at[:, inner_rows[k], past_cross], ring.at[k, :, :, past_cross],
                halo_sems, 6 + k, along[k],
            )
        )
    for slot in range(2):
        swap_piece(slot, depth, 0).start()
    for k in range(2):
        halo[3 + k].wait_recv()
        halo.append(
            send(
                ring.at[k, :, :, near_mate], ring.at[k, :, :, past_cross],
                halo_sems, 8 + k, mate,
            )
        )
    halo[5].wait_recv()
    halo[2].wait_recv()
    for slot in range(2):
        for part in range(2):
            extract_front(slot, part)
        swap_piece(slot, depth, 1).start()
    for copy in halo[6:]:
        copy.wait_recv()
    for k in range(2):
        for part in range(2):
            pad[part, outer_rows[k]] = ring[k, part]

    def propagate(slot):
        obj_real, obj_imag = patch_of(0, slot)
        wave_real, wave_imag = transform3(
            probe_real * obj_real - probe_imag * obj_imag,
            probe_real * obj_imag + probe_imag * obj_real,
            2, True,
        )
        wave[slot, 0] = wave_real.astype(BF16)
        wave[slot, 1] = wave_imag.astype(BF16)

    for slot in range(2):
        for part in range(2):
            extract_back(slot, part)
            swap_piece(slot, depth, 2 + part).start()

    @pl.when(depth == 0)
    def _():
        for slot in range(2):
            propagate(slot)

    for slot in range(2):
        for piece in range(4):
            swap_piece(slot, 1 - depth, piece).wait_recv()

        @pl.when(depth == 1)
        def _():
            propagate(slot)

        wave_real, wave_imag = wave[slot, 0].astype(F32), wave[slot, 1].astype(F32)
        obj_real, obj_imag = patch_of(1, slot)
        far_real, far_imag = transform3(
            wave_real * obj_real - wave_imag * obj_imag,
            wave_real * obj_imag + wave_imag * obj_real,
            0, False,
        )
        power = far_real * far_real + far_imag * far_imag
        weight = live[0, 0, slot].astype(F32)
        factor = weight * (
            1.0 - turned_amp[slot].astype(F32) * lax.rsqrt(jnp.maximum(power, 0.0625))
        )
        back_real, back_imag = conjugate1(far_real * factor, far_imag * factor, 0, False)
        back_real = back_real.astype(BF16).astype(F32)
        back_imag = back_imag.astype(BF16).astype(F32)

        @pl.when(depth == 1)
        def _():
            grads[slot, 0] = (wave_real * back_real + wave_imag * back_imag).astype(BF16)
            grads[slot, 1] = (wave_real * back_imag - wave_imag * back_real).astype(BF16)

        @pl.when(depth == 0)
        def _():
            first_real, first_imag = conjugate1(
                obj_real * back_real + obj_imag * back_imag,
                obj_real * back_imag - obj_imag * back_real,
                2, True,
            )
            first_real = first_real.astype(BF16).astype(F32)
            first_imag = first_imag.astype(BF16).astype(F32)
            grads[slot, 0] = (probe_real * first_real + probe_imag * first_imag).astype(BF16)
            grads[slot, 1] = (probe_real * first_imag - probe_imag * first_real).astype(BF16)

        if slot == 0:
            cells = dot(grads[0].reshape(2 * patch, patch), put_cols[0]).astype(BF16)
            for part in range(2):
                spread[part, 0:patch] = cells[part * patch:(part + 1) * patch]

    outer_cols = jnp.concatenate((put_cols[1, :, 0:rim], put_cols[1, :, rim + tile:]), axis=1)
    outer_ends = jnp.concatenate((put_rows[0:rim], put_rows[rim + tile:]), axis=0)
    last_grads = grads[1].reshape(2 * patch, patch)
    cells = dot(last_grads, outer_cols).astype(BF16)
    for part in range(2):
        spread[part, patch:, 0:rim] = cells[part * patch:(part + 1) * patch, 0:rim]
        spread[part, patch:, rim + tile:] = cells[part * patch:(part + 1) * patch, rim:]
    sides = [(part, place) for place in (past_cross, past_mate) for part in range(2)]
    lanes = jnp.concatenate([spread[part, :, place] for part, place in sides], axis=1)
    cells = dot(outer_ends, lanes).astype(BF16)
    for index, (part, place) in enumerate(sides):
        gpad[part, 0:rim, place] = cells[0:rim, index * rim:(index + 1) * rim]
        gpad[part, rim + tile:, place] = cells[rim:, index * rim:(index + 1) * rim]
    rim_sems = (rim_send, rim_recv)
    edge_rows = (pl.ds(0, rim), pl.ds(rim + tile, rim))
    rims = [
        send(gpad.at[:, edge_rows[k], past_cross], got_c.at[0, k], rim_sems, k, along[k])
        for k in range(2)
    ]
    rims += [
        send(gpad.at[:, edge_rows[k], past_mate], got_c.at[1, k], rim_sems, 2 + k, mate)
        for k in range(2)
    ]
    cells = dot(put_rows[rim:rim + tile], lanes).astype(BF16)
    for index, (part, place) in enumerate(sides):
        gpad[part, middle, place] = cells[:, index * rim:(index + 1) * rim]
    rims.append(
        send(
            gpad.at[:, pl.ds(2 * rim, tile - 2 * rim), past_cross],
            got_x.at[odd, :, pl.ds(rim, tile - 2 * rim)], rim_sems, 4, cross,
        )
    )
    rims.append(send(gpad.at[:, middle, past_mate], got_x.at[1 - odd], rim_sems, 5, mate))

    cells = dot(last_grads, put_cols[1, :, rim:rim + tile]).astype(BF16)
    for part in range(2):
        spread[part, patch:, rim:rim + tile] = cells[part * patch:(part + 1) * patch]
    lanes = jnp.concatenate([spread[part, :, rim:rim + tile] for part in range(2)], axis=1)
    cells = dot(outer_ends, lanes).astype(BF16)
    for part in range(2):
        gpad[part, 0:rim, rim:rim + tile] = cells[0:rim, part * tile:(part + 1) * tile]
        gpad[part, rim + tile:, rim:rim + tile] = cells[rim:, part * tile:(part + 1) * tile]
    rims += [
        send(
            gpad.at[:, edge_rows[k], pl.ds(rim * (1 + odd), tile - rim)],
            got_y.at[k, :, :, pl.ds(rim * odd, tile - rim)], rim_sems, 6 + k, along[k],
        )
        for k in range(2)
    ]
    for k in range(2):
        rims[2 + k].wait_recv()
        for part in range(2):
            total = gpad[part, edge_rows[k], near_mate].astype(F32) + got_c[1, k, part].astype(F32)
            gpad[part, edge_rows[k], near_mate] = total.astype(BF16)
        rims.append(
            send(
                gpad.at[:, edge_rows[k], near_mate], got_y.at[k, :, :, edge_mate],
                rim_sems, 8 + k, along[k],
            )
        )

    tile_rows = (pl.ds(tile - rim, rim), pl.ds(0, rim))
    for k in range(2):
        rims[k].wait_recv()
        rows = inner_rows[1 - k]
        for part in range(2):
            total = gpad[part, rows, past_cross].astype(F32) + got_c[0, k, part].astype(F32)
            gpad[part, rows, past_cross] = total.astype(BF16)
        rims.append(
            send(
                gpad.at[:, rows, past_cross], got_x.at[odd, :, tile_rows[k]],
                rim_sems, 10 + k, cross,
            )
        )
    for part in range(2):
        out[0, part] = dot(put_rows[rim:rim + tile], spread[part, :, rim:rim + tile])

    for copy in rims[4:10]:
        copy.wait_recv()
    core = pl.ds(rim, tile - 2 * rim)
    for part in range(2):
        out[0, part, :, edge_mate] += got_x[odd, part].astype(F32)
        out[0, part, core, edge_cross] += got_x[1 - odd, part, core].astype(F32)
        for k in range(2):
            out[0, part, tile_rows[k]] += got_y[k, part].astype(F32)
    for k in range(2):
        rims[10 + k].wait_recv()
        for part in range(2):
            out[0, part, tile_rows[k], edge_cross] += got_x[1 - odd, part, tile_rows[k]].astype(F32)

    for copy in halo:
        copy.wait_send()
    for slot in range(2):
        for piece in range(4):
            swap_piece(slot, depth, piece).wait_send()
    for copy in rims:
        copy.wait_send()


def on_device(object_field, probe, amplitude, positions, live):
    tile = object_field.shape[2]
    patch = probe.shape[1]
    rim = patch // 2
    full = tile + patch
    left, right = tables(patch)
    vmem = pl.BlockSpec(memory_space=pltpu.VMEM)
    smem = pl.BlockSpec(memory_space=pltpu.SMEM)
    hbm = pl.BlockSpec(memory_space=pl.ANY)
    dma = pltpu.SemaphoreType.DMA
    gradient = pl.pallas_call(
        functools.partial(
            kernel, tile, patch, lax.axis_size("row"), lax.axis_size("col")
        ),
        out_shape=pltpu.VMEM(object_field.shape, F32),
        in_specs=[smem, smem, hbm, hbm, hbm, hbm, hbm],
        out_specs=vmem,
        scratch_shapes=[
            pltpu.VMEM((2, tile, rim), F32),
            pltpu.VMEM((2, tile, tile), F32),
            pltpu.VMEM((2, patch, patch), BF16),
            pltpu.VMEM((2, patch, patch), BF16),
            pltpu.VMEM((2, patch, patch), BF16),
            pltpu.VMEM((2, full, full), jnp.int16),
            pltpu.VMEM((2, 2, rim, full), jnp.int16),
            pltpu.VMEM((2, 2, 2, patch, patch), jnp.int16),
            pltpu.VMEM((2, 2, patch, patch), BF16),
            pltpu.VMEM((2, 2, patch, patch), BF16),
            pltpu.VMEM((2, full, full), BF16),
            pltpu.VMEM((2, 2, tile, rim), BF16),
            pltpu.VMEM((2, 2, rim, tile), BF16),
            pltpu.VMEM((2, 2, 2, rim, rim), BF16),
            pltpu.VMEM(left.shape, BF16),
            pltpu.VMEM(right.shape, BF16),
            pltpu.VMEM((2, rim, patch + rim), BF16),
            pltpu.VMEM((2, patch + rim, patch), BF16),
            pltpu.VMEM((full, 2 * patch), BF16),
            pltpu.VMEM((2, patch, full), BF16),
            pltpu.VMEM((2, rim, patch), BF16),
            pltpu.VMEM((2, patch, rim), BF16),
            pltpu.VMEM((2, 2 * patch, full), BF16),
            dma((7,)), dma((10,)), dma((10,)), dma((8,)), dma((8,)), dma((12,)), dma((12,)),
        ],
        compiler_params=pltpu.CompilerParams(
            collective_id=0, has_side_effects=True, vmem_limit_bytes=56 * 1024 * 1024
        ),
    )(positions, live, object_field, probe, amplitude, jnp.asarray(left), jnp.asarray(right))
    return gradient


def solution(mesh):
    in_specs = (
        P("depth", None, "row", "col"),
        P(),
        P("row", "col", None, None, None),
        P("row", "col", None, None),
        P("row", "col", None),
    )
    out_specs = P("depth", None, "row", "col")
    return jax.shard_map(
        on_device, mesh=mesh, in_specs=in_specs, out_specs=out_specs, check_vma=False
    )
```

```python
import functools
import math

import jax
import jax.numpy as jnp
import ml_dtypes
import numpy as np
from jax import lax
from jax.experimental import pallas as pl
from jax.experimental.pallas import tpu as pltpu
from jax.sharding import PartitionSpec as P

MESH = pl.DeviceIdType.MESH
SCALE = 16384.0
F32 = jnp.float32
BF16 = jnp.bfloat16


def split(values):
    high = values.astype(ml_dtypes.bfloat16)
    low = (values - high.astype(np.float64)).astype(ml_dtypes.bfloat16)
    return high, low


def tables(size):
    steps = np.arange(size)
    angles = 2.0 * math.pi * ((steps[:, None] * steps[None, :]) % size) / size
    fourier = np.exp(-1j * angles) / math.sqrt(size)
    frequency = (steps + size // 2) % size - size // 2
    chirp = np.exp(-1j * math.pi * frequency.astype(np.float64) ** 2 / (2.0 * size))
    spread = fourier.conj() @ (chirp[:, None] * fourier)
    half = size // 2
    same, swapped = spread[:half, :half], spread[:half, half:]
    left, right = [], []
    for table in (fourier[0::2, :half], fourier[1::2, :half], (same + swapped) / 2, (same - swapped) / 2):
        whole = np.block([[table.real, -table.imag], [table.imag, table.real]])
        high, low = split(whole)
        left.append(np.concatenate((high, low, high), axis=1))
        right.append(np.concatenate((high.T, low.T, high.T), axis=0))
    return np.stack(left), np.stack(right)


def dot(left, right):
    return jnp.dot(left, right, preferred_element_type=F32)


def halves(values):
    high = values.astype(BF16)
    return high, (values - high.astype(F32)).astype(BF16)


def kernel(
    tile, patch, n_row, n_col,
    pos, live, obj_hbm, probe_hbm, amp_hbm, left_hbm, right_hbm, out,
    edge, obj, probe, amp, turned_amp, pad, ring, win, wave, grads, gpad, got_x, got_y, got_c,
    left3, right3, pick_rows, pick_cols, put_rows, put_cols, quad_rows, quad_cols, spread,
    in_sem, halo_send, halo_recv, swap_send, swap_recv, rim_send, rim_recv,
):
    rim = patch // 2
    full = tile + patch
    span = patch + rim
    depth, row, col = lax.axis_index("depth"), lax.axis_index("row"), lax.axis_index("col")
    partner = (1 - depth, row, col)

    odd = lax.rem(col, 2)
    away = 2 * odd - 1
    mate = (depth, row, col - away)
    cross = (depth, row, lax.rem(col + away + n_col, n_col))
    along = [(depth, lax.rem(row + step + n_row, n_row), col) for step in (-1, 1)]

    def send(source, target, sems, index, device):
        copy = pltpu.make_async_remote_copy(
            src_ref=source, dst_ref=target, send_sem=sems[0].at[index],
            recv_sem=sems[1].at[index], device_id=device, device_id_type=MESH,
        )
        copy.start()
        return copy

    barrier = pltpu.get_barrier_semaphore()
    for device in (mate, cross, *along, partner):
        pl.semaphore_signal(barrier, inc=1, device_id=device, device_id_type=MESH)
    last = tile // rim
    near_mate, near_cross = pl.ds(rim * (last - (last - 1) * odd), rim), pl.ds(rim * (1 + (last - 1) * odd), rim)
    past_mate, past_cross = pl.ds(rim * ((last + 1) * (1 - odd)), rim), pl.ds(rim * ((last + 1) * odd), rim)
    middle = pl.ds(rim, tile)
    inner_rows = (pl.ds(rim, rim), pl.ds(tile, rim))
    outer_rows = (pl.ds(rim + tile, rim), pl.ds(0, rim))
    halo_sems = (halo_send, halo_recv)
    edge_cross, edge_mate = pl.ds(rim * (last - 1) * odd, rim), pl.ds(rim * (last - 1) * (1 - odd), rim)
    loads = [
        pltpu.make_async_copy(source, target, in_sem.at[index])
        for index, (source, target) in enumerate((
            (obj_hbm.at[0, 0], obj.at[0]), (obj_hbm.at[0, 1], obj.at[1]),
            (left_hbm, left3), (probe_hbm, probe), (amp_hbm.at[0, 0], amp),
            (obj_hbm.at[0, :, :, edge_cross], edge), (right_hbm, right3),
        ))
    ]
    for load in (loads[5], loads[0], loads[1]):
        load.start()

    def fixed_point(values):
        return jnp.round(values * SCALE).astype(jnp.int32).astype(jnp.int16)

    loads[5].wait()
    for part in range(2):
        pad[part, middle, near_cross] = fixed_point(edge[part])
    pl.semaphore_wait(barrier, 5)
    halo = [
        send(pad.at[:, rows, near_cross], pad.at[:, rows, past_mate], halo_sems, index, cross)
        for index, rows in enumerate((*inner_rows, pl.ds(2 * rim, tile - 2 * rim)))
    ]
    for load in (*loads[2:5], loads[6]):
        load.start()
    for part in range(2):
        loads[part].wait()
        pad[part, middle, 2 * rim:tile] = fixed_point(obj[part, :, rim:tile - rim])
        pad[part, middle, near_mate] = fixed_point(obj[part, :, edge_mate])
    halo += [
        send(pad.at[:, inner_rows[k], middle], ring.at[k, :, :, middle], halo_sems, 3 + k, along[k])
        for k in range(2)
    ]
    halo.append(send(pad.at[:, middle, near_mate], pad.at[:, middle, past_cross], halo_sems, 5, mate))

    def halved(values, axis):
        if axis == 0:
            return values[0:rim], values[rim:]
        return values[:, 0:rim], values[:, rim:]

    def stacked(real, imag, axis, mix):
        (real0, real1), (imag0, imag1) = halved(real, axis), halved(imag, axis)
        if mix:
            real0, real1 = real0 + real1, real0 - real1
            imag0, imag1 = imag0 + imag1, imag0 - imag1
        return [jnp.concatenate(pair, axis=axis) for pair in ((real0, imag0), (real1, imag1))]

    def unstacked(first, second, axis, mix):
        (real0, imag0), (real1, imag1) = halved(first, axis), halved(second, axis)
        if mix:
            real0, real1 = real0 + real1, real0 - real1
            imag0, imag1 = imag0 + imag1, imag0 - imag1
        return [jnp.concatenate(pair, axis=axis) for pair in ((real0, real1), (imag0, imag1))]

    def transform3(real, imag, base, mix_after):
        for axis in range(2):
            sides = []
            for place, values in enumerate(stacked(real, imag, axis, True)):
                high, low = halves(values)
                values = jnp.concatenate((high, high, low), axis=axis)
                if axis == 0:
                    sides.append(dot(left3[base + place], values))
                else:
                    sides.append(dot(values, right3[base + place]))
            real, imag = unstacked(*sides, axis, mix_after)
        return real, imag

    def conjugate1(real, imag, base, mix_before):
        for axis in range(2):
            sides = []
            for place, values in enumerate(stacked(real, imag, axis, mix_before)):
                values = values.astype(BF16)
                if axis == 0:
                    sides.append(dot(right3[base + place, 0:patch], values))
                else:
                    sides.append(dot(values, left3[base + place, :, 0:patch]))
            real, imag = unstacked(*sides, axis, True)
        return real, imag

    def one_hot(shape, axis, shift, turn=None):
        index = lax.broadcasted_iota(jnp.int32, shape, 1 - axis)
        if turn is not None:
            index = index + turn
            index = jnp.where(index >= patch, index - patch, index)
        hit = lax.broadcasted_iota(jnp.int32, shape, axis) == index + shift
        return hit.astype(F32).astype(BF16)

    blocks, quads, turned = [], [], []
    for slot in range(2):
        corner = [pos[0, 0, slot, axis] for axis in range(2)]
        turned.append([start < patch for start in corner])
        turns = [jnp.where(flag, rim, 0) for flag in turned[slot]]
        block = [jnp.minimum(start >> 7, (full - span) // 128) for start in corner]
        blocks.append(block)
        pick_rows[slot] = one_hot((rim, span), 1, corner[0] - block[0] * 128, turns[0] + rim)
        pick_cols[slot] = one_hot((span, patch), 0, corner[1] - block[1] * 128, turns[1])
        put_rows[:, slot * patch:(slot + 1) * patch] = one_hot((full, patch), 0, corner[0])
        put_cols[slot] = one_hot((patch, full), 1, corner[1])
        first = [start - rim + turn for start, turn in zip(corner, turns)]
        quad = [jnp.minimum(start >> 7, (tile - patch) // 128) for start in first]
        quads.append(quad)
        quad_rows[slot] = one_hot((rim, patch), 1, first[0] - quad[0] * 128)
        quad_cols[slot] = one_hot((patch, rim), 0, first[1] - quad[1] * 128)

    def select(codes, rows, cols):
        width, height = codes[0].shape[1], rows.shape[0]
        pieces = [piece for values in codes for piece in halves(values)]
        picked = dot(rows, jnp.concatenate(pieces, axis=1)).astype(BF16)
        picked = jnp.concatenate([picked[:, k * width:(k + 1) * width] for k in range(4)], axis=0)
        cells = dot(picked, cols)
        cells = [cells[k * height:(k + 1) * height] for k in range(4)]
        return [
            (cells[2 * part] + cells[2 * part + 1]).astype(jnp.int32).astype(jnp.int16)
            for part in range(2)
        ]

    for slot in range(2):
        codes = [
            jnp.round(
                obj[part, pl.ds(quads[slot][0] * 128, patch), pl.ds(quads[slot][1] * 128, patch)]
                * SCALE
            )
            for part in range(2)
        ]
        for part, cells in enumerate(select(codes, quad_rows[slot], quad_cols[slot])):
            win[depth, slot, part, 0:rim, 0:rim] = cells

    def extract_front(slot):
        codes = [
            pad[
                part, pl.ds((quads[slot][0] + 1) * 128, patch), pl.ds(blocks[slot][1] * 128, span)
            ].astype(F32)
            for part in range(2)
        ]
        for part, cells in enumerate(select(codes, quad_rows[slot], pick_cols[slot, :, rim:])):
            win[depth, slot, part, 0:rim, rim:] = cells

    def extract_back(slot):
        codes = [
            pad[
                part, pl.ds(blocks[slot][0] * 128, span), pl.ds(blocks[slot][1] * 128, span)
            ].astype(F32)
            for part in range(2)
        ]
        for part, cells in enumerate(select(codes, pick_rows[slot], pick_cols[slot])):
            win[depth, slot, part, rim:] = cells

    def swap(buffer, index):
        return pltpu.make_async_remote_copy(
            src_ref=buffer, dst_ref=buffer,
            send_sem=swap_send.at[index], recv_sem=swap_recv.at[index],
            device_id=partner, device_id_type=MESH,
        )

    def patch_of(section, slot):
        parts = []
        for part in range(2):
            codes = win[section, slot, part].astype(F32) * (1.0 / SCALE)
            for axis in range(2):
                front, back = (codes[0:rim], codes[rim:]) if axis == 0 else (codes[:, 0:rim], codes[:, rim:])
                flag = turned[slot][axis]
                codes = jnp.concatenate(
                    (jnp.where(flag, back, front), jnp.where(flag, front, back)), axis=axis
                )
            parts.append(codes)
        return parts

    def swap_piece(slot, section, piece):
        source = win.at[section, slot]
        if piece < 2:
            source = source.at[:, 0:rim, piece * rim:(piece + 1) * rim]
        else:
            source = source.at[pl.ds(piece - 2, 1), rim:patch]
        return swap(source, 4 * slot + piece)

    loads[2].wait()
    loads[3].wait()
    loads[4].wait()
    loads[6].wait()
    place = lax.broadcasted_iota(jnp.int32, (patch, patch), 0)
    order = (
        lax.broadcasted_iota(jnp.int32, (patch, patch), 1)
        == 2 * place - jnp.where(place >= rim, patch - 1, 0)
    ).astype(F32).astype(BF16)
    for slot in range(2):
        rows = dot(order, amp[slot]).astype(BF16)
        turned_amp[slot] = lax.dot_general(
            rows, order, (((1,), (1,)), ((), ())), preferred_element_type=F32
        ).astype(BF16)
    probe_real, probe_imag = probe[0].astype(F32), probe[1].astype(F32)
    for k in range(2):
        halo[k].wait_recv()
        halo.append(
            send(
                pad.at[:, inner_rows[k], past_cross], ring.at[k, :, :, past_cross],
                halo_sems, 6 + k, along[k],
            )
        )
    for slot in range(2):
        swap_piece(slot, depth, 0).start()
    for k in range(2):
        halo[3 + k].wait_recv()
        halo.append(
            send(
                ring.at[k, :, :, near_mate], ring.at[k, :, :, past_cross],
                halo_sems, 8 + k, mate,
            )
        )
    halo[5].wait_recv()
    halo[2].wait_recv()
    for slot in range(2):
        extract_front(slot)
        swap_piece(slot, depth, 1).start()
    for copy in halo[6:]:
        copy.wait_recv()
    for k in range(2):
        for part in range(2):
            pad[part, outer_rows[k]] = ring[k, part]

    def propagate(slot):
        obj_real, obj_imag = patch_of(0, slot)
        wave_real, wave_imag = transform3(
            probe_real * obj_real - probe_imag * obj_imag,
            probe_real * obj_imag + probe_imag * obj_real,
            2, True,
        )
        wave[slot, 0] = wave_real.astype(BF16)
        wave[slot, 1] = wave_imag.astype(BF16)

    for slot in range(2):
        extract_back(slot)
        for part in range(2):
            swap_piece(slot, depth, 2 + part).start()

    @pl.when(depth == 0)
    def _():
        for slot in range(2):
            propagate(slot)

    for slot in range(2):
        for piece in range(4):
            swap_piece(slot, 1 - depth, piece).wait_recv()

        @pl.when(depth == 1)
        def _():
            propagate(slot)

        wave_real, wave_imag = wave[slot, 0].astype(F32), wave[slot, 1].astype(F32)
        obj_real, obj_imag = patch_of(1, slot)
        far_real, far_imag = transform3(
            wave_real * obj_real - wave_imag * obj_imag,
            wave_real * obj_imag + wave_imag * obj_real,
            0, False,
        )
        power = far_real * far_real + far_imag * far_imag
        weight = live[0, 0, slot].astype(F32)
        factor = weight * (
            1.0 - turned_amp[slot].astype(F32) * lax.rsqrt(jnp.maximum(power, 0.0625))
        )
        back_real, back_imag = conjugate1(far_real * factor, far_imag * factor, 0, False)
        back_real = back_real.astype(BF16).astype(F32)
        back_imag = back_imag.astype(BF16).astype(F32)

        @pl.when(depth == 1)
        def _():
            grads[slot, 0] = (wave_real * back_real + wave_imag * back_imag).astype(BF16)
            grads[slot, 1] = (wave_real * back_imag - wave_imag * back_real).astype(BF16)

        @pl.when(depth == 0)
        def _():
            first_real, first_imag = conjugate1(
                obj_real * back_real + obj_imag * back_imag,
                obj_real * back_imag - obj_imag * back_real,
                2, True,
            )
            first_real = first_real.astype(BF16).astype(F32)
            first_imag = first_imag.astype(BF16).astype(F32)
            grads[slot, 0] = (probe_real * first_real + probe_imag * first_imag).astype(BF16)
            grads[slot, 1] = (probe_real * first_imag - probe_imag * first_real).astype(BF16)

        if slot == 0:
            cells = dot(grads[0].reshape(2 * patch, patch), put_cols[0]).astype(BF16)
            for part in range(2):
                spread[part, 0:patch] = cells[part * patch:(part + 1) * patch]

    outer_cols = jnp.concatenate((put_cols[1, :, 0:rim], put_cols[1, :, rim + tile:]), axis=1)
    outer_ends = jnp.concatenate((put_rows[0:rim], put_rows[rim + tile:]), axis=0)
    last_grads = grads[1].reshape(2 * patch, patch)
    cells = dot(last_grads, outer_cols).astype(BF16)
    for part in range(2):
        spread[part, patch:, 0:rim] = cells[part * patch:(part + 1) * patch, 0:rim]
        spread[part, patch:, rim + tile:] = cells[part * patch:(part + 1) * patch, rim:]
    sides = [(part, place) for place in (past_cross, past_mate) for part in range(2)]
    lanes = jnp.concatenate([spread[part, :, place] for part, place in sides], axis=1)
    cells = dot(outer_ends, lanes).astype(BF16)
    for index, (part, place) in enumerate(sides):
        gpad[part, 0:rim, place] = cells[0:rim, index * rim:(index + 1) * rim]
        gpad[part, rim + tile:, place] = cells[rim:, index * rim:(index + 1) * rim]
    rim_sems = (rim_send, rim_recv)
    edge_rows = (pl.ds(0, rim), pl.ds(rim + tile, rim))
    rims = [
        send(gpad.at[:, edge_rows[k], past_cross], got_c.at[0, k], rim_sems, k, along[k])
        for k in range(2)
    ]
    rims += [
        send(gpad.at[:, edge_rows[k], past_mate], got_c.at[1, k], rim_sems, 2 + k, mate)
        for k in range(2)
    ]
    cells = dot(put_rows[rim:rim + tile], lanes).astype(BF16)
    for index, (part, place) in enumerate(sides):
        gpad[part, middle, place] = cells[:, index * rim:(index + 1) * rim]
    rims.append(
        send(
            gpad.at[:, pl.ds(2 * rim, tile - 2 * rim), past_cross],
            got_x.at[odd, :, pl.ds(rim, tile - 2 * rim)], rim_sems, 4, cross,
        )
    )
    rims.append(send(gpad.at[:, middle, past_mate], got_x.at[1 - odd], rim_sems, 5, mate))

    cells = dot(last_grads, put_cols[1, :, rim:rim + tile]).astype(BF16)
    for part in range(2):
        spread[part, patch:, rim:rim + tile] = cells[part * patch:(part + 1) * patch]
    lanes = jnp.concatenate([spread[part, :, rim:rim + tile] for part in range(2)], axis=1)
    cells = dot(outer_ends, lanes).astype(BF16)
    for part in range(2):
        gpad[part, 0:rim, rim:rim + tile] = cells[0:rim, part * tile:(part + 1) * tile]
        gpad[part, rim + tile:, rim:rim + tile] = cells[rim:, part * tile:(part + 1) * tile]
    rims += [
        send(
            gpad.at[:, edge_rows[k], pl.ds(rim * (1 + odd), tile - rim)],
            got_y.at[k, :, :, pl.ds(rim * odd, tile - rim)], rim_sems, 6 + k, along[k],
        )
        for k in range(2)
    ]
    for k in range(2):
        rims[2 + k].wait_recv()
        for part in range(2):
            total = gpad[part, edge_rows[k], near_mate].astype(F32) + got_c[1, k, part].astype(F32)
            gpad[part, edge_rows[k], near_mate] = total.astype(BF16)
        rims.append(
            send(
                gpad.at[:, edge_rows[k], near_mate], got_y.at[k, :, :, edge_mate],
                rim_sems, 8 + k, along[k],
            )
        )

    for part in range(2):
        out[0, part] = dot(put_rows[rim:rim + tile], spread[part, :, rim:rim + tile])

    tile_rows = (pl.ds(tile - rim, rim), pl.ds(0, rim))
    for k in range(2):
        rims[k].wait_recv()
        rows = inner_rows[1 - k]
        for part in range(2):
            total = gpad[part, rows, past_cross].astype(F32) + got_c[0, k, part].astype(F32)
            gpad[part, rows, past_cross] = total.astype(BF16)
        rims.append(
            send(
                gpad.at[:, rows, past_cross], got_x.at[odd, :, tile_rows[k]],
                rim_sems, 10 + k, cross,
            )
        )
    for copy in rims[4:10]:
        copy.wait_recv()
    core = pl.ds(rim, tile - 2 * rim)
    for part in range(2):
        out[0, part, :, edge_mate] += got_x[odd, part].astype(F32)
        out[0, part, core, edge_cross] += got_x[1 - odd, part, core].astype(F32)
        for k in range(2):
            out[0, part, tile_rows[k]] += got_y[k, part].astype(F32)
    for k in range(2):
        rims[10 + k].wait_recv()
        for part in range(2):
            out[0, part, tile_rows[k], edge_cross] += got_x[1 - odd, part, tile_rows[k]].astype(F32)

    for copy in halo:
        copy.wait_send()
    for slot in range(2):
        for piece in range(4):
            swap_piece(slot, depth, piece).wait_send()
    for copy in rims:
        copy.wait_send()


def on_device(object_field, probe, amplitude, positions, live):
    tile = object_field.shape[2]
    patch = probe.shape[1]
    rim = patch // 2
    full = tile + patch
    left, right = tables(patch)
    vmem = pl.BlockSpec(memory_space=pltpu.VMEM)
    smem = pl.BlockSpec(memory_space=pltpu.SMEM)
    hbm = pl.BlockSpec(memory_space=pl.ANY)
    dma = pltpu.SemaphoreType.DMA
    gradient = pl.pallas_call(
        functools.partial(
            kernel, tile, patch, lax.axis_size("row"), lax.axis_size("col")
        ),
        out_shape=pltpu.VMEM(object_field.shape, F32),
        in_specs=[smem, smem, hbm, hbm, hbm, hbm, hbm],
        out_specs=vmem,
        scratch_shapes=[
            pltpu.VMEM((2, tile, rim), F32),
            pltpu.VMEM((2, tile, tile), F32),
            pltpu.VMEM((2, patch, patch), BF16),
            pltpu.VMEM((2, patch, patch), BF16),
            pltpu.VMEM((2, patch, patch), BF16),
            pltpu.VMEM((2, full, full), jnp.int16),
            pltpu.VMEM((2, 2, rim, full), jnp.int16),
            pltpu.VMEM((2, 2, 2, patch, patch), jnp.int16),
            pltpu.VMEM((2, 2, patch, patch), BF16),
            pltpu.VMEM((2, 2, patch, patch), BF16),
            pltpu.VMEM((2, full, full), BF16),
            pltpu.VMEM((2, 2, tile, rim), BF16),
            pltpu.VMEM((2, 2, rim, tile), BF16),
            pltpu.VMEM((2, 2, 2, rim, rim), BF16),
            pltpu.VMEM(left.shape, BF16),
            pltpu.VMEM(right.shape, BF16),
            pltpu.VMEM((2, rim, patch + rim), BF16),
            pltpu.VMEM((2, patch + rim, patch), BF16),
            pltpu.VMEM((full, 2 * patch), BF16),
            pltpu.VMEM((2, patch, full), BF16),
            pltpu.VMEM((2, rim, patch), BF16),
            pltpu.VMEM((2, patch, rim), BF16),
            pltpu.VMEM((2, 2 * patch, full), BF16),
            dma((7,)), dma((10,)), dma((10,)), dma((8,)), dma((8,)), dma((12,)), dma((12,)),
        ],
        compiler_params=pltpu.CompilerParams(
            collective_id=0, has_side_effects=True, vmem_limit_bytes=56 * 1024 * 1024
        ),
    )(positions, live, object_field, probe, amplitude, jnp.asarray(left), jnp.asarray(right))
    return gradient


def solution(mesh):
    in_specs = (
        P("depth", None, "row", "col"),
        P(),
        P("row", "col", None, None, None),
        P("row", "col", None, None),
        P("row", "col", None),
    )
    out_specs = P("depth", None, "row", "col")
    return jax.shard_map(
        on_device, mesh=mesh, in_specs=in_specs, out_specs=out_specs, check_vma=False
    )
```

```python
import functools
import math

import jax
import jax.numpy as jnp
import ml_dtypes
import numpy as np
from jax import lax
from jax.experimental import pallas as pl
from jax.experimental.pallas import tpu as pltpu
from jax.sharding import PartitionSpec as P

MESH = pl.DeviceIdType.MESH
SCALE = 16384.0
F32 = jnp.float32
BF16 = jnp.bfloat16


def split(values):
    high = values.astype(ml_dtypes.bfloat16)
    low = (values - high.astype(np.float64)).astype(ml_dtypes.bfloat16)
    return high, low


def tables(size):
    steps = np.arange(size)
    angles = 2.0 * math.pi * ((steps[:, None] * steps[None, :]) % size) / size
    fourier = np.exp(-1j * angles) / math.sqrt(size)
    frequency = (steps + size // 2) % size - size // 2
    chirp = np.exp(-1j * math.pi * frequency.astype(np.float64) ** 2 / (2.0 * size))
    spread = fourier.conj() @ (chirp[:, None] * fourier)
    half = size // 2
    same, swapped = spread[:half, :half], spread[:half, half:]
    left, right = [], []
    for table in (fourier[0::2, :half], fourier[1::2, :half], (same + swapped) / 2, (same - swapped) / 2):
        whole = np.block([[table.real, -table.imag], [table.imag, table.real]])
        high, low = split(whole)
        left.append(np.concatenate((high, low, high), axis=1))
        right.append(np.concatenate((high.T, low.T, high.T), axis=0))
    return np.stack(left), np.stack(right)


def dot(left, right):
    return jnp.dot(left, right, preferred_element_type=F32)


def halves(values):
    high = values.astype(BF16)
    return high, (values - high.astype(F32)).astype(BF16)


def kernel(
    tile, patch, n_row, n_col,
    pos, live, obj_hbm, probe_hbm, amp_hbm, left_hbm, right_hbm, out,
    edge, obj, probe, amp, turned_amp, pad, ring, win, wave, grads, gpad, got_x, got_y, got_c,
    left3, right3, pick_rows, pick_cols, put_rows, put_cols, quad_rows, quad_cols, spread,
    in_sem, halo_send, halo_recv, swap_send, swap_recv, rim_send, rim_recv,
):
    rim = patch // 2
    full = tile + patch
    span = patch + rim
    depth, row, col = lax.axis_index("depth"), lax.axis_index("row"), lax.axis_index("col")
    partner = (1 - depth, row, col)

    odd = lax.rem(col, 2)
    away = 2 * odd - 1
    mate = (depth, row, col - away)
    cross = (depth, row, lax.rem(col + away + n_col, n_col))
    along = [(depth, lax.rem(row + step + n_row, n_row), col) for step in (-1, 1)]

    def send(source, target, sems, index, device):
        copy = pltpu.make_async_remote_copy(
            src_ref=source, dst_ref=target, send_sem=sems[0].at[index],
            recv_sem=sems[1].at[index], device_id=device, device_id_type=MESH,
        )
        copy.start()
        return copy

    barrier = pltpu.get_barrier_semaphore()
    for device in (mate, cross, *along, partner):
        pl.semaphore_signal(barrier, inc=1, device_id=device, device_id_type=MESH)
    last = tile // rim
    near_mate, near_cross = pl.ds(rim * (last - (last - 1) * odd), rim), pl.ds(rim * (1 + (last - 1) * odd), rim)
    past_mate, past_cross = pl.ds(rim * ((last + 1) * (1 - odd)), rim), pl.ds(rim * ((last + 1) * odd), rim)
    middle = pl.ds(rim, tile)
    inner_rows = (pl.ds(rim, rim), pl.ds(tile, rim))
    outer_rows = (pl.ds(rim + tile, rim), pl.ds(0, rim))
    halo_sems = (halo_send, halo_recv)
    edge_cross, edge_mate = pl.ds(rim * (last - 1) * odd, rim), pl.ds(rim * (last - 1) * (1 - odd), rim)
    loads = [
        pltpu.make_async_copy(source, target, in_sem.at[index])
        for index, (source, target) in enumerate((
            (obj_hbm.at[0, 0], obj.at[0]), (obj_hbm.at[0, 1], obj.at[1]),
            (left_hbm, left3), (probe_hbm, probe), (amp_hbm.at[0, 0], amp),
            (obj_hbm.at[0, :, :, edge_cross], edge), (right_hbm, right3),
        ))
    ]
    for load in (loads[5], loads[0], loads[1]):
        load.start()

    def fixed_point(values):
        return jnp.round(values * SCALE).astype(jnp.int32).astype(jnp.int16)

    loads[5].wait()
    for part in range(2):
        pad[part, middle, near_cross] = fixed_point(edge[part])
    pl.semaphore_wait(barrier, 5)
    halo = [
        send(pad.at[:, rows, near_cross], pad.at[:, rows, past_mate], halo_sems, index, cross)
        for index, rows in enumerate((*inner_rows, pl.ds(2 * rim, tile - 2 * rim)))
    ]
    for load in (*loads[2:5], loads[6]):
        load.start()
    for part in range(2):
        loads[part].wait()
        pad[part, middle, 2 * rim:tile] = fixed_point(obj[part, :, rim:tile - rim])
        pad[part, middle, near_mate] = fixed_point(obj[part, :, edge_mate])
    halo += [
        send(pad.at[:, inner_rows[k], middle], ring.at[k, :, :, middle], halo_sems, 3 + k, along[k])
        for k in range(2)
    ]
    halo.append(send(pad.at[:, middle, near_mate], pad.at[:, middle, past_cross], halo_sems, 5, mate))

    def halved(values, axis):
        if axis == 0:
            return values[0:rim], values[rim:]
        return values[:, 0:rim], values[:, rim:]

    def stacked(real, imag, axis, mix):
        (real0, real1), (imag0, imag1) = halved(real, axis), halved(imag, axis)
        if mix:
            real0, real1 = real0 + real1, real0 - real1
            imag0, imag1 = imag0 + imag1, imag0 - imag1
        return [jnp.concatenate(pair, axis=axis) for pair in ((real0, imag0), (real1, imag1))]

    def unstacked(first, second, axis, mix):
        (real0, imag0), (real1, imag1) = halved(first, axis), halved(second, axis)
        if mix:
            real0, real1 = real0 + real1, real0 - real1
            imag0, imag1 = imag0 + imag1, imag0 - imag1
        return [jnp.concatenate(pair, axis=axis) for pair in ((real0, real1), (imag0, imag1))]

    def transform3(real, imag, base, mix_after):
        for axis in range(2):
            sides = []
            for place, values in enumerate(stacked(real, imag, axis, True)):
                high, low = halves(values)
                values = jnp.concatenate((high, high, low), axis=axis)
                if axis == 0:
                    sides.append(dot(left3[base + place], values))
                else:
                    sides.append(dot(values, right3[base + place]))
            real, imag = unstacked(*sides, axis, mix_after)
        return real, imag

    def conjugate1(real, imag, base, mix_before):
        for axis in range(2):
            sides = []
            for place, values in enumerate(stacked(real, imag, axis, mix_before)):
                values = values.astype(BF16)
                if axis == 0:
                    sides.append(dot(right3[base + place, 0:patch], values))
                else:
                    sides.append(dot(values, left3[base + place, :, 0:patch]))
            real, imag = unstacked(*sides, axis, True)
        return real, imag

    def one_hot(shape, axis, shift, turn=None):
        index = lax.broadcasted_iota(jnp.int32, shape, 1 - axis)
        if turn is not None:
            index = index + turn
            index = jnp.where(index >= patch, index - patch, index)
        hit = lax.broadcasted_iota(jnp.int32, shape, axis) == index + shift
        return hit.astype(F32).astype(BF16)

    blocks, quads, turned = [], [], []
    for slot in range(2):
        corner = [pos[0, 0, slot, axis] for axis in range(2)]
        turned.append([start < patch for start in corner])
        turns = [jnp.where(flag, rim, 0) for flag in turned[slot]]
        block = [jnp.minimum(start >> 7, (full - span) // 128) for start in corner]
        blocks.append(block)
        pick_rows[slot] = one_hot((rim, span), 1, corner[0] - block[0] * 128, turns[0] + rim)
        pick_cols[slot] = one_hot((span, patch), 0, corner[1] - block[1] * 128, turns[1])
        put_rows[:, slot * patch:(slot + 1) * patch] = one_hot((full, patch), 0, corner[0])
        put_cols[slot] = one_hot((patch, full), 1, corner[1])
        first = [start - rim + turn for start, turn in zip(corner, turns)]
        quad = [jnp.minimum(start >> 7, (tile - patch) // 128) for start in first]
        quads.append(quad)
        quad_rows[slot] = one_hot((rim, patch), 1, first[0] - quad[0] * 128)
        quad_cols[slot] = one_hot((patch, rim), 0, first[1] - quad[1] * 128)

    def select(codes, rows, cols):
        width, height = codes[0].shape[1], rows.shape[0]
        pieces = [piece for values in codes for piece in halves(values)]
        picked = dot(rows, jnp.concatenate(pieces, axis=1)).astype(BF16)
        picked = jnp.concatenate([picked[:, k * width:(k + 1) * width] for k in range(4)], axis=0)
        cells = dot(picked, cols)
        cells = [cells[k * height:(k + 1) * height] for k in range(4)]
        return [
            (cells[2 * part] + cells[2 * part + 1]).astype(jnp.int32).astype(jnp.int16)
            for part in range(2)
        ]

    for slot in range(2):
        codes = [
            jnp.round(
                obj[part, pl.ds(quads[slot][0] * 128, patch), pl.ds(quads[slot][1] * 128, patch)]
                * SCALE
            )
            for part in range(2)
        ]
        for part, cells in enumerate(select(codes, quad_rows[slot], quad_cols[slot])):
            win[depth, slot, part, 0:rim, 0:rim] = cells

    def extract_front(slot):
        codes = [
            pad[
                part, pl.ds((quads[slot][0] + 1) * 128, patch), pl.ds(blocks[slot][1] * 128, span)
            ].astype(F32)
            for part in range(2)
        ]
        for part, cells in enumerate(select(codes, quad_rows[slot], pick_cols[slot, :, rim:])):
            win[depth, slot, part, 0:rim, rim:] = cells

    def extract_back(slot):
        codes = [
            pad[
                part, pl.ds(blocks[slot][0] * 128, span), pl.ds(blocks[slot][1] * 128, span)
            ].astype(F32)
            for part in range(2)
        ]
        for part, cells in enumerate(select(codes, pick_rows[slot], pick_cols[slot])):
            win[depth, slot, part, rim:] = cells

    def swap(buffer, index):
        return pltpu.make_async_remote_copy(
            src_ref=buffer, dst_ref=buffer,
            send_sem=swap_send.at[index], recv_sem=swap_recv.at[index],
            device_id=partner, device_id_type=MESH,
        )

    def patch_of(section, slot):
        parts = []
        for part in range(2):
            codes = win[section, slot, part].astype(F32) * (1.0 / SCALE)
            for axis in range(2):
                front, back = (codes[0:rim], codes[rim:]) if axis == 0 else (codes[:, 0:rim], codes[:, rim:])
                flag = turned[slot][axis]
                codes = jnp.concatenate(
                    (jnp.where(flag, back, front), jnp.where(flag, front, back)), axis=axis
                )
            parts.append(codes)
        return parts

    def swap_piece(slot, section, piece):
        source = win.at[section, slot]
        if piece < 2:
            source = source.at[:, 0:rim, piece * rim:(piece + 1) * rim]
        else:
            source = source.at[pl.ds(piece - 2, 1), rim:patch]
        return swap(source, 4 * slot + piece)

    loads[2].wait()
    loads[3].wait()
    loads[4].wait()
    loads[6].wait()
    place = lax.broadcasted_iota(jnp.int32, (patch, patch), 0)
    order = (
        lax.broadcasted_iota(jnp.int32, (patch, patch), 1)
        == 2 * place - jnp.where(place >= rim, patch - 1, 0)
    ).astype(F32).astype(BF16)
    for slot in range(2):
        rows = dot(order, amp[slot]).astype(BF16)
        turned_amp[slot] = lax.dot_general(
            rows, order, (((1,), (1,)), ((), ())), preferred_element_type=F32
        ).astype(BF16)
    probe_real, probe_imag = probe[0].astype(F32), probe[1].astype(F32)
    for k in range(2):
        halo[k].wait_recv()
        halo.append(
            send(
                pad.at[:, inner_rows[k], past_cross], ring.at[k, :, :, past_cross],
                halo_sems, 6 + k, along[k],
            )
        )
    for slot in range(2):
        swap_piece(slot, depth, 0).start()
    for k in range(2):
        halo[3 + k].wait_recv()
        halo.append(
            send(
                ring.at[k, :, :, near_mate], ring.at[k, :, :, past_cross],
                halo_sems, 8 + k, mate,
            )
        )
    halo[5].wait_recv()
    halo[2].wait_recv()
    for slot in range(2):
        extract_front(slot)
        swap_piece(slot, depth, 1).start()
    for copy in halo[6:]:
        copy.wait_recv()
    for k in range(2):
        for part in range(2):
            pad[part, outer_rows[k]] = ring[k, part]

    def propagate(slot):
        obj_real, obj_imag = patch_of(0, slot)
        wave_real, wave_imag = transform3(
            probe_real * obj_real - probe_imag * obj_imag,
            probe_real * obj_imag + probe_imag * obj_real,
            2, True,
        )
        wave[slot, 0] = wave_real.astype(BF16)
        wave[slot, 1] = wave_imag.astype(BF16)

    for slot in range(2):
        extract_back(slot)
        for part in range(2):
            swap_piece(slot, depth, 2 + part).start()

    @pl.when(depth == 0)
    def _():
        for slot in range(2):
            propagate(slot)

    for slot in range(2):
        for piece in range(4):
            swap_piece(slot, 1 - depth, piece).wait_recv()

        @pl.when(depth == 1)
        def _():
            propagate(slot)

        wave_real, wave_imag = wave[slot, 0].astype(F32), wave[slot, 1].astype(F32)
        obj_real, obj_imag = patch_of(1, slot)
        far_real, far_imag = transform3(
            wave_real * obj_real - wave_imag * obj_imag,
            wave_real * obj_imag + wave_imag * obj_real,
            0, False,
        )
        power = far_real * far_real + far_imag * far_imag
        weight = live[0, 0, slot].astype(F32)
        factor = weight * (
            1.0 - turned_amp[slot].astype(F32) * lax.rsqrt(jnp.maximum(power, 0.0625))
        )
        back_real, back_imag = conjugate1(far_real * factor, far_imag * factor, 0, False)
        back_real = back_real.astype(BF16).astype(F32)
        back_imag = back_imag.astype(BF16).astype(F32)

        @pl.when(depth == 1)
        def _():
            grads[slot, 0] = (wave_real * back_real + wave_imag * back_imag).astype(BF16)
            grads[slot, 1] = (wave_real * back_imag - wave_imag * back_real).astype(BF16)

        @pl.when(depth == 0)
        def _():
            first_real, first_imag = conjugate1(
                obj_real * back_real + obj_imag * back_imag,
                obj_real * back_imag - obj_imag * back_real,
                2, True,
            )
            first_real = first_real.astype(BF16).astype(F32)
            first_imag = first_imag.astype(BF16).astype(F32)
            grads[slot, 0] = (probe_real * first_real + probe_imag * first_imag).astype(BF16)
            grads[slot, 1] = (probe_real * first_imag - probe_imag * first_real).astype(BF16)

        if slot == 0:
            cells = dot(grads[0].reshape(2 * patch, patch), put_cols[0]).astype(BF16)
            for part in range(2):
                spread[part, 0:patch] = cells[part * patch:(part + 1) * patch]

    outer_cols = jnp.concatenate((put_cols[1, :, 0:rim], put_cols[1, :, rim + tile:]), axis=1)
    outer_ends = jnp.concatenate((put_rows[0:rim], put_rows[rim + tile:]), axis=0)
    last_grads = grads[1].reshape(2 * patch, patch)
    cells = dot(last_grads, outer_cols).astype(BF16)
    for part in range(2):
        spread[part, patch:, 0:rim] = cells[part * patch:(part + 1) * patch, 0:rim]
        spread[part, patch:, rim + tile:] = cells[part * patch:(part + 1) * patch, rim:]
    sides = [(part, place) for place in (past_cross, past_mate) for part in range(2)]
    lanes = jnp.concatenate([spread[part, :, place] for part, place in sides], axis=1)
    cells = dot(outer_ends, lanes).astype(BF16)
    for index, (part, place) in enumerate(sides):
        gpad[part, 0:rim, place] = cells[0:rim, index * rim:(index + 1) * rim]
        gpad[part, rim + tile:, place] = cells[rim:, index * rim:(index + 1) * rim]
    rim_sems = (rim_send, rim_recv)
    edge_rows = (pl.ds(0, rim), pl.ds(rim + tile, rim))
    rims = [
        send(gpad.at[:, edge_rows[k], past_cross], got_c.at[0, k], rim_sems, k, along[k])
        for k in range(2)
    ]
    rims += [
        send(gpad.at[:, edge_rows[k], past_mate], got_c.at[1, k], rim_sems, 2 + k, mate)
        for k in range(2)
    ]
    cells = dot(put_rows[rim:rim + tile], lanes[:, 0:2 * rim]).astype(BF16)
    for part in range(2):
        gpad[part, middle, past_cross] = cells[:, part * rim:(part + 1) * rim]
    rims.append(
        send(
            gpad.at[:, pl.ds(2 * rim, tile - 2 * rim), past_cross],
            got_x.at[odd, :, pl.ds(rim, tile - 2 * rim)], rim_sems, 4, cross,
        )
    )
    mate_lanes = lanes[:, 2 * rim:]

    cells = dot(last_grads, put_cols[1, :, rim:rim + tile]).astype(BF16)
    for part in range(2):
        spread[part, patch:, rim:rim + tile] = cells[part * patch:(part + 1) * patch]
    lanes = jnp.concatenate([spread[part, :, rim:rim + tile] for part in range(2)], axis=1)
    cells = dot(outer_ends, lanes).astype(BF16)
    for part in range(2):
        gpad[part, 0:rim, rim:rim + tile] = cells[0:rim, part * tile:(part + 1) * tile]
        gpad[part, rim + tile:, rim:rim + tile] = cells[rim:, part * tile:(part + 1) * tile]
    rims += [
        send(
            gpad.at[:, edge_rows[k], pl.ds(rim * (1 + odd), tile - rim)],
            got_y.at[k, :, :, pl.ds(rim * odd, tile - rim)], rim_sems, 6 + k, along[k],
        )
        for k in range(2)
    ]
    for k in range(2):
        rims[2 + k].wait_recv()
        for part in range(2):
            total = gpad[part, edge_rows[k], near_mate].astype(F32) + got_c[1, k, part].astype(F32)
            gpad[part, edge_rows[k], near_mate] = total.astype(BF16)
        rims.append(
            send(
                gpad.at[:, edge_rows[k], near_mate], got_y.at[k, :, :, edge_mate],
                rim_sems, 8 + k, along[k],
            )
        )
    cells = dot(put_rows[rim:rim + tile], mate_lanes).astype(BF16)
    for part in range(2):
        gpad[part, middle, past_mate] = cells[:, part * rim:(part + 1) * rim]
    rims.insert(5, send(gpad.at[:, middle, past_mate], got_x.at[1 - odd], rim_sems, 5, mate))

    for part in range(2):
        out[0, part] = dot(put_rows[rim:rim + tile], spread[part, :, rim:rim + tile])

    tile_rows = (pl.ds(tile - rim, rim), pl.ds(0, rim))
    for k in range(2):
        rims[k].wait_recv()
        rows = inner_rows[1 - k]
        for part in range(2):
            total = gpad[part, rows, past_cross].astype(F32) + got_c[0, k, part].astype(F32)
            gpad[part, rows, past_cross] = total.astype(BF16)
        rims.append(
            send(
                gpad.at[:, rows, past_cross], got_x.at[odd, :, tile_rows[k]],
                rim_sems, 10 + k, cross,
            )
        )
    for copy in rims[4:10]:
        copy.wait_recv()
    core = pl.ds(rim, tile - 2 * rim)
    for part in range(2):
        out[0, part, :, edge_mate] += got_x[odd, part].astype(F32)
        out[0, part, core, edge_cross] += got_x[1 - odd, part, core].astype(F32)
        for k in range(2):
            out[0, part, tile_rows[k]] += got_y[k, part].astype(F32)
    for k in range(2):
        rims[10 + k].wait_recv()
        for part in range(2):
            out[0, part, tile_rows[k], edge_cross] += got_x[1 - odd, part, tile_rows[k]].astype(F32)

    for copy in halo:
        copy.wait_send()
    for slot in range(2):
        for piece in range(4):
            swap_piece(slot, depth, piece).wait_send()
    for copy in rims:
        copy.wait_send()


def on_device(object_field, probe, amplitude, positions, live):
    tile = object_field.shape[2]
    patch = probe.shape[1]
    rim = patch // 2
    full = tile + patch
    left, right = tables(patch)
    vmem = pl.BlockSpec(memory_space=pltpu.VMEM)
    smem = pl.BlockSpec(memory_space=pltpu.SMEM)
    hbm = pl.BlockSpec(memory_space=pl.ANY)
    dma = pltpu.SemaphoreType.DMA
    gradient = pl.pallas_call(
        functools.partial(
            kernel, tile, patch, lax.axis_size("row"), lax.axis_size("col")
        ),
        out_shape=pltpu.VMEM(object_field.shape, F32),
        in_specs=[smem, smem, hbm, hbm, hbm, hbm, hbm],
        out_specs=vmem,
        scratch_shapes=[
            pltpu.VMEM((2, tile, rim), F32),
            pltpu.VMEM((2, tile, tile), F32),
            pltpu.VMEM((2, patch, patch), BF16),
            pltpu.VMEM((2, patch, patch), BF16),
            pltpu.VMEM((2, patch, patch), BF16),
            pltpu.VMEM((2, full, full), jnp.int16),
            pltpu.VMEM((2, 2, rim, full), jnp.int16),
            pltpu.VMEM((2, 2, 2, patch, patch), jnp.int16),
            pltpu.VMEM((2, 2, patch, patch), BF16),
            pltpu.VMEM((2, 2, patch, patch), BF16),
            pltpu.VMEM((2, full, full), BF16),
            pltpu.VMEM((2, 2, tile, rim), BF16),
            pltpu.VMEM((2, 2, rim, tile), BF16),
            pltpu.VMEM((2, 2, 2, rim, rim), BF16),
            pltpu.VMEM(left.shape, BF16),
            pltpu.VMEM(right.shape, BF16),
            pltpu.VMEM((2, rim, patch + rim), BF16),
            pltpu.VMEM((2, patch + rim, patch), BF16),
            pltpu.VMEM((full, 2 * patch), BF16),
            pltpu.VMEM((2, patch, full), BF16),
            pltpu.VMEM((2, rim, patch), BF16),
            pltpu.VMEM((2, patch, rim), BF16),
            pltpu.VMEM((2, 2 * patch, full), BF16),
            dma((7,)), dma((10,)), dma((10,)), dma((8,)), dma((8,)), dma((12,)), dma((12,)),
        ],
        compiler_params=pltpu.CompilerParams(
            collective_id=0, has_side_effects=True, vmem_limit_bytes=56 * 1024 * 1024
        ),
    )(positions, live, object_field, probe, amplitude, jnp.asarray(left), jnp.asarray(right))
    return gradient


def solution(mesh):
    in_specs = (
        P("depth", None, "row", "col"),
        P(),
        P("row", "col", None, None, None),
        P("row", "col", None, None),
        P("row", "col", None),
    )
    out_specs = P("depth", None, "row", "col")
    return jax.shard_map(
        on_device, mesh=mesh, in_specs=in_specs, out_specs=out_specs, check_vma=False
    )
```
